256 devices in a mesh: layer: 4 (over z_lo), vocab: 16 (over y, x), dp: 4 (over z_hi, core).
Axes of the slice: x: 4, y: 4, z: 8 (z_hi: 2, z_lo: 4; z = z_hi * 4 + z_lo), core: 2. Of those that a mesh axis runs over, the one named last changes fastest.
Arguments:
- hidden: bfloat16 [4, 512, 4096], P('layer', None, 'vocab'), may hold values from -50 to 50
- translator: bfloat16 [4, 4096, 4096], P('layer', 'vocab', 'dp'), may hold values from -3 to 3
- bias: float32 [4, 4096], P('layer', 'dp'), may hold values from -12 to 12
- gain: float32 [4096], P('dp'), may hold values from 0.5 to 1.5
- head: bfloat16 [4096, 65536], P('dp', 'vocab'), may hold values from -8 to 8
- final_logits: bfloat16 [4, 128, 65536], P('dp', 'layer', 'vocab'), may hold values from -20 to 310
Outputs:
- grad_translator: float32 [4, 4096, 4096], P('layer', 'vocab', 'dp')
- grad_bias: float32 [4, 4096], P('layer', 'dp')
- divergence: float32 [4], P('layer')
The draws below stay inside these ranges and needn't reach their ends.
All inputs are finite; a program needn't handle non-finite values.
Results may differ from the reference program's by a relative error of at most 0.0065.
Values may be sent and summed in bfloat16 or wider, within the bound.
A program may use at most 64 MiB of HBM per device.

```python
import math
import jax
import jax.numpy as jnp
from jax import lax

D = 4096
TOK_DEV = 128
LAYERS = 4
TOKENS = 512
VOCAB = 65536
DP_BLOCKS = 4


def draw_hidden(key, part):
    key = jax.random.fold_in(key, 11)
    first, second = jax.random.split(key)
    scales = jnp.exp(jax.random.uniform(second, (LAYERS, TOKENS, 1), jnp.float32, 0.0, math.log(10.0)))
    values = jnp.clip(jax.random.normal(first, (LAYERS, TOKENS, D), jnp.float32), -5.0, 5.0)
    return (values * scales).astype(jnp.bfloat16)


def draw_translator(key, part):
    key = jax.random.fold_in(key, 12)
    first, second = jax.random.split(key)
    columns = jnp.arange(D).astype(jnp.float32)
    rising = jnp.exp(math.log(3.0) * columns / D)
    factors = jnp.exp(jax.random.uniform(second, (LAYERS, 1, D), jnp.float32, math.log(0.5), math.log(2.0)))
    values = jnp.clip(jax.random.normal(first, (LAYERS, D, D), jnp.float32), -3.0, 3.0)
    return (values * rising * factors / math.sqrt(D)).astype(jnp.bfloat16)


def draw_bias(key, part):
    key = jax.random.fold_in(key, 13)
    first = jax.random.fold_in(key, 0)
    return 0.5 * jnp.clip(jax.random.normal(first, (LAYERS, D), jnp.float32), -5.0, 5.0)


def draw_head(key, part):
    key = jax.random.fold_in(key, 14)
    first = jax.random.fold_in(key, 0)
    scale = 3.0 / math.sqrt(D)
    values = scale * jnp.clip(jax.random.normal(first, (D, VOCAB), jnp.float32), -5.0, 5.0)
    return values.astype(jnp.bfloat16)


def draw_final_logits(key, part):
    key = jax.random.fold_in(key, 15)
    first = jax.random.fold_in(key, 0)
    shape = (DP_BLOCKS, TOK_DEV, VOCAB)
    values = 3.0 * jnp.clip(jax.random.normal(first, shape, jnp.float32), -5.0, 5.0)
    return values.astype(jnp.bfloat16)


def setup_inputs(seed: int = 0) -> dict:
    splits = jax.random.split(jax.random.key(seed), 7)
    return {
        "hidden": draw_hidden(jax.random.fold_in(splits[6], 71), 0),
        "translator": draw_translator(jax.random.fold_in(splits[6], 71), 0),
        "bias": draw_bias(jax.random.fold_in(splits[6], 71), 0),
        "gain": jnp.clip(1.0 + 0.1 * jax.random.normal(splits[3], (D,), jnp.float32), 0.5, 1.5),
        "head": draw_head(jax.random.fold_in(splits[6], 71), 0),
        "final_logits": draw_final_logits(jax.random.fold_in(splits[6], 71), 0),
    }


epsilon = 1e-05

def row_lse(values):
    top = lax.optimization_barrier(jnp.max(values, axis=1))
    return top + jnp.log(lax.optimization_barrier(jnp.sum(jnp.exp(values - top[:, None]), axis=1)))

def reference(hidden, translator, bias, gain, head, final_logits):
    target_logits = final_logits.reshape(TOKENS, VOCAB).astype(jnp.float32)
    target_lse = row_lse(target_logits)
    target = jnp.exp(target_logits - target_lse[:, None])

    def one_layer(inputs):
        features, weights, offsets = inputs
        projected = jnp.dot(features, weights, preferred_element_type=jnp.float32) + offsets
        inverse = lax.rsqrt(lax.optimization_barrier(jnp.mean(projected * projected, axis=1)) + epsilon)
        scaled = projected * inverse[:, None]
        normed = (scaled * gain).astype(jnp.bfloat16)
        logits = jnp.dot(normed, head, preferred_element_type=jnp.float32)
        logit_lse = row_lse(logits)
        predicted = jnp.exp(logits - logit_lse[:, None])
        divergence = (jnp.sum(target * (target_logits - logits)) + jnp.sum(logit_lse - target_lse)) / TOKENS
        grad_logits = (predicted - target).astype(jnp.bfloat16)
        grad_normed = lax.dot_general(grad_logits, head, (((1,), (1,)), ((), ())), preferred_element_type=jnp.float32)
        grad_scaled = grad_normed * gain
        inner = lax.optimization_barrier(jnp.mean(grad_scaled * scaled, axis=1))
        grad_projected = (inverse[:, None] * (grad_scaled - scaled * inner[:, None])).astype(jnp.bfloat16)
        grad_weights = lax.dot_general(features, grad_projected, (((0,), (0,)), ((), ())), preferred_element_type=jnp.float32)
        grad_offsets = lax.optimization_barrier(jnp.sum(grad_projected.astype(jnp.float32), axis=0))
        return (grad_weights, grad_offsets, divergence)
    grad_translator, grad_bias, divergence = lax.map(one_layer, (hidden, translator, bias))
    return (grad_translator, grad_bias, divergence)
```

```python
import jax
import jax.numpy as jnp
from jax import lax
from jax.experimental import pallas as pl
from jax.experimental.pallas import tpu as pltpu
from jax.sharding import PartitionSpec as P

D = 4096
TOKENS = 512
LAYERS = 4
GROUPS = 16
BLOCKS = 4
BLOCK = D // BLOCKS
QUARTER = 1024
ROWS = TOKENS // GROUPS
HALF = BLOCK // 2
CHUNK = 32
CHUNKS = HALF // CHUNK

epsilon = 1e-05
f32 = jnp.float32
bf16 = jnp.bfloat16
MESH = pl.DeviceIdType.MESH


def aligned(start, size, unit=None):
    return pl.ds(pl.multiple_of(start, unit or size), size)


def kernel(
    hidden, translator, bias, gain, head, final, grad_out, div_out,
    heads, passing, normed, partial, parts, target, scaled, squares, logits, stats, stats2, ends_lse,
    grads, crossing, crossed, summing, sums, half_sum, other_sum, inners, finals,
    chain_send, chain_recv, pass_send, pass_recv, head_send, head_recv, fin_send, fin_recv,
    rs_send, rs_recv, sq_send, sq_recv, ag_send, ag_recv, opp_send, opp_recv, sib_send, sib_recv,
    st_send, st_recv, st2_send, st2_recv, gx_send, gx_recv, gs_send, gs_recv, go_send, go_recv,
    in_send, in_recv, gp_send, gp_recv, local_sem,
):
    l = lax.axis_index("layer")
    v = lax.axis_index("vocab")
    d = lax.axis_index("dp")
    h = lax.div(d, 2)
    c = lax.rem(d, 2)
    sib = h * 2 + 1 - c
    opp = lax.rem(d + 2, BLOCKS)
    opp_sib = (1 - h) * 2 + 1 - c
    up_l = lax.rem(l + 1, LAYERS)
    up_d = lax.rem(d + 2 * lax.div(l + 1, LAYERS), BLOCKS)
    down_l = lax.rem(l + LAYERS - 1, LAYERS)
    down_d = lax.rem(d + 2 * (1 - lax.div(l + LAYERS - 1, LAYERS)), BLOCKS)
    column = l * BLOCKS + d
    NCOL = LAYERS * BLOCKS

    def in_plane(k):
        return lax.rem(v + k, GROUPS)

    def in_column(k):
        return lax.rem(column + k, NCOL)

    def remote(src, dst, send, recv, ll, vv, dd):
        return pltpu.make_async_remote_copy(
            src_ref=src, dst_ref=dst, send_sem=send, recv_sem=recv,
            device_id=(ll, vv, dd), device_id_type=MESH,
        )

    def arrive(dst, sem):
        remote(dst, dst, sem, sem, l, v, d).wait_recv()

    def sent(src, sem):
        remote(src, src, sem, sem, l, v, d).wait_send()

    def each(lo, hi, f):
        def step(k, carry):
            f(k)
            return carry
        lax.fori_loop(lo, hi, step, 0)

    barrier = pltpu.get_barrier_semaphore()

    def greet_plane(k):
        pl.semaphore_signal(barrier, inc=1, device_id=(l, in_plane(k), d), device_id_type=MESH)

    def greet_column(k):
        m = in_column(k)
        pl.semaphore_signal(
            barrier, inc=1, device_id=(lax.div(m, BLOCKS), v, lax.rem(m, BLOCKS)), device_id_type=MESH
        )

    each(1, GROUPS, greet_plane)
    each(1, NCOL, greet_column)
    pl.semaphore_wait(barrier, GROUPS - 1 + NCOL - 1)

    def cols(q):
        return aligned(q * QUARTER, QUARTER)

    def rows_of(s, k):
        return aligned(s * HALF + k * CHUNK, CHUNK)

    def chain_copy(s, j, k, from_own):
        rows = rows_of(s, k)
        ll, dd = (up_l, up_d) if s == 0 else (down_l, down_d)
        if from_own:
            src = head.at[rows, cols((1 - h) * 2 + (c if j == 0 else 1 - c))]
            dst = heads.at[d, rows, :] if j == 0 else passing.at[rows, :]
        else:
            src = heads.at[opp, rows, :] if j == 0 else passing.at[rows, :]
            dst = src
        return remote(src, dst, chain_send.at[s, j, k], chain_recv.at[s, j, k], ll, v, dd)

    ends = (l == LAYERS - 1, l == 0)
    relays = (l != LAYERS - 1, l != 0)

    def source(s):
        def one(k):
            chain_copy(s, 0, k, True).start()
            chain_copy(s, 1, k, True).start()

        @pl.when(ends[s])
        def _():
            each(0, CHUNKS, one)

    def chain(lo, hi):
        def one(k):
            for s in (0, 1):
                rows = rows_of(s, k)
                arrive(heads.at[opp, rows, :], chain_recv.at[s, 0, k])
                arrive(passing.at[rows, :], chain_recv.at[s, 1, k])

                @pl.when(relays[s])
                def _(s=s):
                    chain_copy(s, 0, k, False).start()
                    chain_copy(s, 1, k, False).start()

                remote(
                    passing.at[rows, :], heads.at[opp, rows, :],
                    pass_send.at[s, k], pass_recv.at[s, k], l, v, sib,
                ).start()

        each(lo, hi, one)

    source(0)
    source(1)
    head_copy = remote(head.at[:, cols(sib)], heads.at[d], head_send, head_recv, l, v, sib)
    head_copy.start()
    own_head = pltpu.make_async_copy(head.at[:, cols(d)], heads.at[d], local_sem.at[0])
    own_head.start()
    own_final = pltpu.make_async_copy(
        final.at[:, cols(d)], target.at[aligned(d * 128 + l * 32, 32), :], local_sem.at[1]
    )
    own_final.start()

    def product(n):
        at = aligned(n * 256, 256)
        partial[:, at] = jnp.dot(hidden[...], translator[:, at], preferred_element_type=f32)

    each(0, BLOCK // 256, product)

    def own_rows(p):
        return aligned(p * ROWS, ROWS)

    def scatter(k):
        p = in_plane(k)
        remote(partial.at[own_rows(p), :], parts.at[v], rs_send.at[k], rs_recv.at[v], l, p, d).start()

    each(1, GROUPS, scatter)

    def final_copy(k):
        m = in_column(k)
        ll, dd = lax.div(m, BLOCKS), lax.rem(m, BLOCKS)
        remote(
            final.at[:, cols(dd)], target.at[aligned(d * 128 + l * 32, 32), :],
            fin_send.at[k], fin_recv.at[column], ll, v, dd,
        ).start()

    each(1, NCOL, final_copy)

    scaled[...] = partial[own_rows(v), :] + bias[...]

    def add_part(k):
        p = in_plane(k)
        arrive(parts.at[p], rs_recv.at[p])
        scaled[...] += parts[p]

    each(1, GROUPS, add_part)
    projected = scaled[...]
    squares[d] = jnp.broadcast_to(jnp.sum(projected * projected, axis=1, keepdims=True), (ROWS, 128))

    def to_blocks(buf, send, recv):
        def go(k):
            dd = lax.rem(d + k, BLOCKS)
            remote(buf.at[d], buf.at[d], send.at[k], recv.at[d], l, v, dd).start()
        each(1, BLOCKS, go)

    def from_blocks(buf, recv):
        def come(k):
            dd = lax.rem(d + k, BLOCKS)
            arrive(buf.at[dd], recv.at[dd])
        each(1, BLOCKS, come)

    to_blocks(squares, sq_send, sq_recv)
    chain(0, 4)
    from_blocks(squares, sq_recv)
    inverse = lax.rsqrt(jnp.sum(squares[...], axis=0)[:, :1] / D + epsilon)
    scaled[...] = projected * inverse
    normed[d, own_rows(v), :] = (scaled[...] * gain[...]).astype(bf16)

    mine = normed.at[d, own_rows(v), :]
    opp_copy = remote(mine, mine, opp_send, opp_recv, l, v, opp)
    opp_copy.start()

    def gather(block, i):
        def go(k):
            ref = normed.at[block, own_rows(v), :]
            remote(ref, ref, ag_send.at[i, k], ag_recv.at[i, v], l, in_plane(k), d).start()
        each(1, GROUPS, go)

    def gathered(block, i):
        def come(k):
            p = in_plane(k)
            arrive(normed.at[block, own_rows(p), :], ag_recv.at[i, p])
        each(1, GROUPS, come)

    gather(d, 0)
    chain(4, 6)
    arrive(normed.at[opp, own_rows(v), :], opp_recv)
    gather(opp, 1)
    chain(6, 8)
    gathered(d, 0)
    sib_copy0 = remote(normed.at[d], normed.at[d], sib_send.at[0], sib_recv.at[0], l, v, sib)
    sib_copy0.start()
    chain(8, 10)
    gathered(opp, 1)
    sib_copy1 = remote(normed.at[opp], normed.at[opp], sib_send.at[1], sib_recv.at[1], l, v, sib)
    sib_copy1.start()
    own_head.wait()
    own_final.wait()

    def multiply(block, first):
        def go(n):
            at = aligned(n * 256, 256)
            value = jnp.dot(normed[block], heads[block, :, at], preferred_element_type=f32)
            if first:
                logits[:, at] = value
            else:
                logits[:, at] += value
        each(0, QUARTER // 256, go)

    multiply(d, True)
    chain(10, 13)
    arrive(normed.at[sib], sib_recv.at[0])
    arrive(heads.at[sib], head_recv)
    multiply(sib, False)
    chain(13, CHUNKS)
    multiply(opp, False)
    arrive(normed.at[opp_sib], sib_recv.at[1])

    def passed(k):
        for s in (0, 1):
            arrive(heads.at[opp_sib, rows_of(s, k), :], pass_recv.at[s, k])

    each(0, CHUNKS, passed)
    multiply(opp_sib, False)

    def final_arrived(k):
        m = in_column(k)
        ll, dd = lax.div(m, BLOCKS), lax.rem(m, BLOCKS)
        arrive(target.at[aligned(dd * 128 + ll * 32, 32), :], fin_recv.at[m])

    each(1, NCOL, final_arrived)

    def local_stats(t):
        at = aligned(t * 128, 128)
        want = target[at, :].astype(f32)
        have = logits[at, :]
        want_top = jnp.max(want, axis=1, keepdims=True)
        want_exp = jnp.exp(want - want_top)
        have_top = jnp.max(have, axis=1, keepdims=True)
        have_sum = jnp.sum(jnp.exp(have - have_top), axis=1, keepdims=True)
        want_sum = jnp.sum(want_exp, axis=1, keepdims=True)
        cross = jnp.sum(want_exp * (want - have), axis=1, keepdims=True)
        lane = lax.broadcasted_iota(jnp.int32, (128, 128), 1)
        packed = jnp.where(
            lane == 0, want_top,
            jnp.where(
                lane == 1, want_sum,
                jnp.where(lane == 2, cross, jnp.where(lane == 3, have_top, have_sum)),
            ),
        )
        stats[v, :, at] = packed.T[0:8, :]

    each(0, TOKENS // 128, local_stats)

    def stats_out(k):
        remote(stats.at[v], stats.at[v], st_send.at[k], st_recv.at[v], l, in_plane(k), d).start()

    def stats_in(k):
        p = in_plane(k)
        arrive(stats.at[p], st_recv.at[p])

    each(1, GROUPS, stats_out)
    each(1, GROUPS, stats_in)

    def merge(buf):
        want_top = jnp.max(buf[:, 0, :], axis=0, keepdims=True)
        have_top = jnp.max(buf[:, 3, :], axis=0, keepdims=True)
        want_scale = jnp.exp(buf[:, 0, :] - want_top)
        have_scale = jnp.exp(buf[:, 3, :] - have_top)
        want_sum = jnp.sum(buf[:, 1, :] * want_scale, axis=0, keepdims=True)
        cross = jnp.sum(buf[:, 2, :] * want_scale, axis=0, keepdims=True)
        have_sum = jnp.sum(buf[:, 4, :] * have_scale, axis=0, keepdims=True)
        return want_top, want_sum, cross, have_top, have_sum

    merged = merge(stats)
    stats2[d] = jnp.concatenate(merged + merged[2:], axis=0)
    to_blocks(stats2, st2_send, st2_recv)
    from_blocks(stats2, st2_recv)
    want_top, want_sum, cross, have_top, have_sum = merge(stats2)
    want_lse = want_top + jnp.log(want_sum)
    have_lse = have_top + jnp.log(have_sum)
    per_token = cross / want_sum + (have_lse - want_lse)
    div_out[...] = jnp.broadcast_to(jnp.sum(per_token, axis=1, keepdims=True) / TOKENS, (8, 128))
    ends_lse[0:1, :] = want_lse
    ends_lse[1:2, :] = have_lse
    ends_lse[2:8, :] = jnp.zeros((6, TOKENS), f32)

    def grad_rows(t):
        at = aligned(t * 128, 128)
        both = jnp.concatenate([ends_lse[:, at]] * 16, axis=0).T
        want = jnp.exp(target[at, :].astype(f32) - both[:, 0:1])
        have = jnp.exp(logits[at, :] - both[:, 1:2])
        grads[at, :] = (have - want).astype(bf16)

    each(0, TOKENS // 128, grad_rows)

    def back(block, write):
        def go(n):
            at = aligned(n * 256, 256)
            write(
                at,
                lax.dot_general(
                    grads[...], heads[block, at, :], (((1,), (1,)), ((), ())),
                    preferred_element_type=f32,
                ),
            )
        each(0, BLOCK // 256, go)

    def crossing_copy(i):
        return remote(crossing.at[i], crossed.at[i], gx_send.at[i], gx_recv.at[i], l, v, sib)

    for i, block in ((0, opp_sib), (1, sib)):
        def to_crossing(at, value, i=i):
            crossing[i, :, at] = value.astype(bf16)
        back(block, to_crossing)
        crossing_copy(i).start()

    for i, block in ((0, opp), (1, d)):
        def to_logits(at, value):
            logits[:, at] = value
        back(block, to_logits)
        arrive(crossed.at[i], gx_recv.at[i])

        def add_rows(t, i=i):
            at = aligned(t * 128, 128)
            summing[i, at, :] = (logits[at, :] + crossed[i, at, :].astype(f32)).astype(bf16)
        each(0, TOKENS // 128, add_rows)

        def scatter_sum(k, i=i):
            p = in_plane(k)
            remote(
                summing.at[i, own_rows(p), :], sums.at[i, v],
                gs_send.at[i, k], gs_recv.at[i, v], l, p, d,
            ).start()
        each(1, GROUPS, scatter_sum)

    for i, out in ((0, half_sum), (1, inners)):
        if i == 0:
            out[...] = summing[0, own_rows(v), :].astype(f32)
        else:
            finals[...] = summing[1, own_rows(v), :].astype(f32)

        def add_sum(k, i=i):
            p = in_plane(k)
            arrive(sums.at[i, p], gs_recv.at[i, p])
            if i == 0:
                half_sum[...] += sums[0, p].astype(f32)
            else:
                finals[...] += sums[1, p].astype(f32)
        each(1, GROUPS, add_sum)
        if i == 0:
            go_copy = remote(half_sum, other_sum, go_send, go_recv, l, v, opp)
            go_copy.start()

    arrive(other_sum, go_recv)
    grad_scaled = (finals[...] + other_sum[...]) * gain[...]
    inners[d] = jnp.broadcast_to(
        jnp.sum(grad_scaled * scaled[...], axis=1, keepdims=True), (ROWS, 128)
    )
    to_blocks(inners, in_send, in_recv)
    from_blocks(inners, in_recv)
    inner = jnp.sum(inners[...], axis=0)[:, :1] / D
    inverse = lax.rsqrt(jnp.sum(squares[...], axis=0)[:, :1] / D + epsilon)
    grad_out[own_rows(v), :] = (inverse * (grad_scaled - scaled[...] * inner)).astype(bf16)

    def grad_go(k):
        ref = grad_out.at[own_rows(v), :]
        remote(ref, ref, gp_send.at[k], gp_recv.at[v], l, in_plane(k), d).start()

    def grad_come(k):
        p = in_plane(k)
        arrive(grad_out.at[own_rows(p), :], gp_recv.at[p])

    each(1, GROUPS, grad_go)
    each(1, GROUPS, grad_come)

    for s in (0, 1):
        def chain_sent(k, s=s):
            chain_copy(s, 0, k, False).wait_send()
            chain_copy(s, 1, k, False).wait_send()
            sent(passing.at[rows_of(s, k), :], pass_send.at[s, k])
        each(0, CHUNKS, chain_sent)
    head_copy.wait_send()
    opp_copy.wait_send()
    sib_copy0.wait_send()
    sib_copy1.wait_send()
    go_copy.wait_send()
    crossing_copy(0).wait_send()
    crossing_copy(1).wait_send()

    def plane_sent(k):
        sent(parts.at[0], rs_send.at[k])
        sent(mine, ag_send.at[0, k])
        sent(mine, ag_send.at[1, k])
        sent(stats.at[0], st_send.at[k])
        sent(sums.at[0, 0], gs_send.at[0, k])
        sent(sums.at[0, 0], gs_send.at[1, k])
        sent(grad_out.at[own_rows(v), :], gp_send.at[k])
        sent(target.at[aligned(d * 128 + l * 32, 32), :], fin_send.at[k])

    each(1, GROUPS, plane_sent)

    def blocks_sent(k):
        sent(squares.at[0], sq_send.at[k])
        sent(stats2.at[0], st2_send.at[k])
        sent(inners.at[0], in_send.at[k])

    each(1, BLOCKS, blocks_sent)


def run(hidden, translator, bias, gain, head, final):
    dma = pltpu.SemaphoreType.DMA
    vmem = pltpu.VMEM
    in_vmem = pl.BlockSpec(memory_space=pltpu.VMEM)
    anywhere = pl.BlockSpec(memory_space=pl.ANY)
    return pl.pallas_call(
        kernel,
        out_shape=[
            jax.ShapeDtypeStruct((TOKENS, BLOCK), bf16),
            jax.ShapeDtypeStruct((8, 128), f32),
        ],
        in_specs=[in_vmem] * 4 + [anywhere] * 2,
        out_specs=[in_vmem] * 2,
        scratch_shapes=[
            vmem((BLOCKS, BLOCK, QUARTER), bf16),
            vmem((BLOCK, QUARTER), bf16),
            vmem((BLOCKS, TOKENS, BLOCK), bf16),
            vmem((TOKENS, BLOCK), f32),
            vmem((GROUPS, ROWS, BLOCK), f32),
            vmem((TOKENS, QUARTER), bf16),
            vmem((ROWS, BLOCK), f32),
            vmem((BLOCKS, ROWS, 128), f32),
            vmem((TOKENS, QUARTER), f32),
            vmem((GROUPS, 8, TOKENS), f32),
            vmem((BLOCKS, 8, TOKENS), f32),
            vmem((8, TOKENS), f32),
            vmem((TOKENS, QUARTER), bf16),
            vmem((2, TOKENS, BLOCK), bf16),
            vmem((2, TOKENS, BLOCK), bf16),
            vmem((2, TOKENS, BLOCK), bf16),
            vmem((2, GROUPS, ROWS, BLOCK), bf16),
            vmem((ROWS, BLOCK), f32),
            vmem((ROWS, BLOCK), f32),
            vmem((BLOCKS, ROWS, 128), f32),
            vmem((ROWS, BLOCK), f32),
            dma((2, 2, CHUNKS)), dma((2, 2, CHUNKS)),
            dma((2, CHUNKS)), dma((2, CHUNKS)),
            dma, dma,
            dma((16,)), dma((16,)),
            dma((GROUPS,)), dma((GROUPS,)),
            dma((BLOCKS,)), dma((BLOCKS,)),
            dma((2, GROUPS)), dma((2, GROUPS)),
            dma, dma,
            dma((2,)), dma((2,)),
            dma((GROUPS,)), dma((GROUPS,)),
            dma((BLOCKS,)), dma((BLOCKS,)),
            dma((2,)), dma((2,)),
            dma((2, GROUPS)), dma((2, GROUPS)),
            dma, dma,
            dma((BLOCKS,)), dma((BLOCKS,)),
            dma((GROUPS,)), dma((GROUPS,)),
            dma((2,)),
        ],
        compiler_params=pltpu.CompilerParams(
            collective_id=0, has_side_effects=True, vmem_limit_bytes=56 * 1024 * 1024
        ),
        name="lens",
    )(hidden, translator, bias, gain, head, final)


def shards(hidden, translator, bias, gain, head, final_logits):
    features = hidden[0]
    grad_projected, divergence = run(
        features, translator[0], bias, gain[None], head, final_logits[0]
    )
    grad_weights = lax.dot_general(
        features, grad_projected, (((0,), (0,)), ((), ())), preferred_element_type=f32
    )
    grad_offsets = jnp.sum(grad_projected.astype(f32), axis=0)
    return (grad_weights[None], grad_offsets[None], divergence[0, :1])


def solution(mesh):
    in_specs = (
        P("layer", None, "vocab"),
        P("layer", "vocab", "dp"),
        P("layer", "dp"),
        P("dp"),
        P("dp", "vocab"),
        P("dp", "layer", "vocab"),
    )
    out_specs = (P("layer", "vocab", "dp"), P("layer", "dp"), P("layer"))
    return jax.shard_map(shards, mesh=mesh, in_specs=in_specs, out_specs=out_specs, check_vma=False)
```

```python
import jax
import jax.numpy as jnp
from jax import lax
from jax.experimental import pallas as pl
from jax.experimental.pallas import tpu as pltpu
from jax.sharding import PartitionSpec as P

D = 4096
TOKENS = 512
LAYERS = 4
GROUPS = 16
BLOCKS = 4
BLOCK = D // BLOCKS
QUARTER = 1024
ROWS = TOKENS // GROUPS
HALF = BLOCK // 2
CHUNK = 32
CHUNKS = HALF // CHUNK

epsilon = 1e-05
f32 = jnp.float32
bf16 = jnp.bfloat16
MESH = pl.DeviceIdType.MESH


def aligned(start, size, unit=None):
    return pl.ds(pl.multiple_of(start, unit or size), size)


def kernel(
    hidden, translator, bias, gain, head, final, grad_out, div_out,
    heads, passing, normed, partial, parts, target, scaled, squares, logits, stats, stats2, ends_lse,
    grads, crossing, crossed, summing, sums, half_sum, other_sum, inners, finals,
    chain_send, chain_recv, pass_send, pass_recv, head_send, head_recv, fin_send, fin_recv,
    rs_send, rs_recv, sq_send, sq_recv, ag_send, ag_recv, opp_send, opp_recv, sib_send, sib_recv,
    st_send, st_recv, st2_send, st2_recv, gx_send, gx_recv, gs_send, gs_recv, go_send, go_recv,
    in_send, in_recv, gp_send, gp_recv, local_sem,
):
    l = lax.axis_index("layer")
    v = lax.axis_index("vocab")
    d = lax.axis_index("dp")
    h = lax.div(d, 2)
    c = lax.rem(d, 2)
    sib = h * 2 + 1 - c
    opp = lax.rem(d + 2, BLOCKS)
    opp_sib = (1 - h) * 2 + 1 - c
    up_l = lax.rem(l + 1, LAYERS)
    up_d = lax.rem(d + 2 * lax.div(l + 1, LAYERS), BLOCKS)
    down_l = lax.rem(l + LAYERS - 1, LAYERS)
    down_d = lax.rem(d + 2 * (1 - lax.div(l + LAYERS - 1, LAYERS)), BLOCKS)
    column = l * BLOCKS + d
    NCOL = LAYERS * BLOCKS

    def in_plane(k):
        return lax.rem(v + k, GROUPS)

    def in_column(k):
        return lax.rem(column + k, NCOL)

    def remote(src, dst, send, recv, ll, vv, dd):
        return pltpu.make_async_remote_copy(
            src_ref=src, dst_ref=dst, send_sem=send, recv_sem=recv,
            device_id=(ll, vv, dd), device_id_type=MESH,
        )

    def arrive(dst, sem):
        remote(dst, dst, sem, sem, l, v, d).wait_recv()

    def sent(src, sem):
        remote(src, src, sem, sem, l, v, d).wait_send()

    def each(lo, hi, f):
        def step(k, carry):
            f(k)
            return carry
        lax.fori_loop(lo, hi, step, 0)

    barrier = pltpu.get_barrier_semaphore()

    def greet_plane(k):
        pl.semaphore_signal(barrier, inc=1, device_id=(l, in_plane(k), d), device_id_type=MESH)

    def greet_column(k):
        m = in_column(k)
        pl.semaphore_signal(
            barrier, inc=1, device_id=(lax.div(m, BLOCKS), v, lax.rem(m, BLOCKS)), device_id_type=MESH
        )

    each(1, GROUPS, greet_plane)
    each(1, NCOL, greet_column)
    pl.semaphore_wait(barrier, GROUPS - 1 + NCOL - 1)

    def cols(q):
        return aligned(q * QUARTER, QUARTER)

    def rows_of(s, k):
        return aligned(s * HALF + k * CHUNK, CHUNK)

    def chain_copy(s, j, k, from_own):
        rows = rows_of(s, k)
        ll, dd = (up_l, up_d) if s == 0 else (down_l, down_d)
        if from_own:
            src = head.at[rows, cols((1 - h) * 2 + (c if j == 0 else 1 - c))]
            dst = heads.at[d, rows, :] if j == 0 else passing.at[rows, :]
        else:
            src = heads.at[opp, rows, :] if j == 0 else passing.at[rows, :]
            dst = src
        return remote(src, dst, chain_send.at[s, j, k], chain_recv.at[s, j, k], ll, v, dd)

    ends = (l == LAYERS - 1, l == 0)
    relays = (l != LAYERS - 1, l != 0)

    def source(s):
        def one(k):
            chain_copy(s, 0, k, True).start()
            chain_copy(s, 1, k, True).start()

        @pl.when(ends[s])
        def _():
            each(0, CHUNKS, one)

    lag = (l, LAYERS - 1 - l)
    TURNS = CHUNKS + LAYERS - 1

    def chain(lo, hi):
        def one(turn):
            for s in (0, 1):
                k = turn - lag[s]

                @pl.when(jnp.logical_and(k >= 0, k < CHUNKS))
                def _(s=s, k=k):
                    rows = rows_of(s, k)
                    arrive(heads.at[opp, rows, :], chain_recv.at[s, 0, k])
                    arrive(passing.at[rows, :], chain_recv.at[s, 1, k])

                    @pl.when(relays[s])
                    def _():
                        chain_copy(s, 0, k, False).start()
                        chain_copy(s, 1, k, False).start()

                    remote(
                        passing.at[rows, :], heads.at[opp, rows, :],
                        pass_send.at[s, k], pass_recv.at[s, k], l, v, sib,
                    ).start()

        each(lo, hi, one)

    source(0)
    source(1)
    head_copy = remote(head.at[:, cols(sib)], heads.at[d], head_send, head_recv, l, v, sib)
    head_copy.start()
    own_head = pltpu.make_async_copy(head.at[:, cols(d)], heads.at[d], local_sem.at[0])
    own_head.start()
    own_final = pltpu.make_async_copy(
        final.at[:, cols(d)], target.at[aligned(d * 128 + l * 32, 32), :], local_sem.at[1]
    )
    own_final.start()

    def product(n):
        at = aligned(n * 256, 256)
        partial[:, at] = jnp.dot(hidden[...], translator[:, at], preferred_element_type=f32)

    each(0, BLOCK // 256, product)

    def own_rows(p):
        return aligned(p * ROWS, ROWS)

    def scatter(k):
        p = in_plane(k)
        remote(partial.at[own_rows(p), :], parts.at[v], rs_send.at[k], rs_recv.at[v], l, p, d).start()

    each(1, GROUPS, scatter)

    def final_copy(k):
        m = in_column(k)
        ll, dd = lax.div(m, BLOCKS), lax.rem(m, BLOCKS)
        remote(
            final.at[:, cols(dd)], target.at[aligned(d * 128 + l * 32, 32), :],
            fin_send.at[k], fin_recv.at[column], ll, v, dd,
        ).start()

    each(1, NCOL, final_copy)

    scaled[...] = partial[own_rows(v), :] + bias[...]
    chain(0, 6)

    def add_part(k):
        p = in_plane(k)
        arrive(parts.at[p], rs_recv.at[p])
        scaled[...] += parts[p]

    each(1, GROUPS, add_part)
    projected = scaled[...]
    squares[d] = jnp.broadcast_to(jnp.sum(projected * projected, axis=1, keepdims=True), (ROWS, 128))

    def to_blocks(buf, send, recv):
        def go(k):
            dd = lax.rem(d + k, BLOCKS)
            remote(buf.at[d], buf.at[d], send.at[k], recv.at[d], l, v, dd).start()
        each(1, BLOCKS, go)

    def from_blocks(buf, recv):
        def come(k):
            dd = lax.rem(d + k, BLOCKS)
            arrive(buf.at[dd], recv.at[dd])
        each(1, BLOCKS, come)

    to_blocks(squares, sq_send, sq_recv)
    chain(6, 8)
    from_blocks(squares, sq_recv)
    inverse = lax.rsqrt(jnp.sum(squares[...], axis=0)[:, :1] / D + epsilon)
    scaled[...] = projected * inverse
    normed[d, own_rows(v), :] = (scaled[...] * gain[...]).astype(bf16)

    mine = normed.at[d, own_rows(v), :]
    opp_copy = remote(mine, mine, opp_send, opp_recv, l, v, opp)
    opp_copy.start()

    def gather(block, i):
        def go(k):
            ref = normed.at[block, own_rows(v), :]
            remote(ref, ref, ag_send.at[i, k], ag_recv.at[i, v], l, in_plane(k), d).start()
        each(1, GROUPS, go)

    def gathered(block, i):
        def come(k):
            p = in_plane(k)
            arrive(normed.at[block, own_rows(p), :], ag_recv.at[i, p])
        each(1, GROUPS, come)

    gather(d, 0)
    chain(8, 10)
    arrive(normed.at[opp, own_rows(v), :], opp_recv)
    gather(opp, 1)
    chain(10, 12)
    gathered(d, 0)
    sib_copy0 = remote(normed.at[d], normed.at[d], sib_send.at[0], sib_recv.at[0], l, v, sib)
    sib_copy0.start()
    chain(12, 14)
    gathered(opp, 1)
    sib_copy1 = remote(normed.at[opp], normed.at[opp], sib_send.at[1], sib_recv.at[1], l, v, sib)
    sib_copy1.start()
    own_head.wait()
    own_final.wait()

    def multiply(block, first):
        def go(n):
            at = aligned(n * 256, 256)
            value = jnp.dot(normed[block], heads[block, :, at], preferred_element_type=f32)
            if first:
                logits[:, at] = value
            else:
                logits[:, at] += value
        each(0, QUARTER // 256, go)

    multiply(d, True)
    chain(14, 15)
    arrive(normed.at[sib], sib_recv.at[0])
    arrive(heads.at[sib], head_recv)
    multiply(sib, False)
    chain(15, TURNS)
    multiply(opp, False)
    arrive(normed.at[opp_sib], sib_recv.at[1])

    def passed(k):
        for s in (0, 1):
            arrive(heads.at[opp_sib, rows_of(s, k), :], pass_recv.at[s, k])

    each(0, CHUNKS, passed)
    multiply(opp_sib, False)

    def final_arrived(k):
        m = in_column(k)
        ll, dd = lax.div(m, BLOCKS), lax.rem(m, BLOCKS)
        arrive(target.at[aligned(dd * 128 + ll * 32, 32), :], fin_recv.at[m])

    each(1, NCOL, final_arrived)

    def local_stats(t):
        at = aligned(t * 128, 128)
        want = target[at, :].astype(f32)
        have = logits[at, :]
        want_top = jnp.max(want, axis=1, keepdims=True)
        want_exp = jnp.exp(want - want_top)
        have_top = jnp.max(have, axis=1, keepdims=True)
        have_sum = jnp.sum(jnp.exp(have - have_top), axis=1, keepdims=True)
        want_sum = jnp.sum(want_exp, axis=1, keepdims=True)
        cross = jnp.sum(want_exp * (want - have), axis=1, keepdims=True)
        lane = lax.broadcasted_iota(jnp.int32, (128, 128), 1)
        packed = jnp.where(
            lane == 0, want_top,
            jnp.where(
                lane == 1, want_sum,
                jnp.where(lane == 2, cross, jnp.where(lane == 3, have_top, have_sum)),
            ),
        )
        stats[v, :, at] = packed.T[0:8, :]

    each(0, TOKENS // 128, local_stats)

    def stats_out(k):
        remote(stats.at[v], stats.at[v], st_send.at[k], st_recv.at[v], l, in_plane(k), d).start()

    def stats_in(k):
        p = in_plane(k)
        arrive(stats.at[p], st_recv.at[p])

    each(1, GROUPS, stats_out)
    each(1, GROUPS, stats_in)

    def merge(buf):
        want_top = jnp.max(buf[:, 0, :], axis=0, keepdims=True)
        have_top = jnp.max(buf[:, 3, :], axis=0, keepdims=True)
        want_scale = jnp.exp(buf[:, 0, :] - want_top)
        have_scale = jnp.exp(buf[:, 3, :] - have_top)
        want_sum = jnp.sum(buf[:, 1, :] * want_scale, axis=0, keepdims=True)
        cross = jnp.sum(buf[:, 2, :] * want_scale, axis=0, keepdims=True)
        have_sum = jnp.sum(buf[:, 4, :] * have_scale, axis=0, keepdims=True)
        return want_top, want_sum, cross, have_top, have_sum

    merged = merge(stats)
    stats2[d] = jnp.concatenate(merged + merged[2:], axis=0)
    to_blocks(stats2, st2_send, st2_recv)
    from_blocks(stats2, st2_recv)
    want_top, want_sum, cross, have_top, have_sum = merge(stats2)
    want_lse = want_top + jnp.log(want_sum)
    have_lse = have_top + jnp.log(have_sum)
    per_token = cross / want_sum + (have_lse - want_lse)
    div_out[...] = jnp.broadcast_to(jnp.sum(per_token, axis=1, keepdims=True) / TOKENS, (8, 128))
    ends_lse[0:1, :] = want_lse
    ends_lse[1:2, :] = have_lse
    ends_lse[2:8, :] = jnp.zeros((6, TOKENS), f32)

    def grad_rows(t):
        at = aligned(t * 128, 128)
        both = jnp.concatenate([ends_lse[:, at]] * 16, axis=0).T
        want = jnp.exp(target[at, :].astype(f32) - both[:, 0:1])
        have = jnp.exp(logits[at, :] - both[:, 1:2])
        grads[at, :] = (have - want).astype(bf16)

    each(0, TOKENS // 128, grad_rows)

    def back(block, write):
        def go(n):
            at = aligned(n * 256, 256)
            write(
                at,
                lax.dot_general(
                    grads[...], heads[block, at, :], (((1,), (1,)), ((), ())),
                    preferred_element_type=f32,
                ),
            )
        each(0, BLOCK // 256, go)

    def crossing_copy(i):
        return remote(crossing.at[i], crossed.at[i], gx_send.at[i], gx_recv.at[i], l, v, sib)

    for i, block in ((0, opp_sib), (1, sib)):
        def to_crossing(at, value, i=i):
            crossing[i, :, at] = value.astype(bf16)
        back(block, to_crossing)
        crossing_copy(i).start()

    for i, block in ((0, opp), (1, d)):
        def to_logits(at, value):
            logits[:, at] = value
        back(block, to_logits)
        arrive(crossed.at[i], gx_recv.at[i])

        def add_rows(t, i=i):
            at = aligned(t * 128, 128)
            summing[i, at, :] = (logits[at, :] + crossed[i, at, :].astype(f32)).astype(bf16)
        each(0, TOKENS // 128, add_rows)

        def scatter_sum(k, i=i):
            p = in_plane(k)
            remote(
                summing.at[i, own_rows(p), :], sums.at[i, v],
                gs_send.at[i, k], gs_recv.at[i, v], l, p, d,
            ).start()
        each(1, GROUPS, scatter_sum)

    for i, out in ((0, half_sum), (1, inners)):
        if i == 0:
            out[...] = summing[0, own_rows(v), :].astype(f32)
        else:
            finals[...] = summing[1, own_rows(v), :].astype(f32)

        def add_sum(k, i=i):
            p = in_plane(k)
            arrive(sums.at[i, p], gs_recv.at[i, p])
            if i == 0:
                half_sum[...] += sums[0, p].astype(f32)
            else:
                finals[...] += sums[1, p].astype(f32)
        each(1, GROUPS, add_sum)
        if i == 0:
            go_copy = remote(half_sum, other_sum, go_send, go_recv, l, v, opp)
            go_copy.start()

    arrive(other_sum, go_recv)
    grad_scaled = (finals[...] + other_sum[...]) * gain[...]
    inners[d] = jnp.broadcast_to(
        jnp.sum(grad_scaled * scaled[...], axis=1, keepdims=True), (ROWS, 128)
    )
    to_blocks(inners, in_send, in_recv)
    from_blocks(inners, in_recv)
    inner = jnp.sum(inners[...], axis=0)[:, :1] / D
    inverse = lax.rsqrt(jnp.sum(squares[...], axis=0)[:, :1] / D + epsilon)
    grad_out[own_rows(v), :] = (inverse * (grad_scaled - scaled[...] * inner)).astype(bf16)

    def grad_go(k):
        ref = grad_out.at[own_rows(v), :]
        remote(ref, ref, gp_send.at[k], gp_recv.at[v], l, in_plane(k), d).start()

    def grad_come(k):
        p = in_plane(k)
        arrive(grad_out.at[own_rows(p), :], gp_recv.at[p])

    each(1, GROUPS, grad_go)
    each(1, GROUPS, grad_come)

    for s in (0, 1):
        def chain_sent(k, s=s):
            chain_copy(s, 0, k, False).wait_send()
            chain_copy(s, 1, k, False).wait_send()
            sent(passing.at[rows_of(s, k), :], pass_send.at[s, k])
        each(0, CHUNKS, chain_sent)
    head_copy.wait_send()
    opp_copy.wait_send()
    sib_copy0.wait_send()
    sib_copy1.wait_send()
    go_copy.wait_send()
    crossing_copy(0).wait_send()
    crossing_copy(1).wait_send()

    def plane_sent(k):
        sent(parts.at[0], rs_send.at[k])
        sent(mine, ag_send.at[0, k])
        sent(mine, ag_send.at[1, k])
        sent(stats.at[0], st_send.at[k])
        sent(sums.at[0, 0], gs_send.at[0, k])
        sent(sums.at[0, 0], gs_send.at[1, k])
        sent(grad_out.at[own_rows(v), :], gp_send.at[k])
        sent(target.at[aligned(d * 128 + l * 32, 32), :], fin_send.at[k])

    each(1, GROUPS, plane_sent)

    def blocks_sent(k):
        sent(squares.at[0], sq_send.at[k])
        sent(stats2.at[0], st2_send.at[k])
        sent(inners.at[0], in_send.at[k])

    each(1, BLOCKS, blocks_sent)


def run(hidden, translator, bias, gain, head, final):
    dma = pltpu.SemaphoreType.DMA
    vmem = pltpu.VMEM
    in_vmem = pl.BlockSpec(memory_space=pltpu.VMEM)
    anywhere = pl.BlockSpec(memory_space=pl.ANY)
    return pl.pallas_call(
        kernel,
        out_shape=[
            jax.ShapeDtypeStruct((TOKENS, BLOCK), bf16),
            jax.ShapeDtypeStruct((8, 128), f32),
        ],
        in_specs=[in_vmem] * 4 + [anywhere] * 2,
        out_specs=[in_vmem] * 2,
        scratch_shapes=[
            vmem((BLOCKS, BLOCK, QUARTER), bf16),
            vmem((BLOCK, QUARTER), bf16),
            vmem((BLOCKS, TOKENS, BLOCK), bf16),
            vmem((TOKENS, BLOCK), f32),
            vmem((GROUPS, ROWS, BLOCK), f32),
            vmem((TOKENS, QUARTER), bf16),
            vmem((ROWS, BLOCK), f32),
            vmem((BLOCKS, ROWS, 128), f32),
            vmem((TOKENS, QUARTER), f32),
            vmem((GROUPS, 8, TOKENS), f32),
            vmem((BLOCKS, 8, TOKENS), f32),
            vmem((8, TOKENS), f32),
            vmem((TOKENS, QUARTER), bf16),
            vmem((2, TOKENS, BLOCK), bf16),
            vmem((2, TOKENS, BLOCK), bf16),
            vmem((2, TOKENS, BLOCK), bf16),
            vmem((2, GROUPS, ROWS, BLOCK), bf16),
            vmem((ROWS, BLOCK), f32),
            vmem((ROWS, BLOCK), f32),
            vmem((BLOCKS, ROWS, 128), f32),
            vmem((ROWS, BLOCK), f32),
            dma((2, 2, CHUNKS)), dma((2, 2, CHUNKS)),
            dma((2, CHUNKS)), dma((2, CHUNKS)),
            dma, dma,
            dma((16,)), dma((16,)),
            dma((GROUPS,)), dma((GROUPS,)),
            dma((BLOCKS,)), dma((BLOCKS,)),
            dma((2, GROUPS)), dma((2, GROUPS)),
            dma, dma,
            dma((2,)), dma((2,)),
            dma((GROUPS,)), dma((GROUPS,)),
            dma((BLOCKS,)), dma((BLOCKS,)),
            dma((2,)), dma((2,)),
            dma((2, GROUPS)), dma((2, GROUPS)),
            dma, dma,
            dma((BLOCKS,)), dma((BLOCKS,)),
            dma((GROUPS,)), dma((GROUPS,)),
            dma((2,)),
        ],
        compiler_params=pltpu.CompilerParams(
            collective_id=0, has_side_effects=True, vmem_limit_bytes=56 * 1024 * 1024
        ),
        name="lens",
    )(hidden, translator, bias, gain, head, final)


def shards(hidden, translator, bias, gain, head, final_logits):
    features = hidden[0]
    grad_projected, divergence = run(
        features, translator[0], bias, gain[None], head, final_logits[0]
    )
    grad_weights = lax.dot_general(
        features, grad_projected, (((0,), (0,)), ((), ())), preferred_element_type=f32
    )
    grad_offsets = jnp.sum(grad_projected.astype(f32), axis=0)
    return (grad_weights[None], grad_offsets[None], divergence[0, :1])


def solution(mesh):
    in_specs = (
        P("layer", None, "vocab"),
        P("layer", "vocab", "dp"),
        P("layer", "dp"),
        P("dp"),
        P("dp", "vocab"),
        P("dp", "layer", "vocab"),
    )
    out_specs = (P("layer", "vocab", "dp"), P("layer", "dp"), P("layer"))
    return jax.shard_map(shards, mesh=mesh, in_specs=in_specs, out_specs=out_specs, check_vma=False)
```

```python
import jax
import jax.numpy as jnp
from jax import lax
from jax.experimental import pallas as pl
from jax.experimental.pallas import tpu as pltpu
from jax.sharding import PartitionSpec as P

D = 4096
TOKENS = 512
LAYERS = 4
GROUPS = 16
SIDE = 4
BLOCKS = 4
BLOCK = D // BLOCKS
QUARTER = 1024
ROWS = TOKENS // GROUPS
TILE = 128
HALF = BLOCK // 2
CHUNK = 16
CHUNKS = HALF // CHUNK
LAG = 3

epsilon = 1e-05
f32 = jnp.float32
bf16 = jnp.bfloat16
MESH = pl.DeviceIdType.MESH


def aligned(start, size):
    return pl.ds(pl.multiple_of(start, size), size)


def each(lo, hi, f):
    def step(k, carry):
        f(k)
        return carry

    lax.fori_loop(lo, hi, step, 0)


def kernel(
    hidden, translator, bias, gain, head, final, weights_out, offsets_out, div_out,
    heads, passing, normed, partial, target, final_own, pad, scaled, squares, logits,
    top_stats, want_lse, stats, stats2, lse, cross, inner, crosses, crosses2, grads, crossing, crossed, summing,
    parts, part_mid, part_end, sum_parts, sum_mid, sum_end, half_sum, other_sum, finals, gathered_grad,
    chain_send, chain_recv, pass_send, pass_recv, head_send, head_recv, fin_send, fin_recv,
    sq_send, sq_recv, opp_send, opp_recv, sib_send, sib_recv,
    top_send, top_recv, wl_send, wl_recv, st_send, st_recv, st2_send, st2_recv, cr_send, cr_recv,
    cr2_send, cr2_recv, gx_send, gx_recv, rs_send, rs_recv, ag_send, ag_recv,
    go_send, go_recv, local_sem,
):
    l = lax.axis_index("layer")
    v = lax.axis_index("vocab")
    d = lax.axis_index("dp")
    y = lax.div(v, SIDE)
    x = lax.rem(v, SIDE)
    h = lax.div(d, 2)
    c = lax.rem(d, 2)
    sib = h * 2 + 1 - c
    opp = lax.rem(d + 2, BLOCKS)
    opp_sib = (1 - h) * 2 + 1 - c
    up_l = lax.rem(l + 1, LAYERS)
    up_d = lax.rem(d + 2 * lax.div(l + 1, LAYERS), BLOCKS)
    down_l = lax.rem(l + LAYERS - 1, LAYERS)
    down_d = lax.rem(d + 2 * (1 - lax.div(l + LAYERS - 1, LAYERS)), BLOCKS)
    column = l * BLOCKS + d
    NCOL = LAYERS * BLOCKS

    def in_plane(k):
        return lax.rem(v + k, GROUPS)

    def in_column(k):
        return lax.rem(column + k, NCOL)

    def along_x(k):
        return lax.rem(x + k, SIDE)

    def along_y(k):
        return lax.rem(y + k, SIDE)

    def remote(src, dst, send, recv, ll, vv, dd):
        return pltpu.make_async_remote_copy(
            src_ref=src, dst_ref=dst, send_sem=send, recv_sem=recv,
            device_id=(ll, vv, dd), device_id_type=MESH,
        )

    def arrive(dst, sem):
        remote(dst, dst, sem, sem, l, v, d).wait_recv()

    def sent(src, sem):
        remote(src, src, sem, sem, l, v, d).wait_send()

    leaving = []

    def drain():
        for f in leaving:
            f()

    def start_each(count, make, send, shape):
        each(1, count, lambda k: make(k).start())
        leaving.append(lambda: each(1, count, lambda k: sent(shape, send.at[k])))

    def cols(q):
        return aligned(q * QUARTER, QUARTER)

    def own_rows(p):
        return aligned(p * ROWS, ROWS)

    own_head = pltpu.make_async_copy(head.at[:, cols(d)], heads.at[d], local_sem.at[0])
    own_head.start()
    own_rows_final = aligned(d * TILE + l * ROWS, ROWS)
    own_final = pltpu.make_async_copy(final.at[:, cols(d)], target.at[own_rows_final, :], local_sem.at[1])
    own_final.start()
    whole_final = pltpu.make_async_copy(final, final_own, local_sem.at[2])
    whole_final.start()

    barrier = pltpu.get_barrier_semaphore()

    def greet_plane(k):
        pl.semaphore_signal(barrier, inc=1, device_id=(l, in_plane(k), d), device_id_type=MESH)

    def greet_column(k):
        m = in_column(k)
        pl.semaphore_signal(
            barrier, inc=1, device_id=(lax.div(m, BLOCKS), v, lax.rem(m, BLOCKS)), device_id_type=MESH
        )

    each(1, GROUPS, greet_plane)
    each(1, NCOL, greet_column)

    def product(n):
        at = aligned(n * 256, 256)
        value = jnp.dot(hidden[...], translator[:, at], preferred_element_type=f32)
        partial[:, :, :, at] = value.reshape(SIDE, SIDE, ROWS, 256)

    each(0, BLOCK // 256, product)
    pl.semaphore_wait(barrier, GROUPS - 1 + NCOL - 1)

    def rows_of(s, k):
        return aligned(s * HALF + k * CHUNK, CHUNK)

    def chain_copy(s, j, k, from_own):
        rows = rows_of(s, k)
        ll, dd = (up_l, up_d) if s == 0 else (down_l, down_d)
        if from_own:
            src = head.at[rows, cols((1 - h) * 2 + (c if j == 0 else 1 - c))]
            dst = heads.at[d, rows, :] if j == 0 else passing.at[rows, :]
        else:
            src = heads.at[opp, rows, :] if j == 0 else passing.at[rows, :]
            dst = src
        return remote(src, dst, chain_send.at[s, j, k], chain_recv.at[s, j, k], ll, v, dd)

    ends = (l == LAYERS - 1, l == 0)
    relays = (l != LAYERS - 1, l != 0)

    def source(s):
        def one(k):
            chain_copy(s, 0, k, True).start()
            chain_copy(s, 1, k, True).start()

        @pl.when(ends[s])
        def _():
            each(0, CHUNKS, one)

    def chain_sent(k):
        for s in (0, 1):
            chain_copy(s, 0, k, False).wait_send()
            chain_copy(s, 1, k, False).wait_send()
            sent(passing.at[rows_of(s, k), :], pass_send.at[s, k])

    leaving.append(lambda: each(0, CHUNKS, chain_sent))
    lag = (LAG * l, LAG * (LAYERS - 1 - l))
    TURNS = CHUNKS + LAG * (LAYERS - 1)
    done = [0]

    def chain(until):
        def one(turn):
            for s in (0, 1):
                k = turn - lag[s]

                @pl.when(jnp.logical_and(k >= 0, k < CHUNKS))
                def _(s=s, k=k):
                    rows = rows_of(s, k)
                    arrive(heads.at[opp, rows, :], chain_recv.at[s, 0, k])
                    arrive(passing.at[rows, :], chain_recv.at[s, 1, k])

                    @pl.when(relays[s])
                    def _():
                        chain_copy(s, 0, k, False).start()
                        chain_copy(s, 1, k, False).start()

                    remote(
                        passing.at[rows, :], heads.at[opp, rows, :],
                        pass_send.at[s, k], pass_recv.at[s, k], l, v, sib,
                    ).start()

        hi = int(TURNS * until)
        each(done[0], hi, one)
        done[0] = hi

    def final_copy(k):
        m = in_column(k)
        ll, dd = lax.div(m, BLOCKS), lax.rem(m, BLOCKS)
        return remote(
            final.at[:, cols(dd)], target.at[own_rows_final, :],
            fin_send.at[k], fin_recv.at[column], ll, v, dd,
        )

    left = pl.ds(0, HALF)
    right = pl.ds(HALF, HALF)

    def at_x(k):
        return y * SIDE + along_x(k)

    def at_y(k):
        return along_y(k) * SIDE + x

    def sums_start(src, part, send, recv):
        start_each(
            SIDE,
            lambda k: remote(
                src.at[:, along_x(k), :, left], part.at[0, x], send.at[0, k], recv.at[0, x], l, at_x(k), d
            ),
            send.at[0], part.at[0, 0],
        )
        start_each(
            SIDE,
            lambda k: remote(
                src.at[along_y(k), :, :, right], part.at[1, y], send.at[1, k], recv.at[1, y], l, at_y(k), d
            ),
            send.at[1], part.at[0, 0],
        )

    def sums_middle(src, part, mid, end, send, recv):
        each(1, SIDE, lambda k: arrive(part.at[0, along_x(k)], recv.at[0, along_x(k)]))
        for n in range(SIDE):
            value = src[n, x, :, left].astype(f32)
            for k in range(1, SIDE):
                value += part[0, along_x(k), n].astype(f32)
            mid[0, n] = value.astype(mid.dtype)
        start_each(
            SIDE,
            lambda k: remote(
                mid.at[0, along_y(k)], end.at[0, y], send.at[2, k], recv.at[2, y], l, at_y(k), d
            ),
            send.at[2], end.at[0, 0],
        )
        each(1, SIDE, lambda k: arrive(part.at[1, along_y(k)], recv.at[1, along_y(k)]))
        for n in range(SIDE):
            value = src[y, n, :, right].astype(f32)
            for k in range(1, SIDE):
                value += part[1, along_y(k), n].astype(f32)
            mid[1, n] = value.astype(mid.dtype)
        start_each(
            SIDE,
            lambda k: remote(
                mid.at[1, along_x(k)], end.at[1, x], send.at[3, k], recv.at[3, x], l, at_x(k), d
            ),
            send.at[3], end.at[0, 0],
        )

    def sums_end(mid, end, recv):
        each(1, SIDE, lambda k: arrive(end.at[0, along_y(k)], recv.at[2, along_y(k)]))
        each(1, SIDE, lambda k: arrive(end.at[1, along_x(k)], recv.at[3, along_x(k)]))
        value_left = mid[0, y].astype(f32)
        value_right = mid[1, x].astype(f32)
        for k in range(1, SIDE):
            value_left += end[0, along_y(k)].astype(f32)
            value_right += end[1, along_x(k)].astype(f32)
        return value_left, value_right

    def gather_start(buf, send, recv):
        my_left = buf.at[y, x, :, left]
        my_right = buf.at[y, x, :, right]
        start_each(
            SIDE, lambda k: remote(my_left, my_left, send.at[0, k], recv.at[0, x], l, at_x(k), d), send.at[0], my_left
        )
        start_each(
            SIDE, lambda k: remote(my_right, my_right, send.at[1, k], recv.at[1, y], l, at_y(k), d),
            send.at[1], my_right,
        )

    def gather_middle(buf, send, recv):
        row_left = buf.at[y, :, :, left]
        column_right = buf.at[:, x, :, right]
        each(1, SIDE, lambda k: arrive(buf.at[y, along_x(k), :, left], recv.at[0, along_x(k)]))
        start_each(
            SIDE, lambda k: remote(row_left, row_left, send.at[2, k], recv.at[2, y], l, at_y(k), d),
            send.at[2], row_left,
        )
        each(1, SIDE, lambda k: arrive(buf.at[along_y(k), x, :, right], recv.at[1, along_y(k)]))
        start_each(
            SIDE, lambda k: remote(column_right, column_right, send.at[3, k], recv.at[3, x], l, at_x(k), d),
            send.at[3], column_right,
        )

    def gather_end(buf, recv):
        each(1, SIDE, lambda k: arrive(buf.at[along_y(k), :, :, left], recv.at[2, along_y(k)]))
        each(1, SIDE, lambda k: arrive(buf.at[:, along_x(k), :, right], recv.at[3, along_x(k)]))

    source(0)
    source(1)
    sums_start(partial, parts, rs_send.at[0], rs_recv.at[0])
    start_each(NCOL, final_copy, fin_send, target.at[own_rows_final, :])
    head_copy = remote(head.at[:, cols(sib)], heads.at[d], head_send, head_recv, l, v, sib)
    head_copy.start()
    leaving.append(head_copy.wait_send)

    lane = lax.broadcasted_iota(jnp.int32, (8, TILE), 1)
    own_lanes = jnp.logical_and(lane >= l * ROWS, lane < l * ROWS + ROWS)
    pad[...] = jnp.zeros((TILE, TILE), f32)
    whole_final.wait()
    wanted = final_own[...].astype(f32)
    want_top = jnp.max(wanted, axis=1, keepdims=True)
    want_sum = jnp.sum(jnp.exp(wanted - want_top), axis=1, keepdims=True)
    column_lane = lax.broadcasted_iota(jnp.int32, (ROWS, TILE), 1)
    pad[own_rows(l), :] = jnp.where(column_lane == 0, want_top, want_sum)
    top_stats[v] = pad[...].T[0:8, :]

    def plane_copy(buf, send, recv):
        return lambda k: remote(buf.at[v], buf.at[v], send.at[k], recv.at[v], l, in_plane(k), d)

    def plane_arrive(buf, recv):
        each(1, GROUPS, lambda k: arrive(buf.at[in_plane(k)], recv.at[in_plane(k)]))

    start_each(GROUPS, plane_copy(top_stats, top_send, top_recv), top_send, top_stats.at[0])
    chain(0.2)
    sums_middle(partial, parts, part_mid, part_end, rs_send.at[0], rs_recv.at[0])
    plane_arrive(top_stats, top_recv)
    all_top = jnp.max(top_stats[:, 0:1, :], axis=0)
    all_sum = jnp.sum(top_stats[:, 1:2, :] * jnp.exp(top_stats[:, 0:1, :] - all_top[None]), axis=0)
    row_lse = all_top + jnp.log(jnp.where(own_lanes[0:1, :], all_sum, 1.0))
    want_lse[column] = jnp.broadcast_to(jnp.where(own_lanes[0:1, :], row_lse, 0.0), (8, TILE))

    def want_copy(k):
        m = in_column(k)
        return remote(
            want_lse.at[column], want_lse.at[column], wl_send.at[k], wl_recv.at[column],
            lax.div(m, BLOCKS), v, lax.rem(m, BLOCKS),
        )

    start_each(NCOL, want_copy, wl_send, want_lse.at[0])

    chain(0.26)
    value_left, value_right = sums_end(part_mid, part_end, rs_recv.at[0])
    scaled[:, left] = value_left + bias[:, left]
    scaled[:, right] = value_right + bias[:, right]
    projected = scaled[...]
    squares[d] = jnp.broadcast_to(jnp.sum(projected * projected, axis=1, keepdims=True), (ROWS, 128))

    def to_blocks(buf, send, recv):
        def copy(k):
            return remote(buf.at[d], buf.at[d], send.at[k], recv.at[d], l, v, lax.rem(d + k, BLOCKS))

        start_each(BLOCKS, copy, send, buf.at[0])

    def from_blocks(buf, recv):
        def come(k):
            dd = lax.rem(d + k, BLOCKS)
            arrive(buf.at[dd], recv.at[dd])

        each(1, BLOCKS, come)

    to_blocks(squares, sq_send, sq_recv)
    chain(0.34)
    from_blocks(squares, sq_recv)
    inverse = lax.rsqrt(jnp.sum(squares[...], axis=0)[:, :1] / D + epsilon)
    scaled[...] = projected * inverse
    normed[d, y, x] = (scaled[...] * gain[...]).astype(bf16)

    mine = normed.at[d, y, x]
    opp_copy = remote(mine, mine, opp_send, opp_recv, l, v, opp)
    opp_copy.start()
    leaving.append(opp_copy.wait_send)

    def to_sibling(block, i):
        copy = remote(normed.at[block], normed.at[block], sib_send.at[i], sib_recv.at[i], l, v, sib)
        copy.start()
        leaving.append(copy.wait_send)

    here, there = normed.at[d], normed.at[opp]
    gather_start(here, ag_send.at[0], ag_recv.at[0])
    chain(0.39)
    gather_middle(here, ag_send.at[0], ag_recv.at[0])
    arrive(normed.at[opp, y, x], opp_recv)
    gather_start(there, ag_send.at[1], ag_recv.at[1])
    chain(0.44)
    gather_middle(there, ag_send.at[1], ag_recv.at[1])
    chain(0.56)
    gather_end(here, ag_recv.at[0])
    to_sibling(d, 0)
    chain(0.66)
    gather_end(there, ag_recv.at[1])
    to_sibling(opp, 1)
    own_head.wait()
    own_final.wait()

    def multiply(block, first):
        def go(n):
            at = aligned(n * 256, 256)
            value = jnp.dot(
                normed[block].reshape(TOKENS, BLOCK), heads[block, :, at], preferred_element_type=f32
            )
            if first:
                logits[:, at] = value
            else:
                logits[:, at] += value

        each(0, QUARTER // 256, go)

    multiply(d, True)
    chain(0.74)
    arrive(normed.at[sib], sib_recv.at[0])
    arrive(heads.at[sib], head_recv)
    multiply(sib, False)
    chain(1)
    multiply(opp, False)
    arrive(normed.at[opp_sib], sib_recv.at[1])

    def passed(k):
        for s in (0, 1):
            arrive(heads.at[opp_sib, rows_of(s, k), :], pass_recv.at[s, k])

    each(0, CHUNKS, passed)
    multiply(opp_sib, False)

    for t in range(TOKENS // TILE):
        have = logits[t * TILE:(t + 1) * TILE, :]
        have_top = jnp.max(have, axis=1, keepdims=True)
        have_sum = jnp.sum(jnp.exp(have - have_top), axis=1, keepdims=True)
        tile_lane = lax.broadcasted_iota(jnp.int32, (TILE, TILE), 1)
        turned = jnp.where(tile_lane == 0, have_top, have_sum).T
        stats[v, t:t + 1, :] = turned[0:1, :]
        stats[v, 4 + t:5 + t, :] = turned[1:2, :]

    start_each(GROUPS, plane_copy(stats, st_send, st_recv), st_send, stats.at[0])

    def merge(buf):
        top = jnp.max(buf[:, 0:4, :], axis=0)
        return top, jnp.sum(buf[:, 4:8, :] * jnp.exp(buf[:, 0:4, :] - top[None]), axis=0)

    plane_arrive(stats, st_recv)
    top, total = merge(stats)
    stats2[d] = jnp.concatenate([top, total], axis=0)
    to_blocks(stats2, st2_send, st2_recv)

    def final_arrived(k):
        m = in_column(k)
        ll, dd = lax.div(m, BLOCKS), lax.rem(m, BLOCKS)
        arrive(want_lse.at[m], wl_recv.at[m])
        arrive(target.at[aligned(dd * TILE + ll * ROWS, ROWS), :], fin_recv.at[m])

    each(1, NCOL, final_arrived)
    for t in range(BLOCKS):
        lse[4 + t:5 + t, :] = (
            want_lse[t, 0:1, :] + want_lse[4 + t, 0:1, :] + want_lse[8 + t, 0:1, :] + want_lse[12 + t, 0:1, :]
        )
    from_blocks(stats2, st2_recv)
    top, total = merge(stats2)
    lse[0:4, :] = top + jnp.log(total)

    cross[...] = jnp.zeros((1, QUARTER), f32)
    for t in range(BLOCKS):
        at = pl.ds(t * TILE, TILE)
        have_lse = jnp.broadcast_to(lse[t:t + 1, :], (TILE, TILE)).T[:, 0:1]
        target_lse = jnp.broadcast_to(lse[4 + t:5 + t, :], (TILE, TILE)).T[:, 0:1]
        wanted = target[at, :].astype(f32)
        have = logits[at, :]
        want = jnp.exp(wanted - target_lse)
        grad = (jnp.exp(have - have_lse) - want).astype(bf16)
        grads[at, :] = grad
        inner[at, :] = jnp.broadcast_to(
            jnp.sum(grad.astype(f32) * have, axis=1, keepdims=True), (TILE, TILE)
        )
        cross[...] += jnp.sum(want * (wanted - have), axis=0, keepdims=True)

    def back(block, write):
        def go(n):
            at = aligned(n * 256, 256)
            write(
                at,
                lax.dot_general(
                    grads[...], heads[block, at, :], (((1,), (1,)), ((), ())),
                    preferred_element_type=f32,
                ),
            )

        each(0, BLOCK // 256, go)

    def crossing_copy(i):
        return remote(crossing.at[i], crossed.at[i], gx_send.at[i], gx_recv.at[i], l, v, sib)

    for i, block in ((0, opp_sib), (1, sib)):
        def to_crossing(at, value, i=i):
            crossing[i, :, at] = value.astype(bf16)

        back(block, to_crossing)
        crossing_copy(i).start()
        leaving.append(crossing_copy(i).wait_send)

    for i, block in ((0, opp), (1, d)):
        def to_logits(at, value):
            logits[:, at] = value

        back(block, to_logits)
        arrive(crossed.at[i], gx_recv.at[i])

        def add_rows(t, i=i):
            at = aligned(t * TILE, TILE)
            value = (logits[at, :] + crossed[i, at, :].astype(f32)).astype(bf16)
            summing[i, t] = value.reshape(SIDE, ROWS, BLOCK)

        each(0, TOKENS // TILE, add_rows)
        sums_start(summing.at[i], sum_parts.at[i], rs_send.at[1 + i], rs_recv.at[1 + i])

    for t in range(BLOCKS):
        crosses[v, t:t + 1, :] = inner[t * TILE:(t + 1) * TILE, :].T[0:1, :]
    crosses[v, 4:8, :] = jnp.broadcast_to(jnp.sum(cross[...], axis=1, keepdims=True), (4, 128))
    start_each(GROUPS, plane_copy(crosses, cr_send, cr_recv), cr_send, crosses.at[0])

    for i in (0, 1):
        sums_middle(
            summing.at[i], sum_parts.at[i], sum_mid.at[i], sum_end.at[i], rs_send.at[1 + i], rs_recv.at[1 + i]
        )
        if i == 0:
            plane_arrive(crosses, cr_recv)
            crosses2[d] = jnp.sum(crosses[...], axis=0)
            to_blocks(crosses2, cr2_send, cr2_recv)

    value_left, value_right = sums_end(sum_mid.at[0], sum_end.at[0], rs_recv.at[1])
    half_sum[:, left] = value_left.astype(bf16)
    half_sum[:, right] = value_right.astype(bf16)
    go_copy = remote(half_sum, other_sum, go_send, go_recv, l, v, opp)
    go_copy.start()
    leaving.append(go_copy.wait_send)
    value_left, value_right = sums_end(sum_mid.at[1], sum_end.at[1], rs_recv.at[2])
    finals[:, left] = value_left
    finals[:, right] = value_right
    from_blocks(crosses2, cr2_recv)
    crossed_all = jnp.sum(crosses2[...], axis=0)
    div_out[0] = (jnp.sum(crossed_all[4:5, 0:1]) + jnp.sum(lse[0:4, :] - lse[4:8, :])) / TOKENS
    lse[...] = crossed_all
    pad[...] = jnp.broadcast_to(lse[pl.ds(y, 1), :], (TILE, TILE)).T
    inner_mean = pad[own_rows(x), :][:, 0:1] / D
    arrive(other_sum, go_recv)

    grad_scaled = (finals[...] + other_sum[...].astype(f32)) * gain[...]
    inverse = lax.rsqrt(jnp.sum(squares[...], axis=0)[:, :1] / D + epsilon)
    gathered_grad[y, x] = (inverse * (grad_scaled - scaled[...] * inner_mean)).astype(bf16)
    gather_start(gathered_grad, ag_send.at[2], ag_recv.at[2])
    gather_middle(gathered_grad, ag_send.at[2], ag_recv.at[2])
    gather_end(gathered_grad, ag_recv.at[2])

    def outputs(n):
        at = aligned(n * 256, 256)
        grad = gathered_grad[:, :, :, at].reshape(TOKENS, 256)
        weights_out[0, :, at] = lax.dot_general(
            hidden[...], grad, (((0,), (0,)), ((), ())), preferred_element_type=f32
        )
        offsets_out[:, at] = jnp.sum(grad.astype(f32), axis=0, keepdims=True)

    each(0, BLOCK // 256, outputs)
    drain()


def run(hidden, translator, bias, gain, head, final):
    dma = pltpu.SemaphoreType.DMA
    vmem = pltpu.VMEM
    in_vmem = pl.BlockSpec(memory_space=pltpu.VMEM)
    anywhere = pl.BlockSpec(memory_space=pl.ANY)
    width = hidden.shape[1]
    return pl.pallas_call(
        kernel,
        out_shape=[
            jax.ShapeDtypeStruct((1, width, BLOCK), f32),
            jax.ShapeDtypeStruct((1, BLOCK), f32),
            jax.ShapeDtypeStruct((1,), f32),
        ],
        in_specs=[in_vmem] * 4 + [anywhere] * 2,
        out_specs=[in_vmem] * 2 + [pl.BlockSpec(memory_space=pltpu.SMEM)],
        scratch_shapes=[
            vmem((BLOCKS, BLOCK, QUARTER), bf16),
            vmem((BLOCK, QUARTER), bf16),
            vmem((BLOCKS, SIDE, SIDE, ROWS, BLOCK), bf16),
            vmem((SIDE, SIDE, ROWS, BLOCK), f32),
            vmem((TOKENS, QUARTER), bf16),
            vmem((ROWS, BLOCKS * QUARTER), bf16),
            vmem((TILE, TILE), f32),
            vmem((ROWS, BLOCK), f32),
            vmem((BLOCKS, ROWS, 128), f32),
            vmem((TOKENS, QUARTER), f32),
            vmem((GROUPS, 8, TILE), f32),
            vmem((LAYERS * BLOCKS, 8, TILE), f32),
            vmem((GROUPS, 8, TILE), f32),
            vmem((BLOCKS, 8, TILE), f32),
            vmem((8, TILE), f32),
            vmem((1, QUARTER), f32),
            vmem((TOKENS, TILE), f32),
            vmem((GROUPS, 8, TILE), f32),
            vmem((BLOCKS, 8, TILE), f32),
            vmem((TOKENS, QUARTER), bf16),
            vmem((2, TOKENS, BLOCK), bf16),
            vmem((2, TOKENS, BLOCK), bf16),
            vmem((2, SIDE, SIDE, ROWS, BLOCK), bf16),
            vmem((2, SIDE, SIDE, ROWS, HALF), f32),
            vmem((2, SIDE, ROWS, HALF), f32),
            vmem((2, SIDE, ROWS, HALF), f32),
            vmem((2, 2, SIDE, SIDE, ROWS, HALF), bf16),
            vmem((2, 2, SIDE, ROWS, HALF), bf16),
            vmem((2, 2, SIDE, ROWS, HALF), bf16),
            vmem((ROWS, BLOCK), bf16),
            vmem((ROWS, BLOCK), bf16),
            vmem((ROWS, BLOCK), f32),
            vmem((SIDE, SIDE, ROWS, BLOCK), bf16),
            dma((2, 2, CHUNKS)), dma((2, 2, CHUNKS)),
            dma((2, CHUNKS)), dma((2, CHUNKS)),
            dma, dma,
            dma((16,)), dma((16,)),
            dma((BLOCKS,)), dma((BLOCKS,)),
            dma, dma,
            dma((2,)), dma((2,)),
            dma((GROUPS,)), dma((GROUPS,)),
            dma((16,)), dma((16,)),
            dma((GROUPS,)), dma((GROUPS,)),
            dma((BLOCKS,)), dma((BLOCKS,)),
            dma((GROUPS,)), dma((GROUPS,)),
            dma((BLOCKS,)), dma((BLOCKS,)),
            dma((2,)), dma((2,)),
            dma((3, 4, SIDE)), dma((3, 4, SIDE)),
            dma((3, 4, SIDE)), dma((3, 4, SIDE)),
            dma, dma,
            dma((3,)),
        ],
        compiler_params=pltpu.CompilerParams(
            collective_id=0, has_side_effects=True, vmem_limit_bytes=56 * 1024 * 1024
        ),
        name="lens",
    )(hidden, translator, bias, gain, head, final)


def shards(hidden, translator, bias, gain, head, final_logits):
    return tuple(run(hidden[0], translator[0], bias, gain[None], head, final_logits[0]))


def solution(mesh):
    in_specs = (
        P("layer", None, "vocab"),
        P("layer", "vocab", "dp"),
        P("layer", "dp"),
        P("dp"),
        P("dp", "vocab"),
        P("dp", "layer", "vocab"),
    )
    out_specs = (P("layer", "vocab", "dp"), P("layer", "dp"), P("layer"))
    return jax.shard_map(shards, mesh=mesh, in_specs=in_specs, out_specs=out_specs, check_vma=False)
```

```python
import jax
import jax.numpy as jnp
from jax import lax
from jax.experimental import pallas as pl
from jax.experimental.pallas import tpu as pltpu
from jax.sharding import PartitionSpec as P

D = 4096
TOKENS = 512
LAYERS = 4
GROUPS = 16
SIDE = 4
BLOCKS = 4
BLOCK = D // BLOCKS
QUARTER = 1024
ROWS = TOKENS // GROUPS
TILE = 128
HALF = BLOCK // 2
CHUNK = 16
CHUNKS = HALF // CHUNK
LAG = 3
FINALS = 2 * ROWS // CHUNK
PACE = (0.22, 0.3, 0.4, 0.48, 0.55, 0.75, 0.85, 0.9)

epsilon = 1e-05
f32 = jnp.float32
bf16 = jnp.bfloat16
MESH = pl.DeviceIdType.MESH


def aligned(start, size):
    return pl.ds(pl.multiple_of(start, size), size)


def each(lo, hi, f):
    def step(k, carry):
        f(k)
        return carry

    lax.fori_loop(lo, hi, step, 0)


def kernel(
    hidden, translator, bias, gain, head, final, gathered_grad, div_out,
    heads, passing, normed, partial, target, final_own, pad, scaled, squares, logits,
    top_stats, want_lse, stats, stats2, lse, cross, inner, crosses, crosses2, grads, crossing, crossed, summing,
    parts, part_mid, part_end, sum_parts, sum_mid, sum_end, half_sum, other_sum, finals,
    next_final, passing_final,
    chain_send, chain_recv, pass_send, pass_recv, fchain_send, fchain_recv, fpass_send, fpass_recv,
    next_send, next_recv, head_send, head_recv, fin_send, fin_recv,
    sq_send, sq_recv, opp_send, opp_recv, sib_send, sib_recv,
    top_send, top_recv, wl_send, wl_recv, st_send, st_recv, st2_send, st2_recv, cr_send, cr_recv,
    cr2_send, cr2_recv, gx_send, gx_recv, rs_send, rs_recv, ag_send, ag_recv,
    go_send, go_recv, local_sem,
):
    l = lax.axis_index("layer")
    v = lax.axis_index("vocab")
    d = lax.axis_index("dp")
    y = lax.div(v, SIDE)
    x = lax.rem(v, SIDE)
    h = lax.div(d, 2)
    c = lax.rem(d, 2)
    sib = h * 2 + 1 - c
    opp = lax.rem(d + 2, BLOCKS)
    opp_sib = (1 - h) * 2 + 1 - c
    up_l = lax.rem(l + 1, LAYERS)
    up_d = lax.rem(d + 2 * lax.div(l + 1, LAYERS), BLOCKS)
    down_l = lax.rem(l + LAYERS - 1, LAYERS)
    down_d = lax.rem(d + 2 * (1 - lax.div(l + LAYERS - 1, LAYERS)), BLOCKS)
    column = l * BLOCKS + d
    NCOL = LAYERS * BLOCKS

    def in_plane(k):
        return lax.rem(v + k, GROUPS)

    def in_column(k):
        return lax.rem(column + k, NCOL)

    def along_x(k):
        return lax.rem(x + k, SIDE)

    def along_y(k):
        return lax.rem(y + k, SIDE)

    def remote(src, dst, send, recv, ll, vv, dd):
        return pltpu.make_async_remote_copy(
            src_ref=src, dst_ref=dst, send_sem=send, recv_sem=recv,
            device_id=(ll, vv, dd), device_id_type=MESH,
        )

    def arrive(dst, sem):
        remote(dst, dst, sem, sem, l, v, d).wait_recv()

    def sent(src, sem):
        remote(src, src, sem, sem, l, v, d).wait_send()

    leaving = []

    def drain():
        for f in leaving:
            f()

    def start_each(count, make, send, shape):
        each(1, count, lambda k: make(k).start())
        leaving.append(lambda: each(1, count, lambda k: sent(shape, send.at[k])))

    def cols(q):
        return aligned(q * QUARTER, QUARTER)

    def own_rows(p):
        return aligned(p * ROWS, ROWS)

    own_head = pltpu.make_async_copy(head.at[:, cols(d)], heads.at[d], local_sem.at[0])
    own_head.start()
    own_rows_final = aligned(d * TILE + l * ROWS, ROWS)
    own_final = pltpu.make_async_copy(final.at[:, cols(d)], target.at[own_rows_final, :], local_sem.at[1])
    own_final.start()
    whole_final = pltpu.make_async_copy(final, final_own, local_sem.at[2])
    whole_final.start()

    barrier = pltpu.get_barrier_semaphore()

    def greet_plane(k):
        pl.semaphore_signal(barrier, inc=1, device_id=(l, in_plane(k), d), device_id_type=MESH)

    def greet_column(k):
        m = in_column(k)
        pl.semaphore_signal(
            barrier, inc=1, device_id=(lax.div(m, BLOCKS), v, lax.rem(m, BLOCKS)), device_id_type=MESH
        )

    each(1, GROUPS, greet_plane)
    each(1, NCOL, greet_column)

    def product(n):
        at = aligned(n * 256, 256)
        value = jnp.dot(hidden[...], translator[:, at], preferred_element_type=f32)
        partial[:, :, :, at] = value.reshape(SIDE, SIDE, ROWS, 256)

    each(0, BLOCK // 256, product)
    pl.semaphore_wait(barrier, GROUPS - 1 + NCOL - 1)

    def rows_of(s, k):
        return aligned(s * HALF + k * CHUNK, CHUNK)

    def chain_copy(s, j, k, from_own):
        rows = rows_of(s, k)
        ll, dd = (up_l, up_d) if s == 0 else (down_l, down_d)
        if from_own:
            src = head.at[rows, cols((1 - h) * 2 + (c if j == 0 else 1 - c))]
            dst = heads.at[d, rows, :] if j == 0 else passing.at[rows, :]
        else:
            src = heads.at[opp, rows, :] if j == 0 else passing.at[rows, :]
            dst = src
        return remote(src, dst, chain_send.at[s, j, k], chain_recv.at[s, j, k], ll, v, dd)

    ends = (l == LAYERS - 1, l == 0)
    relays = (l != LAYERS - 1, l != 0)

    def source(s):
        def one(k):
            chain_copy(s, 0, k, True).start()
            chain_copy(s, 1, k, True).start()

        @pl.when(ends[s])
        def _():
            each(0, CHUNKS, one)

    def final_at(s, k):
        return (LAYERS - 1 - lax.div(k, 2) if s == 0 else lax.div(k, 2)) * ROWS + lax.rem(k, 2) * CHUNK

    def final_rows(s, k, block):
        return aligned(block * TILE + final_at(s, k), CHUNK)

    def final_chain(s, j, k, src, block):
        ll, dd = (up_l, up_d) if s == 0 else (down_l, down_d)
        dst = target.at[final_rows(s, k, block), :] if j == 0 else passing_final.at[aligned(final_at(s, k), CHUNK), :]
        return remote(
            dst if src is None else src, dst, fchain_send.at[s, j, k], fchain_recv.at[s, j, k], ll, v, dd
        )

    def final_source(s, lo, hi):
        def one(k):
            rows = aligned(lax.rem(k, 2) * CHUNK, CHUNK)
            for j in (0, 1):
                q = c if j == 0 else 1 - c
                if lo == 0:
                    src = final.at[rows, cols((1 - h) * 2 + q)]
                else:
                    src = next_final.at[rows, cols(q)]
                final_chain(s, j, k, src, d).start()

        each(lo, hi, one)

    next_copy = remote(
        final.at[:, aligned((1 - h) * 2 * QUARTER, 2 * QUARTER)], next_final, next_send, next_recv, 3 * (l - 1), v, d
    )
    inner_layer = jnp.logical_and(l > 0, l < LAYERS - 1)

    def next_sent():
        @pl.when(inner_layer)
        def _():
            next_copy.wait_send()

    leaving.append(next_sent)

    def chain_sent(k):
        for s in (0, 1):
            chain_copy(s, 0, k, False).wait_send()
            chain_copy(s, 1, k, False).wait_send()
            sent(passing.at[rows_of(s, k), :], pass_send.at[s, k])

    def final_chain_sent(k):
        for s in (0, 1):
            final_chain(s, 0, k, None, opp).wait_send()
            final_chain(s, 1, k, None, opp).wait_send()
            sent(passing_final.at[0:CHUNK, :], fpass_send.at[s, k])

    leaving.append(lambda: each(0, CHUNKS, chain_sent))
    leaving.append(lambda: each(0, FINALS, final_chain_sent))
    lag = (LAG * l, LAG * (LAYERS - 1 - l))
    TURNS = CHUNKS + LAG * (LAYERS - 1)
    done = [0]

    def chain(until):
        def one(turn):
            for s in (0, 1):
                k = turn - lag[s]

                @pl.when(jnp.logical_and(k >= 0, k < CHUNKS))
                def _(s=s, k=k):
                    rows = rows_of(s, k)
                    arrive(heads.at[opp, rows, :], chain_recv.at[s, 0, k])
                    arrive(passing.at[rows, :], chain_recv.at[s, 1, k])

                    @pl.when(relays[s])
                    def _():
                        chain_copy(s, 0, k, False).start()
                        chain_copy(s, 1, k, False).start()

                    remote(
                        passing.at[rows, :], heads.at[opp, rows, :],
                        pass_send.at[s, k], pass_recv.at[s, k], l, v, sib,
                    ).start()

                @pl.when(jnp.logical_and(k >= CHUNKS, k < CHUNKS + FINALS))
                def _(s=s, k=k - CHUNKS):
                    rows = final_rows(s, k, opp)
                    passed_rows = passing_final.at[aligned(final_at(s, k), CHUNK), :]
                    arrive(target.at[rows, :], fchain_recv.at[s, 0, k])
                    arrive(passed_rows, fchain_recv.at[s, 1, k])

                    @pl.when(relays[s])
                    def _():
                        final_chain(s, 0, k, None, opp).start()
                        final_chain(s, 1, k, None, opp).start()

                    remote(
                        passed_rows, target.at[rows, :], fpass_send.at[s, k], fpass_recv.at[s, k], l, v, sib
                    ).start()

        hi = min(int(TURNS * until), TURNS + FINALS)
        each(done[0], hi, one)
        done[0] = hi

    HALF_COLUMN = LAYERS * 2
    in_half = l * 2 + c

    def final_copy(k):
        m = lax.rem(in_half + k, HALF_COLUMN)
        dd = h * 2 + lax.rem(m, 2)
        return remote(
            final.at[:, cols(dd)], target.at[own_rows_final, :],
            fin_send.at[k], fin_recv.at[in_half], lax.div(m, 2), v, dd,
        )

    left = pl.ds(0, HALF)
    right = pl.ds(HALF, HALF)

    def at_x(k):
        return y * SIDE + along_x(k)

    def at_y(k):
        return along_y(k) * SIDE + x

    def sums_start(src, part, send, recv):
        start_each(
            SIDE,
            lambda k: remote(
                src.at[:, along_x(k), :, left], part.at[0, x], send.at[0, k], recv.at[0, x], l, at_x(k), d
            ),
            send.at[0], part.at[0, 0],
        )
        start_each(
            SIDE,
            lambda k: remote(
                src.at[along_y(k), :, :, right], part.at[1, y], send.at[1, k], recv.at[1, y], l, at_y(k), d
            ),
            send.at[1], part.at[0, 0],
        )

    def sums_middle(src, part, mid, end, send, recv):
        each(1, SIDE, lambda k: arrive(part.at[0, along_x(k)], recv.at[0, along_x(k)]))
        for n in range(SIDE):
            value = src[n, x, :, left].astype(f32)
            for k in range(1, SIDE):
                value += part[0, along_x(k), n].astype(f32)
            mid[0, n] = value.astype(mid.dtype)
        start_each(
            SIDE,
            lambda k: remote(
                mid.at[0, along_y(k)], end.at[0, y], send.at[2, k], recv.at[2, y], l, at_y(k), d
            ),
            send.at[2], end.at[0, 0],
        )
        each(1, SIDE, lambda k: arrive(part.at[1, along_y(k)], recv.at[1, along_y(k)]))
        for n in range(SIDE):
            value = src[y, n, :, right].astype(f32)
            for k in range(1, SIDE):
                value += part[1, along_y(k), n].astype(f32)
            mid[1, n] = value.astype(mid.dtype)
        start_each(
            SIDE,
            lambda k: remote(
                mid.at[1, along_x(k)], end.at[1, x], send.at[3, k], recv.at[3, x], l, at_x(k), d
            ),
            send.at[3], end.at[0, 0],
        )

    def sums_end(mid, end, recv):
        each(1, SIDE, lambda k: arrive(end.at[0, along_y(k)], recv.at[2, along_y(k)]))
        each(1, SIDE, lambda k: arrive(end.at[1, along_x(k)], recv.at[3, along_x(k)]))
        value_left = mid[0, y].astype(f32)
        value_right = mid[1, x].astype(f32)
        for k in range(1, SIDE):
            value_left += end[0, along_y(k)].astype(f32)
            value_right += end[1, along_x(k)].astype(f32)
        return value_left, value_right

    def gather_start(buf, send, recv):
        my_left = buf.at[y, x, :, left]
        my_right = buf.at[y, x, :, right]
        start_each(
            SIDE, lambda k: remote(my_left, my_left, send.at[0, k], recv.at[0, x], l, at_x(k), d), send.at[0], my_left
        )
        start_each(
            SIDE, lambda k: remote(my_right, my_right, send.at[1, k], recv.at[1, y], l, at_y(k), d),
            send.at[1], my_right,
        )

    def gather_middle(buf, send, recv):
        row_left = buf.at[y, :, :, left]
        column_right = buf.at[:, x, :, right]
        each(1, SIDE, lambda k: arrive(buf.at[y, along_x(k), :, left], recv.at[0, along_x(k)]))
        start_each(
            SIDE, lambda k: remote(row_left, row_left, send.at[2, k], recv.at[2, y], l, at_y(k), d),
            send.at[2], row_left,
        )
        each(1, SIDE, lambda k: arrive(buf.at[along_y(k), x, :, right], recv.at[1, along_y(k)]))
        start_each(
            SIDE, lambda k: remote(column_right, column_right, send.at[3, k], recv.at[3, x], l, at_x(k), d),
            send.at[3], column_right,
        )

    def gather_end(buf, recv):
        each(1, SIDE, lambda k: arrive(buf.at[along_y(k), :, :, left], recv.at[2, along_y(k)]))
        each(1, SIDE, lambda k: arrive(buf.at[:, along_x(k), :, right], recv.at[3, along_x(k)]))

    @pl.when(inner_layer)
    def _():
        next_copy.start()

    source(0)
    source(1)
    for s in (0, 1):
        @pl.when(ends[s])
        def _(s=s):
            final_source(s, 0, 2)

    sums_start(partial, parts, rs_send.at[0], rs_recv.at[0])
    head_copy = remote(head.at[:, cols(sib)], heads.at[d], head_send, head_recv, l, v, sib)
    head_copy.start()
    leaving.append(head_copy.wait_send)

    lane = lax.broadcasted_iota(jnp.int32, (8, TILE), 1)
    own_lanes = jnp.logical_and(lane >= l * ROWS, lane < l * ROWS + ROWS)
    pad[...] = jnp.zeros((TILE, TILE), f32)
    whole_final.wait()
    wanted = final_own[...].astype(f32)
    want_top = jnp.max(wanted, axis=1, keepdims=True)
    want_sum = jnp.sum(jnp.exp(wanted - want_top), axis=1, keepdims=True)
    column_lane = lax.broadcasted_iota(jnp.int32, (ROWS, TILE), 1)
    pad[own_rows(l), :] = jnp.where(column_lane == 0, want_top, want_sum)
    top_stats[v] = pad[...].T[0:8, :]

    def plane_copy(buf, send, recv):
        return lambda k: remote(buf.at[v], buf.at[v], send.at[k], recv.at[v], l, in_plane(k), d)

    def plane_arrive(buf, recv):
        each(1, GROUPS, lambda k: arrive(buf.at[in_plane(k)], recv.at[in_plane(k)]))

    start_each(GROUPS, plane_copy(top_stats, top_send, top_recv), top_send, top_stats.at[0])
    chain(PACE[0])
    for s in (0, 1):
        @pl.when(ends[s])
        def _(s=s):
            arrive(next_final, next_recv)
            final_source(s, 2, FINALS)

    sums_middle(partial, parts, part_mid, part_end, rs_send.at[0], rs_recv.at[0])
    plane_arrive(top_stats, top_recv)
    all_top = jnp.max(top_stats[:, 0:1, :], axis=0)
    all_sum = jnp.sum(top_stats[:, 1:2, :] * jnp.exp(top_stats[:, 0:1, :] - all_top[None]), axis=0)
    row_lse = all_top + jnp.log(jnp.where(own_lanes[0:1, :], all_sum, 1.0))
    want_lse[column] = jnp.broadcast_to(jnp.where(own_lanes[0:1, :], row_lse, 0.0), (8, TILE))

    def want_copy(k):
        m = in_column(k)
        return remote(
            want_lse.at[column], want_lse.at[column], wl_send.at[k], wl_recv.at[column],
            lax.div(m, BLOCKS), v, lax.rem(m, BLOCKS),
        )

    start_each(NCOL, want_copy, wl_send, want_lse.at[0])

    chain(PACE[1])
    value_left, value_right = sums_end(part_mid, part_end, rs_recv.at[0])
    scaled[:, left] = value_left + bias[:, left]
    scaled[:, right] = value_right + bias[:, right]
    projected = scaled[...]
    squares[d] = jnp.broadcast_to(jnp.sum(projected * projected, axis=1, keepdims=True), (ROWS, 128))

    def to_blocks(buf, send, recv):
        def copy(k):
            return remote(buf.at[d], buf.at[d], send.at[k], recv.at[d], l, v, lax.rem(d + k, BLOCKS))

        start_each(BLOCKS, copy, send, buf.at[0])

    def from_blocks(buf, recv):
        def come(k):
            dd = lax.rem(d + k, BLOCKS)
            arrive(buf.at[dd], recv.at[dd])

        each(1, BLOCKS, come)

    to_blocks(squares, sq_send, sq_recv)
    chain(PACE[2])
    from_blocks(squares, sq_recv)
    inverse = lax.rsqrt(jnp.sum(squares[...], axis=0)[:, :1] / D + epsilon)
    scaled[...] = projected * inverse
    normed[d, y, x] = (scaled[...] * gain[...]).astype(bf16)

    mine = normed.at[d, y, x]
    opp_copy = remote(mine, mine, opp_send, opp_recv, l, v, opp)
    opp_copy.start()
    leaving.append(opp_copy.wait_send)

    def to_sibling(block, i):
        copy = remote(normed.at[block], normed.at[block], sib_send.at[i], sib_recv.at[i], l, v, sib)
        copy.start()
        leaving.append(copy.wait_send)

    here, there = normed.at[d], normed.at[opp]
    gather_start(here, ag_send.at[0], ag_recv.at[0])
    chain(PACE[3])
    gather_middle(here, ag_send.at[0], ag_recv.at[0])
    arrive(normed.at[opp, y, x], opp_recv)
    gather_start(there, ag_send.at[1], ag_recv.at[1])
    chain(PACE[4])
    gather_middle(there, ag_send.at[1], ag_recv.at[1])
    chain(PACE[5])
    gather_end(here, ag_recv.at[0])
    to_sibling(d, 0)
    chain(PACE[6])
    gather_end(there, ag_recv.at[1])
    to_sibling(opp, 1)
    own_head.wait()
    own_final.wait()

    def multiply(block, first):
        def go(n):
            at = aligned(n * 256, 256)
            value = jnp.dot(
                normed[block].reshape(TOKENS, BLOCK), heads[block, :, at], preferred_element_type=f32
            )
            if first:
                logits[:, at] = value
            else:
                logits[:, at] += value

        each(0, QUARTER // 256, go)

    multiply(d, True)
    chain(PACE[7])
    arrive(normed.at[sib], sib_recv.at[0])
    arrive(heads.at[sib], head_recv)
    multiply(sib, False)
    chain(1)
    start_each(HALF_COLUMN, final_copy, fin_send, target.at[own_rows_final, :])
    multiply(opp, False)
    arrive(normed.at[opp_sib], sib_recv.at[1])

    def passed(k):
        for s in (0, 1):
            arrive(heads.at[opp_sib, rows_of(s, k), :], pass_recv.at[s, k])

    each(0, CHUNKS, passed)
    multiply(opp_sib, False)

    for t in range(TOKENS // TILE):
        have = logits[t * TILE:(t + 1) * TILE, :]
        have_top = jnp.max(have, axis=1, keepdims=True)
        have_sum = jnp.sum(jnp.exp(have - have_top), axis=1, keepdims=True)
        tile_lane = lax.broadcasted_iota(jnp.int32, (TILE, TILE), 1)
        turned = jnp.where(tile_lane == 0, have_top, have_sum).T
        stats[v, t:t + 1, :] = turned[0:1, :]
        stats[v, 4 + t:5 + t, :] = turned[1:2, :]

    start_each(GROUPS, plane_copy(stats, st_send, st_recv), st_send, stats.at[0])

    def merge(buf):
        top = jnp.max(buf[:, 0:4, :], axis=0)
        return top, jnp.sum(buf[:, 4:8, :] * jnp.exp(buf[:, 0:4, :] - top[None]), axis=0)

    chain(2)
    plane_arrive(stats, st_recv)
    top, total = merge(stats)
    stats2[d] = jnp.concatenate([top, total], axis=0)
    to_blocks(stats2, st2_send, st2_recv)

    def want_arrived(k):
        m = in_column(k)
        arrive(want_lse.at[m], wl_recv.at[m])

    def final_arrived(k):
        m = lax.rem(in_half + k, HALF_COLUMN)
        rows = aligned((h * 2 + lax.rem(m, 2)) * TILE + lax.div(m, 2) * ROWS, ROWS)
        arrive(target.at[rows, :], fin_recv.at[m])

    def final_passed(k):
        for s in (0, 1):
            arrive(target.at[final_rows(s, k, opp_sib), :], fpass_recv.at[s, k])

    each(1, NCOL, want_arrived)
    each(1, HALF_COLUMN, final_arrived)
    each(0, FINALS, final_passed)
    for t in range(BLOCKS):
        lse[4 + t:5 + t, :] = (
            want_lse[t, 0:1, :] + want_lse[4 + t, 0:1, :] + want_lse[8 + t, 0:1, :] + want_lse[12 + t, 0:1, :]
        )
    from_blocks(stats2, st2_recv)
    top, total = merge(stats2)
    lse[0:4, :] = top + jnp.log(total)

    cross[...] = jnp.zeros((1, QUARTER), f32)
    for t in range(BLOCKS):
        at = pl.ds(t * TILE, TILE)
        have_lse = jnp.broadcast_to(lse[t:t + 1, :], (TILE, TILE)).T[:, 0:1]
        target_lse = jnp.broadcast_to(lse[4 + t:5 + t, :], (TILE, TILE)).T[:, 0:1]
        wanted = target[at, :].astype(f32)
        have = logits[at, :]
        want = jnp.exp(wanted - target_lse)
        grad = (jnp.exp(have - have_lse) - want).astype(bf16)
        grads[at, :] = grad
        inner[at, :] = jnp.broadcast_to(
            jnp.sum(grad.astype(f32) * have, axis=1, keepdims=True), (TILE, TILE)
        )
        cross[...] += jnp.sum(want * (wanted - have), axis=0, keepdims=True)

    def back(block, write):
        def go(n):
            at = aligned(n * 256, 256)
            write(
                at,
                lax.dot_general(
                    grads[...], heads[block, at, :], (((1,), (1,)), ((), ())),
                    preferred_element_type=f32,
                ),
            )

        each(0, BLOCK // 256, go)

    def crossing_copy(i):
        return remote(crossing.at[i], crossed.at[i], gx_send.at[i], gx_recv.at[i], l, v, sib)

    for i, block in ((0, opp_sib), (1, sib)):
        def to_crossing(at, value, i=i):
            crossing[i, :, at] = value.astype(bf16)

        back(block, to_crossing)
        crossing_copy(i).start()
        leaving.append(crossing_copy(i).wait_send)

    for i, block in ((0, opp), (1, d)):
        def to_logits(at, value):
            logits[:, at] = value

        back(block, to_logits)
        arrive(crossed.at[i], gx_recv.at[i])

        def add_rows(t, i=i):
            at = aligned(t * TILE, TILE)
            value = (logits[at, :] + crossed[i, at, :].astype(f32)).astype(bf16)
            summing[i, t] = value.reshape(SIDE, ROWS, BLOCK)

        each(0, TOKENS // TILE, add_rows)
        sums_start(summing.at[i], sum_parts.at[i], rs_send.at[1 + i], rs_recv.at[1 + i])

    for t in range(BLOCKS):
        crosses[v, t:t + 1, :] = inner[t * TILE:(t + 1) * TILE, :].T[0:1, :]
    crosses[v, 4:8, :] = jnp.broadcast_to(jnp.sum(cross[...], axis=1, keepdims=True), (4, 128))
    start_each(GROUPS, plane_copy(crosses, cr_send, cr_recv), cr_send, crosses.at[0])

    for i in (0, 1):
        sums_middle(
            summing.at[i], sum_parts.at[i], sum_mid.at[i], sum_end.at[i], rs_send.at[1 + i], rs_recv.at[1 + i]
        )
        if i == 0:
            plane_arrive(crosses, cr_recv)
            crosses2[d] = jnp.sum(crosses[...], axis=0)
            to_blocks(crosses2, cr2_send, cr2_recv)

    value_left, value_right = sums_end(sum_mid.at[0], sum_end.at[0], rs_recv.at[1])
    half_sum[:, left] = value_left.astype(bf16)
    half_sum[:, right] = value_right.astype(bf16)
    go_copy = remote(half_sum, other_sum, go_send, go_recv, l, v, opp)
    go_copy.start()
    leaving.append(go_copy.wait_send)
    value_left, value_right = sums_end(sum_mid.at[1], sum_end.at[1], rs_recv.at[2])
    finals[:, left] = value_left
    finals[:, right] = value_right
    from_blocks(crosses2, cr2_recv)
    crossed_all = jnp.sum(crosses2[...], axis=0)
    div_out[0] = (jnp.sum(crossed_all[4:5, 0:1]) + jnp.sum(lse[0:4, :] - lse[4:8, :])) / TOKENS
    lse[...] = crossed_all
    pad[...] = jnp.broadcast_to(lse[pl.ds(y, 1), :], (TILE, TILE)).T
    inner_mean = pad[own_rows(x), :][:, 0:1] / D
    arrive(other_sum, go_recv)

    grad_scaled = (finals[...] + other_sum[...].astype(f32)) * gain[...]
    inverse = lax.rsqrt(jnp.sum(squares[...], axis=0)[:, :1] / D + epsilon)
    gathered_grad[y, x] = (inverse * (grad_scaled - scaled[...] * inner_mean)).astype(bf16)
    gather_start(gathered_grad, ag_send.at[2], ag_recv.at[2])
    gather_middle(gathered_grad, ag_send.at[2], ag_recv.at[2])
    gather_end(gathered_grad, ag_recv.at[2])

    drain()


def products(hidden, grad, divergence, weights_out, offsets_out, div_out):
    value = grad[...].reshape(TOKENS, grad.shape[-1])
    weights_out[0] = lax.dot_general(
        hidden[...], value, (((0,), (0,)), ((), ())), preferred_element_type=f32
    )
    offsets_out[...] = jnp.sum(value.astype(f32), axis=0, keepdims=True)
    div_out[0] = divergence[0]


def run(hidden, translator, bias, gain, head, final):
    dma = pltpu.SemaphoreType.DMA
    vmem = pltpu.VMEM
    in_vmem = pl.BlockSpec(memory_space=pltpu.VMEM)
    anywhere = pl.BlockSpec(memory_space=pl.ANY)
    width = hidden.shape[1]
    smem = pl.BlockSpec(memory_space=pltpu.SMEM)
    grad, divergence = pl.pallas_call(
        kernel,
        out_shape=[
            jax.ShapeDtypeStruct((SIDE, SIDE, ROWS, BLOCK), bf16),
            jax.ShapeDtypeStruct((1,), f32),
        ],
        in_specs=[in_vmem] * 4 + [anywhere] * 2,
        out_specs=[in_vmem, smem],
        scratch_shapes=[
            vmem((BLOCKS, BLOCK, QUARTER), bf16),
            vmem((BLOCK, QUARTER), bf16),
            vmem((BLOCKS, SIDE, SIDE, ROWS, BLOCK), bf16),
            vmem((SIDE, SIDE, ROWS, BLOCK), f32),
            vmem((TOKENS, QUARTER), bf16),
            vmem((ROWS, BLOCKS * QUARTER), bf16),
            vmem((TILE, TILE), f32),
            vmem((ROWS, BLOCK), f32),
            vmem((BLOCKS, ROWS, 128), f32),
            vmem((TOKENS, QUARTER), f32),
            vmem((GROUPS, 8, TILE), f32),
            vmem((LAYERS * BLOCKS, 8, TILE), f32),
            vmem((GROUPS, 8, TILE), f32),
            vmem((BLOCKS, 8, TILE), f32),
            vmem((8, TILE), f32),
            vmem((1, QUARTER), f32),
            vmem((TOKENS, TILE), f32),
            vmem((GROUPS, 8, TILE), f32),
            vmem((BLOCKS, 8, TILE), f32),
            vmem((TOKENS, QUARTER), bf16),
            vmem((2, TOKENS, BLOCK), bf16),
            vmem((2, TOKENS, BLOCK), bf16),
            vmem((2, SIDE, SIDE, ROWS, BLOCK), bf16),
            vmem((2, SIDE, SIDE, ROWS, HALF), f32),
            vmem((2, SIDE, ROWS, HALF), f32),
            vmem((2, SIDE, ROWS, HALF), f32),
            vmem((2, 2, SIDE, SIDE, ROWS, HALF), bf16),
            vmem((2, 2, SIDE, ROWS, HALF), bf16),
            vmem((2, 2, SIDE, ROWS, HALF), bf16),
            vmem((ROWS, BLOCK), bf16),
            vmem((ROWS, BLOCK), bf16),
            vmem((ROWS, BLOCK), f32),
            vmem((ROWS, 2 * QUARTER), bf16),
            vmem((TILE, QUARTER), bf16),
            dma((2, 2, CHUNKS)), dma((2, 2, CHUNKS)),
            dma((2, CHUNKS)), dma((2, CHUNKS)),
            dma((2, 2, FINALS)), dma((2, 2, FINALS)),
            dma((2, FINALS)), dma((2, FINALS)),
            dma, dma,
            dma, dma,
            dma((16,)), dma((16,)),
            dma((BLOCKS,)), dma((BLOCKS,)),
            dma, dma,
            dma((2,)), dma((2,)),
            dma((GROUPS,)), dma((GROUPS,)),
            dma((16,)), dma((16,)),
            dma((GROUPS,)), dma((GROUPS,)),
            dma((BLOCKS,)), dma((BLOCKS,)),
            dma((GROUPS,)), dma((GROUPS,)),
            dma((BLOCKS,)), dma((BLOCKS,)),
            dma((2,)), dma((2,)),
            dma((3, 4, SIDE)), dma((3, 4, SIDE)),
            dma((3, 4, SIDE)), dma((3, 4, SIDE)),
            dma, dma,
            dma((3,)),
        ],
        compiler_params=pltpu.CompilerParams(
            collective_id=0, has_side_effects=True, vmem_limit_bytes=56 * 1024 * 1024
        ),
        name="lens",
    )(hidden, translator, bias, gain, head, final)
    tile = 256
    return pl.pallas_call(
        products,
        out_shape=[
            jax.ShapeDtypeStruct((1, width, BLOCK), f32),
            jax.ShapeDtypeStruct((1, BLOCK), f32),
            jax.ShapeDtypeStruct((1,), f32),
        ],
        grid=(BLOCK // tile,),
        in_specs=[
            pl.BlockSpec((TOKENS, width), lambda n: (0, 0)),
            pl.BlockSpec((SIDE, SIDE, ROWS, tile), lambda n: (0, 0, 0, n)),
            smem,
        ],
        out_specs=[
            pl.BlockSpec((1, width, tile), lambda n: (0, 0, n)),
            pl.BlockSpec((1, tile), lambda n: (0, n)),
            smem,
        ],
        name="products",
    )(hidden, grad, divergence)


def shards(hidden, translator, bias, gain, head, final_logits):
    return tuple(run(hidden[0], translator[0], bias, gain[None], head, final_logits[0]))


def solution(mesh):
    in_specs = (
        P("layer", None, "vocab"),
        P("layer", "vocab", "dp"),
        P("layer", "dp"),
        P("dp"),
        P("dp", "vocab"),
        P("dp", "layer", "vocab"),
    )
    out_specs = (P("layer", "vocab", "dp"), P("layer", "dp"), P("layer"))
    return jax.shard_map(shards, mesh=mesh, in_specs=in_specs, out_specs=out_specs, check_vma=False)
```

```python
import jax
import jax.numpy as jnp
from jax import lax
from jax.experimental import pallas as pl
from jax.experimental.pallas import tpu as pltpu
from jax.sharding import PartitionSpec as P

D = 4096
TOKENS = 512
LAYERS = 4
GROUPS = 16
SIDE = 4
BLOCKS = 4
BLOCK = D // BLOCKS
QUARTER = 1024
ROWS = TOKENS // GROUPS
TILE = 128
HALF = BLOCK // 2
CHUNK = 32
CHUNKS = HALF // CHUNK
LAG = 3
FINALS = 2 * ROWS // CHUNK
PACE = (0.3, 0.4, 0.5, 0.58, 0.64, 0.82, 0.9, 0.92, 0.94, 0.96, 0.98, 1.0)

epsilon = 1e-05
f32 = jnp.float32
bf16 = jnp.bfloat16
MESH = pl.DeviceIdType.MESH


def aligned(start, size):
    return pl.ds(pl.multiple_of(start, size), size)


def each(lo, hi, f):
    def step(k, carry):
        f(k)
        return carry

    lax.fori_loop(lo, hi, step, 0)


def kernel(
    hidden_hbm, translator_hbm, bias_hbm, gain_hbm, head, final, gathered_grad, turned, div_out,
    hidden, translator, bias, gain,
    heads, normed, partial, target, final_own, pad, scaled, squares, logits,
    top_stats, want_lse, stats, stats2, lse, cross, inner, crosses, crosses2, grads, crossing, crossed, summing,
    parts, part_mid, part_end, sum_parts, sum_mid, sum_end, half_sum, other_sum, finals,
    next_final, passing_final,
    chain_send, chain_recv, pass_send, pass_recv, fchain_send, fchain_recv, fpass_send, fpass_recv,
    next_send, next_recv, head_send, head_recv, fin_send, fin_recv,
    sq_send, sq_recv, opp_send, opp_recv, sib_send, sib_recv,
    top_send, top_recv, wl_send, wl_recv, st_send, st_recv, st2_send, st2_recv, cr_send, cr_recv,
    cr2_send, cr2_recv, gx_send, gx_recv, rs_send, rs_recv, ag_send, ag_recv,
    go_send, go_recv, local_sem,
):
    l = lax.axis_index("layer")
    v = lax.axis_index("vocab")
    d = lax.axis_index("dp")
    y = lax.div(v, SIDE)
    x = lax.rem(v, SIDE)
    h = lax.div(d, 2)
    c = lax.rem(d, 2)
    sib = h * 2 + 1 - c
    opp = lax.rem(d + 2, BLOCKS)
    opp_sib = (1 - h) * 2 + 1 - c
    up_l = lax.rem(l + 1, LAYERS)
    up_d = lax.rem(d + 2 * lax.div(l + 1, LAYERS), BLOCKS)
    down_l = lax.rem(l + LAYERS - 1, LAYERS)
    down_d = lax.rem(d + 2 * (1 - lax.div(l + LAYERS - 1, LAYERS)), BLOCKS)
    column = l * BLOCKS + d
    NCOL = LAYERS * BLOCKS

    def in_plane(k):
        return lax.rem(v + k, GROUPS)

    def in_column(k):
        return lax.rem(column + k, NCOL)

    def along_x(k):
        return lax.rem(x + k, SIDE)

    def along_y(k):
        return lax.rem(y + k, SIDE)

    def remote(src, dst, send, recv, ll, vv, dd):
        return pltpu.make_async_remote_copy(
            src_ref=src, dst_ref=dst, send_sem=send, recv_sem=recv,
            device_id=(ll, vv, dd), device_id_type=MESH,
        )

    def arrive(dst, sem):
        remote(dst, dst, sem, sem, l, v, d).wait_recv()

    def sent(src, sem):
        remote(src, src, sem, sem, l, v, d).wait_send()

    leaving = []

    def drain():
        for f in leaving:
            f()

    def start_each(count, make, send, shape):
        each(1, count, lambda k: make(k).start())
        leaving.append(lambda: each(1, count, lambda k: sent(shape, send.at[k])))

    def cols(q):
        return aligned(q * QUARTER, QUARTER)

    def own_rows(p):
        return aligned(p * ROWS, ROWS)

    staged = [
        pltpu.make_async_copy(src, dst, local_sem.at[3 + n])
        for n, (src, dst) in enumerate(
            ((hidden_hbm, hidden), (translator_hbm, translator), (bias_hbm, bias), (gain_hbm, gain))
        )
    ]
    for copy in staged:
        copy.start()
    own_head = pltpu.make_async_copy(head.at[:, cols(d)], heads.at[d], local_sem.at[0])
    own_head.start()
    own_rows_final = aligned(d * TILE + l * ROWS, ROWS)
    own_final = pltpu.make_async_copy(final.at[:, cols(d)], target.at[own_rows_final, :], local_sem.at[1])
    own_final.start()
    whole_final = pltpu.make_async_copy(final, final_own, local_sem.at[2])
    whole_final.start()

    barrier = pltpu.get_barrier_semaphore()

    def greet_plane(k):
        pl.semaphore_signal(barrier, inc=1, device_id=(l, in_plane(k), d), device_id_type=MESH)

    def greet_column(k):
        m = in_column(k)
        pl.semaphore_signal(
            barrier, inc=1, device_id=(lax.div(m, BLOCKS), v, lax.rem(m, BLOCKS)), device_id_type=MESH
        )

    each(1, GROUPS, greet_plane)
    each(1, NCOL, greet_column)

    def product(n):
        at = aligned(n * 256, 256)
        value = jnp.dot(hidden[...], translator[:, at], preferred_element_type=f32)
        partial[:, :, :, at] = value.reshape(SIDE, SIDE, ROWS, 256)

    for copy in staged:
        copy.wait()
    each(0, BLOCK // 256, product)
    pl.semaphore_wait(barrier, GROUPS - 1 + NCOL - 1)

    def rows_of(s, k):
        return aligned(s * HALF + k * CHUNK, CHUNK)

    def slot(j):
        return opp + j * (BLOCKS - opp)

    def chain_copy(s, j, k, from_own):
        rows = rows_of(s, k)
        ll, dd = (up_l, up_d) if s == 0 else (down_l, down_d)
        if from_own:
            src = head.at[rows, cols((1 - h) * 2 + (c if j == 0 else 1 - c))]
            dst = heads.at[d if j == 0 else BLOCKS, rows, :]
        else:
            src = heads.at[slot(j), rows, :]
            dst = src
        return remote(src, dst, chain_send.at[s, j, k], chain_recv.at[s, j, k], ll, v, dd)

    ends = (l == LAYERS - 1, l == 0)
    relays = (l != LAYERS - 1, l != 0)

    def source(s):
        def one(k):
            chain_copy(s, 0, k, True).start()
            chain_copy(s, 1, k, True).start()

        @pl.when(ends[s])
        def _():
            each(0, CHUNKS, one)

    def final_at(s, k):
        return (LAYERS - 1 - k if s == 0 else k) * ROWS

    def final_rows(s, k, block):
        return aligned(block * TILE + final_at(s, k), CHUNK)

    def final_chain(s, j, k, src, block):
        ll, dd = (up_l, up_d) if s == 0 else (down_l, down_d)
        dst = target.at[final_rows(s, k, block), :] if j == 0 else passing_final.at[aligned(final_at(s, k), CHUNK), :]
        return remote(
            dst if src is None else src, dst, fchain_send.at[s, j, k], fchain_recv.at[s, j, k], ll, v, dd
        )

    def final_source(s, lo, hi):
        def one(k):
            rows = aligned(0, CHUNK)
            for j in (0, 1):
                q = c if j == 0 else 1 - c
                if lo == 0:
                    src = final.at[rows, cols((1 - h) * 2 + q)]
                else:
                    src = next_final.at[rows, cols(q)]
                final_chain(s, j, k, src, d).start()

        each(lo, hi, one)

    next_copy = remote(
        final.at[:, aligned((1 - h) * 2 * QUARTER, 2 * QUARTER)], next_final, next_send, next_recv, 3 * (l - 1), v, d
    )
    inner_layer = jnp.logical_and(l > 0, l < LAYERS - 1)

    def next_sent():
        @pl.when(inner_layer)
        def _():
            next_copy.wait_send()

    leaving.append(next_sent)

    def chain_sent(k):
        for s in (0, 1):
            chain_copy(s, 0, k, False).wait_send()
            chain_copy(s, 1, k, False).wait_send()
            sent(heads.at[BLOCKS, rows_of(s, k), :], pass_send.at[s, k])

    def final_chain_sent(k):
        for s in (0, 1):
            final_chain(s, 0, k, None, opp).wait_send()
            final_chain(s, 1, k, None, opp).wait_send()
            sent(passing_final.at[0:CHUNK, :], fpass_send.at[s, k])

    leaving.append(lambda: each(0, CHUNKS, chain_sent))
    leaving.append(lambda: each(0, FINALS, final_chain_sent))
    lag = (LAG * l, LAG * (LAYERS - 1 - l))
    TURNS = 2 * CHUNKS + LAG * (LAYERS - 1)
    done = [0]

    def chain(until):
        def one(turn):
            for s in (0, 1):
                u = turn - lag[s]

                @pl.when(jnp.logical_and(u >= 0, u < 2 * CHUNKS))
                def _(s=s, u=u):
                    k, j = lax.div(u, 2), lax.rem(u, 2)
                    rows = rows_of(s, k)
                    arrive(heads.at[slot(j), rows, :], chain_recv.at[s, j, k])

                    @pl.when(relays[s])
                    def _():
                        chain_copy(s, j, k, False).start()

                    @pl.when(j == 1)
                    def _():
                        remote(
                            heads.at[BLOCKS, rows, :], heads.at[opp, rows, :],
                            pass_send.at[s, k], pass_recv.at[s, k], l, v, sib,
                        ).start()

                @pl.when(jnp.logical_and(u >= 2 * CHUNKS, u < 2 * (CHUNKS + FINALS)))
                def _(s=s, u=u - 2 * CHUNKS):
                    k, j = lax.div(u, 2), lax.rem(u, 2)
                    rows = final_rows(s, k, opp)
                    passed_rows = passing_final.at[aligned(final_at(s, k), CHUNK), :]

                    @pl.when(j == 0)
                    def _():
                        arrive(target.at[rows, :], fchain_recv.at[s, 0, k])

                        @pl.when(relays[s])
                        def _():
                            final_chain(s, 0, k, None, opp).start()

                    @pl.when(j == 1)
                    def _():
                        arrive(passed_rows, fchain_recv.at[s, 1, k])

                        @pl.when(relays[s])
                        def _():
                            final_chain(s, 1, k, None, opp).start()

                        remote(
                            passed_rows, target.at[rows, :], fpass_send.at[s, k], fpass_recv.at[s, k], l, v, sib
                        ).start()

        hi = min(int(TURNS * until), TURNS + 2 * FINALS)
        each(done[0], hi, one)
        done[0] = hi

    HALF_COLUMN = LAYERS * 2
    in_half = l * 2 + c

    def final_copy(k):
        m = lax.rem(in_half + k, HALF_COLUMN)
        dd = h * 2 + lax.rem(m, 2)
        return remote(
            final.at[:, cols(dd)], target.at[own_rows_final, :],
            fin_send.at[k], fin_recv.at[in_half], lax.div(m, 2), v, dd,
        )

    left = pl.ds(0, HALF)
    right = pl.ds(HALF, HALF)

    def at_x(k):
        return y * SIDE + along_x(k)

    def at_y(k):
        return along_y(k) * SIDE + x

    def sums_start(src, part, send, recv, ways=(0, 1)):
        if 0 in ways:
            start_each(
                SIDE,
                lambda k: remote(
                    src.at[:, along_x(k), :, left], part.at[0, x], send.at[0, k], recv.at[0, x], l, at_x(k), d
                ),
                send.at[0], part.at[0, 0],
            )
        if 1 in ways:
            start_each(
                SIDE,
                lambda k: remote(
                    src.at[along_y(k), :, :, right], part.at[1, y], send.at[1, k], recv.at[1, y], l, at_y(k), d
                ),
                send.at[1], part.at[0, 0],
            )

    def sums_middle(src, part, mid, end, send, recv):
        each(1, SIDE, lambda k: arrive(part.at[0, along_x(k)], recv.at[0, along_x(k)]))
        for n in range(SIDE):
            value = src[n, x, :, left].astype(f32)
            for k in range(1, SIDE):
                value += part[0, along_x(k), n].astype(f32)
            mid[0, n] = value.astype(mid.dtype)
        start_each(
            SIDE,
            lambda k: remote(
                mid.at[0, along_y(k)], end.at[0, y], send.at[2, k], recv.at[2, y], l, at_y(k), d
            ),
            send.at[2], end.at[0, 0],
        )
        each(1, SIDE, lambda k: arrive(part.at[1, along_y(k)], recv.at[1, along_y(k)]))
        for n in range(SIDE):
            value = src[y, n, :, right].astype(f32)
            for k in range(1, SIDE):
                value += part[1, along_y(k), n].astype(f32)
            mid[1, n] = value.astype(mid.dtype)
        start_each(
            SIDE,
            lambda k: remote(
                mid.at[1, along_x(k)], end.at[1, x], send.at[3, k], recv.at[3, x], l, at_x(k), d
            ),
            send.at[3], end.at[0, 0],
        )

    def sums_end(mid, end, recv):
        each(1, SIDE, lambda k: arrive(end.at[0, along_y(k)], recv.at[2, along_y(k)]))
        each(1, SIDE, lambda k: arrive(end.at[1, along_x(k)], recv.at[3, along_x(k)]))
        value_left = mid[0, y].astype(f32)
        value_right = mid[1, x].astype(f32)
        for k in range(1, SIDE):
            value_left += end[0, along_y(k)].astype(f32)
            value_right += end[1, along_x(k)].astype(f32)
        return value_left, value_right

    def gather_start(buf, send, recv):
        my_left = buf.at[y, x, :, left]
        my_right = buf.at[y, x, :, right]
        start_each(
            SIDE, lambda k: remote(my_left, my_left, send.at[0, k], recv.at[0, x], l, at_x(k), d), send.at[0], my_left
        )
        start_each(
            SIDE, lambda k: remote(my_right, my_right, send.at[1, k], recv.at[1, y], l, at_y(k), d),
            send.at[1], my_right,
        )

    def gather_middle(buf, send, recv):
        row_left = buf.at[y, :, :, left]
        column_right = buf.at[:, x, :, right]
        each(1, SIDE, lambda k: arrive(buf.at[y, along_x(k), :, left], recv.at[0, along_x(k)]))
        start_each(
            SIDE, lambda k: remote(row_left, row_left, send.at[2, k], recv.at[2, y], l, at_y(k), d),
            send.at[2], row_left,
        )
        each(1, SIDE, lambda k: arrive(buf.at[along_y(k), x, :, right], recv.at[1, along_y(k)]))
        start_each(
            SIDE, lambda k: remote(column_right, column_right, send.at[3, k], recv.at[3, x], l, at_x(k), d),
            send.at[3], column_right,
        )

    def gather_end(buf, recv):
        each(1, SIDE, lambda k: arrive(buf.at[along_y(k), :, :, left], recv.at[2, along_y(k)]))
        each(1, SIDE, lambda k: arrive(buf.at[:, along_x(k), :, right], recv.at[3, along_x(k)]))

    @pl.when(inner_layer)
    def _():
        next_copy.start()

    source(0)
    source(1)
    for s in (0, 1):
        @pl.when(ends[s])
        def _(s=s):
            final_source(s, 0, 1)

    sums_start(partial, parts, rs_send.at[0], rs_recv.at[0])
    head_copy = remote(head.at[:, cols(sib)], heads.at[d], head_send, head_recv, l, v, sib)
    head_copy.start()
    leaving.append(head_copy.wait_send)

    lane = lax.broadcasted_iota(jnp.int32, (8, TILE), 1)
    own_lanes = jnp.logical_and(lane >= l * ROWS, lane < l * ROWS + ROWS)
    pad[...] = jnp.zeros((TILE, TILE), f32)
    whole_final.wait()
    chain(0.1)
    wanted = final_own[...].astype(f32)
    want_top = jnp.max(wanted, axis=1, keepdims=True)
    want_sum = jnp.sum(jnp.exp(wanted - want_top), axis=1, keepdims=True)
    column_lane = lax.broadcasted_iota(jnp.int32, (ROWS, TILE), 1)
    pad[own_rows(l), :] = jnp.where(column_lane == 0, want_top, want_sum)
    top_stats[v] = pad[...].T[0:8, :]

    def plane_copy(buf, send, recv):
        return lambda k: remote(buf.at[v], buf.at[v], send.at[k], recv.at[v], l, in_plane(k), d)

    def plane_arrive(buf, recv):
        each(1, GROUPS, lambda k: arrive(buf.at[in_plane(k)], recv.at[in_plane(k)]))

    start_each(GROUPS, plane_copy(top_stats, top_send, top_recv), top_send, top_stats.at[0])
    chain(PACE[0])
    for s in (0, 1):
        @pl.when(ends[s])
        def _(s=s):
            arrive(next_final, next_recv)
            final_source(s, 1, FINALS)

    sums_middle(partial, parts, part_mid, part_end, rs_send.at[0], rs_recv.at[0])
    plane_arrive(top_stats, top_recv)
    all_top = jnp.max(top_stats[:, 0:1, :], axis=0)
    all_sum = jnp.sum(top_stats[:, 1:2, :] * jnp.exp(top_stats[:, 0:1, :] - all_top[None]), axis=0)
    row_lse = all_top + jnp.log(jnp.where(own_lanes[0:1, :], all_sum, 1.0))
    want_lse[column] = jnp.broadcast_to(jnp.where(own_lanes[0:1, :], row_lse, 0.0), (8, TILE))

    def want_copy(k):
        m = in_column(k)
        return remote(
            want_lse.at[column], want_lse.at[column], wl_send.at[k], wl_recv.at[column],
            lax.div(m, BLOCKS), v, lax.rem(m, BLOCKS),
        )

    start_each(NCOL, want_copy, wl_send, want_lse.at[0])

    chain(PACE[1])
    value_left, value_right = sums_end(part_mid, part_end, rs_recv.at[0])
    scaled[:, left] = value_left + bias[:, left]
    scaled[:, right] = value_right + bias[:, right]
    projected = scaled[...]
    squares[d] = jnp.broadcast_to(jnp.sum(projected * projected, axis=1, keepdims=True), (ROWS, 128))

    def to_blocks(buf, send, recv):
        def copy(k):
            return remote(buf.at[d], buf.at[d], send.at[k], recv.at[d], l, v, lax.rem(d + k, BLOCKS))

        start_each(BLOCKS, copy, send, buf.at[0])

    def from_blocks(buf, recv):
        def come(k):
            dd = lax.rem(d + k, BLOCKS)
            arrive(buf.at[dd], recv.at[dd])

        each(1, BLOCKS, come)

    to_blocks(squares, sq_send, sq_recv)
    chain(PACE[2])
    from_blocks(squares, sq_recv)
    inverse = lax.rsqrt(jnp.sum(squares[...], axis=0)[:, :1] / D + epsilon)
    scaled[...] = projected * inverse
    normed[d, y, x] = (scaled[...] * gain[...]).astype(bf16)

    mine = normed.at[d, y, x]
    opp_copy = remote(mine, mine, opp_send, opp_recv, l, v, opp)
    opp_copy.start()
    leaving.append(opp_copy.wait_send)

    def to_sibling(block, i):
        copy = remote(normed.at[block], normed.at[block], sib_send.at[i], sib_recv.at[i], l, v, sib)
        copy.start()
        leaving.append(copy.wait_send)

    here, there = normed.at[d], normed.at[opp]
    gather_start(here, ag_send.at[0], ag_recv.at[0])
    chain(PACE[3])
    gather_middle(here, ag_send.at[0], ag_recv.at[0])
    arrive(normed.at[opp, y, x], opp_recv)
    gather_start(there, ag_send.at[1], ag_recv.at[1])
    turned[...] = hidden[...].T
    chain(PACE[4])
    gather_middle(there, ag_send.at[1], ag_recv.at[1])
    chain(PACE[5])
    gather_end(here, ag_recv.at[0])
    to_sibling(d, 0)
    chain(PACE[6])
    gather_end(there, ag_recv.at[1])
    to_sibling(opp, 1)
    own_head.wait()
    own_final.wait()

    def multiply(block, lo, hi, spans=((0, BLOCK),), first=False):
        def go(n):
            at = aligned(n * 256, 256)
            value = None
            for a, b in spans:
                term = jnp.dot(
                    normed[block, :, :, :, a:b].reshape(TOKENS, b - a), heads[block, a:b, at],
                    preferred_element_type=f32,
                )
                value = term if value is None else value + term
            if first:
                logits[:, at] = value
            else:
                logits[:, at] += value

        each(lo, hi, go)

    def passed(k):
        for s in (0, 1):
            arrive(heads.at[opp_sib, rows_of(s, k), :], pass_recv.at[s, k])

    EARLY = CHUNKS // 2
    early = ((0, HALF // 2), (HALF, HALF + HALF // 2))
    late = ((HALF // 2, HALF), (HALF + HALF // 2, BLOCK))
    multiply(d, 0, 2, first=True)
    chain(PACE[7])
    multiply(d, 2, 4, first=True)
    arrive(normed.at[sib], sib_recv.at[0])
    arrive(heads.at[sib], head_recv)
    chain(PACE[8])
    multiply(sib, 0, 2)
    chain(PACE[9])
    multiply(sib, 2, 4)
    chain(PACE[10])
    multiply(opp, 0, 4, early)
    chain(PACE[11])
    arrive(normed.at[opp_sib], sib_recv.at[1])
    each(0, EARLY, passed)
    multiply(opp_sib, 0, 4, early)
    chain(1)
    start_each(HALF_COLUMN, final_copy, fin_send, target.at[own_rows_final, :])
    multiply(opp, 0, 4, late)
    each(EARLY, CHUNKS, passed)
    multiply(opp_sib, 0, 4, late)

    for t in range(TOKENS // TILE):
        have = logits[t * TILE:(t + 1) * TILE, :]
        have_top = jnp.max(have, axis=1, keepdims=True)
        have_sum = jnp.sum(jnp.exp(have - have_top), axis=1, keepdims=True)
        tile_lane = lax.broadcasted_iota(jnp.int32, (TILE, TILE), 1)
        turned = jnp.where(tile_lane == 0, have_top, have_sum).T
        stats[v, t:t + 1, :] = turned[0:1, :]
        stats[v, 4 + t:5 + t, :] = turned[1:2, :]

    start_each(GROUPS, plane_copy(stats, st_send, st_recv), st_send, stats.at[0])

    def merge(buf):
        top = jnp.max(buf[:, 0:4, :], axis=0)
        return top, jnp.sum(buf[:, 4:8, :] * jnp.exp(buf[:, 0:4, :] - top[None]), axis=0)

    chain(2)
    plane_arrive(stats, st_recv)
    top, total = merge(stats)
    stats2[d] = jnp.concatenate([top, total], axis=0)
    to_blocks(stats2, st2_send, st2_recv)

    def want_arrived(k):
        m = in_column(k)
        arrive(want_lse.at[m], wl_recv.at[m])

    def final_arrived(k):
        m = lax.rem(in_half + k, HALF_COLUMN)
        rows = aligned((h * 2 + lax.rem(m, 2)) * TILE + lax.div(m, 2) * ROWS, ROWS)
        arrive(target.at[rows, :], fin_recv.at[m])

    def final_passed(k):
        for s in (0, 1):
            arrive(target.at[final_rows(s, k, opp_sib), :], fpass_recv.at[s, k])

    each(1, NCOL, want_arrived)
    each(1, HALF_COLUMN, final_arrived)
    each(0, FINALS, final_passed)
    for t in range(BLOCKS):
        lse[4 + t:5 + t, :] = (
            want_lse[t, 0:1, :] + want_lse[4 + t, 0:1, :] + want_lse[8 + t, 0:1, :] + want_lse[12 + t, 0:1, :]
        )
    from_blocks(stats2, st2_recv)
    top, total = merge(stats2)
    lse[0:4, :] = top + jnp.log(total)

    cross[...] = jnp.zeros((1, QUARTER), f32)
    for t in range(BLOCKS):
        at = pl.ds(t * TILE, TILE)
        have_lse = jnp.broadcast_to(lse[t:t + 1, :], (TILE, TILE)).T[:, 0:1]
        target_lse = jnp.broadcast_to(lse[4 + t:5 + t, :], (TILE, TILE)).T[:, 0:1]
        wanted = target[at, :].astype(f32)
        have = logits[at, :]
        want = jnp.exp(wanted - target_lse)
        grad = (jnp.exp(have - have_lse) - want).astype(bf16)
        grads[at, :] = grad
        inner[at, :] = jnp.broadcast_to(
            jnp.sum(grad.astype(f32) * have, axis=1, keepdims=True), (TILE, TILE)
        )
        cross[...] += jnp.sum(want * (wanted - have), axis=0, keepdims=True)

    def back(block, lo, hi, write):
        def go(n):
            write(
                n,
                lax.dot_general(
                    grads[...], heads[block, aligned(n * 256, 256), :], (((1,), (1,)), ((), ())),
                    preferred_element_type=f32,
                ),
            )

        each(lo, hi, go)

    def crossing_copy(i, n):
        return remote(crossing.at[i, n], crossed.at[i, n], gx_send.at[i, n], gx_recv.at[i, n], l, v, sib)

    for i, (theirs, ours) in enumerate(((opp_sib, opp), (sib, d))):
        def to_crossing(n, value, i=i):
            crossing[i, n] = value.astype(bf16)
            crossing_copy(i, n).start()

        def to_summing(n, value, i=i):
            arrive(crossed.at[i, n], gx_recv.at[i, n])
            value = (value + crossed[i, n].astype(f32)).astype(bf16)
            summing[i, :, :, :, aligned(n * 256, 256)] = value.reshape(SIDE, SIDE, ROWS, 256)

        back(theirs, 0, 4, to_crossing)
        leaving.append(lambda i=i: each(0, 4, lambda n: crossing_copy(i, n).wait_send()))
        back(ours, 0, 2, to_summing)
        sums_start(summing.at[i], sum_parts.at[i], rs_send.at[1 + i], rs_recv.at[1 + i], (0,))
        back(ours, 2, 4, to_summing)
        sums_start(summing.at[i], sum_parts.at[i], rs_send.at[1 + i], rs_recv.at[1 + i], (1,))

    for t in range(BLOCKS):
        crosses[v, t:t + 1, :] = inner[t * TILE:(t + 1) * TILE, :].T[0:1, :]
    crosses[v, 4:8, :] = jnp.broadcast_to(jnp.sum(cross[...], axis=1, keepdims=True), (4, 128))
    start_each(GROUPS, plane_copy(crosses, cr_send, cr_recv), cr_send, crosses.at[0])

    for i in (0, 1):
        sums_middle(
            summing.at[i], sum_parts.at[i], sum_mid.at[i], sum_end.at[i], rs_send.at[1 + i], rs_recv.at[1 + i]
        )
        if i == 0:
            plane_arrive(crosses, cr_recv)
            crosses2[d] = jnp.sum(crosses[...], axis=0)
            to_blocks(crosses2, cr2_send, cr2_recv)

    value_left, value_right = sums_end(sum_mid.at[0], sum_end.at[0], rs_recv.at[1])
    half_sum[:, left] = value_left.astype(bf16)
    half_sum[:, right] = value_right.astype(bf16)
    go_copy = remote(half_sum, other_sum, go_send, go_recv, l, v, opp)
    go_copy.start()
    leaving.append(go_copy.wait_send)
    value_left, value_right = sums_end(sum_mid.at[1], sum_end.at[1], rs_recv.at[2])
    finals[:, left] = value_left
    finals[:, right] = value_right
    from_blocks(crosses2, cr2_recv)
    crossed_all = jnp.sum(crosses2[...], axis=0)
    div_out[0] = (jnp.sum(crossed_all[4:5, 0:1]) + jnp.sum(lse[0:4, :] - lse[4:8, :])) / TOKENS
    lse[...] = crossed_all
    pad[...] = jnp.broadcast_to(lse[pl.ds(y, 1), :], (TILE, TILE)).T
    inner_mean = pad[own_rows(x), :][:, 0:1] / D
    arrive(other_sum, go_recv)

    grad_scaled = (finals[...] + other_sum[...].astype(f32)) * gain[...]
    inverse = lax.rsqrt(jnp.sum(squares[...], axis=0)[:, :1] / D + epsilon)
    gathered_grad[y, x] = (inverse * (grad_scaled - scaled[...] * inner_mean)).astype(bf16)
    gather_start(gathered_grad, ag_send.at[2], ag_recv.at[2])
    gather_middle(gathered_grad, ag_send.at[2], ag_recv.at[2])
    gather_end(gathered_grad, ag_recv.at[2])

    drain()


def products(turned, grad, divergence, weights_out, offsets_out, div_out):
    value = grad[...].reshape(TOKENS, grad.shape[-1])
    weights_out[0] = jnp.dot(turned[...], value, preferred_element_type=f32)
    offsets_out[...] = jnp.sum(value.astype(f32), axis=0, keepdims=True)
    div_out[0] = divergence[0]


def run(hidden, translator, bias, gain, head, final):
    dma = pltpu.SemaphoreType.DMA
    vmem = pltpu.VMEM
    in_vmem = pl.BlockSpec(memory_space=pltpu.VMEM)
    anywhere = pl.BlockSpec(memory_space=pl.ANY)
    width = hidden.shape[1]
    smem = pl.BlockSpec(memory_space=pltpu.SMEM)
    grad, turned, divergence = pl.pallas_call(
        kernel,
        out_shape=[
            jax.ShapeDtypeStruct((SIDE, SIDE, ROWS, BLOCK), bf16),
            jax.ShapeDtypeStruct((width, TOKENS), bf16),
            jax.ShapeDtypeStruct((1,), f32),
        ],
        in_specs=[anywhere] * 6,
        out_specs=[in_vmem, in_vmem, smem],
        scratch_shapes=[
            vmem((TOKENS, width), bf16),
            vmem((width, BLOCK), bf16),
            vmem((1, BLOCK), f32),
            vmem((1, BLOCK), f32),
            vmem((BLOCKS + 1, BLOCK, QUARTER), bf16),
            vmem((BLOCKS, SIDE, SIDE, ROWS, BLOCK), bf16),
            vmem((SIDE, SIDE, ROWS, BLOCK), f32),
            vmem((TOKENS, QUARTER), bf16),
            vmem((ROWS, BLOCKS * QUARTER), bf16),
            vmem((TILE, TILE), f32),
            vmem((ROWS, BLOCK), f32),
            vmem((BLOCKS, ROWS, 128), f32),
            vmem((TOKENS, QUARTER), f32),
            vmem((GROUPS, 8, TILE), f32),
            vmem((LAYERS * BLOCKS, 8, TILE), f32),
            vmem((GROUPS, 8, TILE), f32),
            vmem((BLOCKS, 8, TILE), f32),
            vmem((8, TILE), f32),
            vmem((1, QUARTER), f32),
            vmem((TOKENS, TILE), f32),
            vmem((GROUPS, 8, TILE), f32),
            vmem((BLOCKS, 8, TILE), f32),
            vmem((TOKENS, QUARTER), bf16),
            vmem((2, 4, TOKENS, 256), bf16),
            vmem((2, 4, TOKENS, 256), bf16),
            vmem((2, SIDE, SIDE, ROWS, BLOCK), bf16),
            vmem((2, SIDE, SIDE, ROWS, HALF), f32),
            vmem((2, SIDE, ROWS, HALF), f32),
            vmem((2, SIDE, ROWS, HALF), f32),
            vmem((2, 2, SIDE, SIDE, ROWS, HALF), bf16),
            vmem((2, 2, SIDE, ROWS, HALF), bf16),
            vmem((2, 2, SIDE, ROWS, HALF), bf16),
            vmem((ROWS, BLOCK), bf16),
            vmem((ROWS, BLOCK), bf16),
            vmem((ROWS, BLOCK), f32),
            vmem((ROWS, 2 * QUARTER), bf16),
            vmem((TILE, QUARTER), bf16),
            dma((2, 2, CHUNKS)), dma((2, 2, CHUNKS)),
            dma((2, CHUNKS)), dma((2, CHUNKS)),
            dma((2, 2, FINALS)), dma((2, 2, FINALS)),
            dma((2, FINALS)), dma((2, FINALS)),
            dma, dma,
            dma, dma,
            dma((16,)), dma((16,)),
            dma((BLOCKS,)), dma((BLOCKS,)),
            dma, dma,
            dma((2,)), dma((2,)),
            dma((GROUPS,)), dma((GROUPS,)),
            dma((16,)), dma((16,)),
            dma((GROUPS,)), dma((GROUPS,)),
            dma((BLOCKS,)), dma((BLOCKS,)),
            dma((GROUPS,)), dma((GROUPS,)),
            dma((BLOCKS,)), dma((BLOCKS,)),
            dma((2, 4)), dma((2, 4)),
            dma((3, 4, SIDE)), dma((3, 4, SIDE)),
            dma((3, 4, SIDE)), dma((3, 4, SIDE)),
            dma, dma,
            dma((7,)),
        ],
        compiler_params=pltpu.CompilerParams(
            collective_id=0, has_side_effects=True, vmem_limit_bytes=56 * 1024 * 1024
        ),
        name="lens",
    )(hidden, translator, bias, gain, head, final)
    tile = 256
    return pl.pallas_call(
        products,
        out_shape=[
            jax.ShapeDtypeStruct((1, width, BLOCK), f32),
            jax.ShapeDtypeStruct((1, BLOCK), f32),
            jax.ShapeDtypeStruct((1,), f32),
        ],
        grid=(BLOCK // tile,),
        in_specs=[
            pl.BlockSpec((width, TOKENS), lambda n: (0, 0)),
            pl.BlockSpec((SIDE, SIDE, ROWS, tile), lambda n: (0, 0, 0, n)),
            smem,
        ],
        out_specs=[
            pl.BlockSpec((1, width, tile), lambda n: (0, 0, n)),
            pl.BlockSpec((1, tile), lambda n: (0, n)),
            smem,
        ],
        name="products",
    )(turned, grad, divergence)


def shards(hidden, translator, bias, gain, head, final_logits):
    return tuple(run(hidden[0], translator[0], bias, gain[None], head, final_logits[0]))


def solution(mesh):
    in_specs = (
        P("layer", None, "vocab"),
        P("layer", "vocab", "dp"),
        P("layer", "dp"),
        P("dp"),
        P("dp", "vocab"),
        P("dp", "layer", "vocab"),
    )
    out_specs = (P("layer", "vocab", "dp"), P("layer", "dp"), P("layer"))
    return jax.shard_map(shards, mesh=mesh, in_specs=in_specs, out_specs=out_specs, check_vma=False)
```

```python
import jax
import jax.numpy as jnp
from jax import lax
from jax.experimental import pallas as pl
from jax.experimental.pallas import tpu as pltpu
from jax.sharding import PartitionSpec as P

D = 4096
TOKENS = 512
LAYERS = 4
GROUPS = 16
SIDE = 4
BLOCKS = 4
BLOCK = D // BLOCKS
QUARTER = 1024
ROWS = TOKENS // GROUPS
TILE = 128
HALF = BLOCK // 2
CHUNK = 32
CHUNKS = HALF // CHUNK
LAG = 3
FINALS = 2 * ROWS // CHUNK
PACE = (0.3, 0.4, 0.5, 0.58, 0.64, 0.82, 0.9, 0.92, 0.94, 0.96, 0.98, 1.0)

epsilon = 1e-05
f32 = jnp.float32
bf16 = jnp.bfloat16
MESH = pl.DeviceIdType.MESH


def aligned(start, size):
    return pl.ds(pl.multiple_of(start, size), size)


def each(lo, hi, f):
    def step(k, carry):
        f(k)
        return carry

    lax.fori_loop(lo, hi, step, 0)


def kernel(
    hidden_hbm, translator_hbm, bias_hbm, gain_hbm, head, final, gathered_grad, turned, div_out,
    hidden, translator, bias, gain,
    heads, normed, partial, target, final_own, pad, scaled, squares, logits,
    top_stats, want_lse, stats, stats2, lse, cross, crosses, crosses2, grads, crossing, crossed, summing,
    parts, part_mid, part_end, sum_parts, sum_mid, sum_end, half_sum, other_sum, finals,
    next_final, passing_final,
    chain_send, chain_recv, pass_send, pass_recv, fchain_send, fchain_recv, fpass_send, fpass_recv,
    next_send, next_recv, head_send, head_recv, fin_send, fin_recv,
    sq_send, sq_recv, opp_send, opp_recv, sib_send, sib_recv,
    top_send, top_recv, wl_send, wl_recv, st_send, st_recv, st2_send, st2_recv, cr_send, cr_recv,
    cr2_send, cr2_recv, gx_send, gx_recv, rs_send, rs_recv, ag_send, ag_recv,
    go_send, go_recv, local_sem,
):
    l = lax.axis_index("layer")
    v = lax.axis_index("vocab")
    d = lax.axis_index("dp")
    y = lax.div(v, SIDE)
    x = lax.rem(v, SIDE)
    h = lax.div(d, 2)
    c = lax.rem(d, 2)
    sib = h * 2 + 1 - c
    opp = lax.rem(d + 2, BLOCKS)
    opp_sib = (1 - h) * 2 + 1 - c
    up_l = lax.rem(l + 1, LAYERS)
    up_d = lax.rem(d + 2 * lax.div(l + 1, LAYERS), BLOCKS)
    down_l = lax.rem(l + LAYERS - 1, LAYERS)
    down_d = lax.rem(d + 2 * (1 - lax.div(l + LAYERS - 1, LAYERS)), BLOCKS)
    column = l * BLOCKS + d
    NCOL = LAYERS * BLOCKS

    def in_plane(k):
        return lax.rem(v + k, GROUPS)

    def in_column(k):
        return lax.rem(column + k, NCOL)

    def along_x(k):
        return lax.rem(x + k, SIDE)

    def along_y(k):
        return lax.rem(y + k, SIDE)

    def remote(src, dst, send, recv, ll, vv, dd):
        return pltpu.make_async_remote_copy(
            src_ref=src, dst_ref=dst, send_sem=send, recv_sem=recv,
            device_id=(ll, vv, dd), device_id_type=MESH,
        )

    def arrive(dst, sem):
        remote(dst, dst, sem, sem, l, v, d).wait_recv()

    def sent(src, sem):
        remote(src, src, sem, sem, l, v, d).wait_send()

    leaving = []

    def drain():
        for f in leaving:
            f()

    def start_each(count, make, send, shape):
        each(1, count, lambda k: make(k).start())
        leaving.append(lambda: each(1, count, lambda k: sent(shape, send.at[k])))

    def cols(q):
        return aligned(q * QUARTER, QUARTER)

    def own_rows(p):
        return aligned(p * ROWS, ROWS)

    staged = [
        pltpu.make_async_copy(src, dst, local_sem.at[3 + n])
        for n, (src, dst) in enumerate(
            ((hidden_hbm, hidden), (translator_hbm, translator), (bias_hbm, bias), (gain_hbm, gain))
        )
    ]
    for copy in staged:
        copy.start()
    own_head = pltpu.make_async_copy(head.at[:, cols(d)], heads.at[d], local_sem.at[0])
    own_head.start()
    own_rows_final = aligned(d * TILE + l * ROWS, ROWS)
    own_final = pltpu.make_async_copy(final.at[:, cols(d)], target.at[own_rows_final, :], local_sem.at[1])
    own_final.start()
    whole_final = pltpu.make_async_copy(final, final_own, local_sem.at[2])
    whole_final.start()

    barrier = pltpu.get_barrier_semaphore()

    def greet_plane(k):
        pl.semaphore_signal(barrier, inc=1, device_id=(l, in_plane(k), d), device_id_type=MESH)

    def greet_column(k):
        m = in_column(k)
        pl.semaphore_signal(
            barrier, inc=1, device_id=(lax.div(m, BLOCKS), v, lax.rem(m, BLOCKS)), device_id_type=MESH
        )

    each(1, GROUPS, greet_plane)
    each(1, NCOL, greet_column)

    def product(n):
        at = aligned(n * 256, 256)
        value = jnp.dot(hidden[...], translator[:, at], preferred_element_type=f32)
        partial[:, :, :, at] = value.reshape(SIDE, SIDE, ROWS, 256)

    for copy in staged:
        copy.wait()
    each(0, BLOCK // 256, product)
    pl.semaphore_wait(barrier, GROUPS - 1 + NCOL - 1)

    def rows_of(s, k):
        return aligned(s * HALF + k * CHUNK, CHUNK)

    def slot(j):
        return opp + j * (BLOCKS - opp)

    def chain_copy(s, j, k, from_own):
        rows = rows_of(s, k)
        ll, dd = (up_l, up_d) if s == 0 else (down_l, down_d)
        if from_own:
            src = head.at[rows, cols((1 - h) * 2 + (c if j == 0 else 1 - c))]
            dst = heads.at[d if j == 0 else BLOCKS, rows, :]
        else:
            src = heads.at[slot(j), rows, :]
            dst = src
        return remote(src, dst, chain_send.at[s, j, k], chain_recv.at[s, j, k], ll, v, dd)

    ends = (l == LAYERS - 1, l == 0)
    relays = (l != LAYERS - 1, l != 0)

    def source(s):
        def one(k):
            chain_copy(s, 0, k, True).start()
            chain_copy(s, 1, k, True).start()

        @pl.when(ends[s])
        def _():
            each(0, CHUNKS, one)

    def final_at(s, k):
        return (LAYERS - 1 - k if s == 0 else k) * ROWS

    def final_rows(s, k, block):
        return aligned(block * TILE + final_at(s, k), CHUNK)

    def final_chain(s, j, k, src, block):
        ll, dd = (up_l, up_d) if s == 0 else (down_l, down_d)
        dst = target.at[final_rows(s, k, block), :] if j == 0 else passing_final.at[aligned(final_at(s, k), CHUNK), :]
        return remote(
            dst if src is None else src, dst, fchain_send.at[s, j, k], fchain_recv.at[s, j, k], ll, v, dd
        )

    def final_source(s, lo, hi):
        def one(k):
            rows = aligned(0, CHUNK)
            for j in (0, 1):
                q = c if j == 0 else 1 - c
                if lo == 0:
                    src = final.at[rows, cols((1 - h) * 2 + q)]
                else:
                    src = next_final.at[rows, cols(q)]
                final_chain(s, j, k, src, d).start()

        each(lo, hi, one)

    next_copy = remote(
        final.at[:, aligned((1 - h) * 2 * QUARTER, 2 * QUARTER)], next_final, next_send, next_recv, 3 * (l - 1), v, d
    )
    inner_layer = jnp.logical_and(l > 0, l < LAYERS - 1)

    def next_sent():
        @pl.when(inner_layer)
        def _():
            next_copy.wait_send()

    leaving.append(next_sent)

    def chain_sent(k):
        for s in (0, 1):
            chain_copy(s, 0, k, False).wait_send()
            chain_copy(s, 1, k, False).wait_send()
            sent(heads.at[BLOCKS, rows_of(s, k), :], pass_send.at[s, k])

    def final_chain_sent(k):
        for s in (0, 1):
            final_chain(s, 0, k, None, opp).wait_send()
            final_chain(s, 1, k, None, opp).wait_send()
            sent(passing_final.at[0:CHUNK, :], fpass_send.at[s, k])

    leaving.append(lambda: each(0, CHUNKS, chain_sent))
    leaving.append(lambda: each(0, FINALS, final_chain_sent))
    lag = (LAG * l, LAG * (LAYERS - 1 - l))
    TURNS = 2 * CHUNKS + LAG * (LAYERS - 1)
    done = [0]

    def chain(until):
        def one(turn):
            for s in (0, 1):
                u = turn - lag[s]

                @pl.when(jnp.logical_and(u >= 0, u < 2 * CHUNKS))
                def _(s=s, u=u):
                    k, j = lax.div(u, 2), lax.rem(u, 2)
                    rows = rows_of(s, k)
                    arrive(heads.at[slot(j), rows, :], chain_recv.at[s, j, k])

                    @pl.when(relays[s])
                    def _():
                        chain_copy(s, j, k, False).start()

                    @pl.when(j == 1)
                    def _():
                        remote(
                            heads.at[BLOCKS, rows, :], heads.at[opp, rows, :],
                            pass_send.at[s, k], pass_recv.at[s, k], l, v, sib,
                        ).start()

                @pl.when(jnp.logical_and(u >= 2 * CHUNKS, u < 2 * (CHUNKS + FINALS)))
                def _(s=s, u=u - 2 * CHUNKS):
                    k, j = lax.div(u, 2), lax.rem(u, 2)
                    rows = final_rows(s, k, opp)
                    passed_rows = passing_final.at[aligned(final_at(s, k), CHUNK), :]

                    @pl.when(j == 0)
                    def _():
                        arrive(target.at[rows, :], fchain_recv.at[s, 0, k])

                        @pl.when(relays[s])
                        def _():
                            final_chain(s, 0, k, None, opp).start()

                    @pl.when(j == 1)
                    def _():
                        arrive(passed_rows, fchain_recv.at[s, 1, k])

                        @pl.when(relays[s])
                        def _():
                            final_chain(s, 1, k, None, opp).start()

                        remote(
                            passed_rows, target.at[rows, :], fpass_send.at[s, k], fpass_recv.at[s, k], l, v, sib
                        ).start()

        hi = min(int(TURNS * until), TURNS + 2 * FINALS)
        each(done[0], hi, one)
        done[0] = hi

    HALF_COLUMN = LAYERS * 2
    in_half = l * 2 + c

    def final_copy(k):
        m = lax.rem(in_half + k, HALF_COLUMN)
        dd = h * 2 + lax.rem(m, 2)
        return remote(
            final.at[:, cols(dd)], target.at[own_rows_final, :],
            fin_send.at[k], fin_recv.at[in_half], lax.div(m, 2), v, dd,
        )

    left = pl.ds(0, HALF)
    right = pl.ds(HALF, HALF)

    def at_x(k):
        return y * SIDE + along_x(k)

    def at_y(k):
        return along_y(k) * SIDE + x

    def sums_start(src, part, send, recv, ways=(0, 1)):
        if 0 in ways:
            start_each(
                SIDE,
                lambda k: remote(
                    src.at[:, along_x(k), :, left], part.at[0, x], send.at[0, k], recv.at[0, x], l, at_x(k), d
                ),
                send.at[0], part.at[0, 0],
            )
        if 1 in ways:
            start_each(
                SIDE,
                lambda k: remote(
                    src.at[along_y(k), :, :, right], part.at[1, y], send.at[1, k], recv.at[1, y], l, at_y(k), d
                ),
                send.at[1], part.at[0, 0],
            )

    def sums_middle(src, part, mid, end, send, recv):
        each(1, SIDE, lambda k: arrive(part.at[0, along_x(k)], recv.at[0, along_x(k)]))
        for n in range(SIDE):
            value = src[n, x, :, left].astype(f32)
            for k in range(1, SIDE):
                value += part[0, along_x(k), n].astype(f32)
            mid[0, n] = value.astype(mid.dtype)
        start_each(
            SIDE,
            lambda k: remote(
                mid.at[0, along_y(k)], end.at[0, y], send.at[2, k], recv.at[2, y], l, at_y(k), d
            ),
            send.at[2], end.at[0, 0],
        )
        each(1, SIDE, lambda k: arrive(part.at[1, along_y(k)], recv.at[1, along_y(k)]))
        for n in range(SIDE):
            value = src[y, n, :, right].astype(f32)
            for k in range(1, SIDE):
                value += part[1, along_y(k), n].astype(f32)
            mid[1, n] = value.astype(mid.dtype)
        start_each(
            SIDE,
            lambda k: remote(
                mid.at[1, along_x(k)], end.at[1, x], send.at[3, k], recv.at[3, x], l, at_x(k), d
            ),
            send.at[3], end.at[0, 0],
        )

    def sums_end(mid, end, recv):
        each(1, SIDE, lambda k: arrive(end.at[0, along_y(k)], recv.at[2, along_y(k)]))
        each(1, SIDE, lambda k: arrive(end.at[1, along_x(k)], recv.at[3, along_x(k)]))
        value_left = mid[0, y].astype(f32)
        value_right = mid[1, x].astype(f32)
        for k in range(1, SIDE):
            value_left += end[0, along_y(k)].astype(f32)
            value_right += end[1, along_x(k)].astype(f32)
        return value_left, value_right

    def gather_start(buf, send, recv):
        my_left = buf.at[y, x, :, left]
        my_right = buf.at[y, x, :, right]
        start_each(
            SIDE, lambda k: remote(my_left, my_left, send.at[0, k], recv.at[0, x], l, at_x(k), d), send.at[0], my_left
        )
        start_each(
            SIDE, lambda k: remote(my_right, my_right, send.at[1, k], recv.at[1, y], l, at_y(k), d),
            send.at[1], my_right,
        )

    def gather_middle(buf, send, recv):
        row_left = buf.at[y, :, :, left]
        column_right = buf.at[:, x, :, right]
        each(1, SIDE, lambda k: arrive(buf.at[y, along_x(k), :, left], recv.at[0, along_x(k)]))
        start_each(
            SIDE, lambda k: remote(row_left, row_left, send.at[2, k], recv.at[2, y], l, at_y(k), d),
            send.at[2], row_left,
        )
        each(1, SIDE, lambda k: arrive(buf.at[along_y(k), x, :, right], recv.at[1, along_y(k)]))
        start_each(
            SIDE, lambda k: remote(column_right, column_right, send.at[3, k], recv.at[3, x], l, at_x(k), d),
            send.at[3], column_right,
        )

    def gather_end(buf, recv):
        each(1, SIDE, lambda k: arrive(buf.at[along_y(k), :, :, left], recv.at[2, along_y(k)]))
        each(1, SIDE, lambda k: arrive(buf.at[:, along_x(k), :, right], recv.at[3, along_x(k)]))

    @pl.when(inner_layer)
    def _():
        next_copy.start()
        each(1, HALF_COLUMN, lambda k: final_copy(k).start())

    leaving.append(lambda: each(1, HALF_COLUMN, lambda k: sent(target.at[own_rows_final, :], fin_send.at[k])))

    source(0)
    source(1)
    for s in (0, 1):
        @pl.when(ends[s])
        def _(s=s):
            final_source(s, 0, 1)

    sums_start(partial, parts, rs_send.at[0], rs_recv.at[0])
    head_copy = remote(head.at[:, cols(sib)], heads.at[d], head_send, head_recv, l, v, sib)
    head_copy.start()
    leaving.append(head_copy.wait_send)

    lane = lax.broadcasted_iota(jnp.int32, (8, TILE), 1)
    own_lanes = jnp.logical_and(lane >= l * ROWS, lane < l * ROWS + ROWS)
    pad[...] = jnp.zeros((TILE, TILE), f32)
    whole_final.wait()
    chain(0.1)
    wanted = final_own[...].astype(f32)
    want_top = jnp.max(wanted, axis=1, keepdims=True)
    want_sum = jnp.sum(jnp.exp(wanted - want_top), axis=1, keepdims=True)
    column_lane = lax.broadcasted_iota(jnp.int32, (ROWS, TILE), 1)
    pad[own_rows(l), :] = jnp.where(column_lane == 0, want_top, want_sum)
    top_stats[v] = pad[...].T[0:8, :]

    def plane_copy(buf, send, recv):
        return lambda k: remote(buf.at[v], buf.at[v], send.at[k], recv.at[v], l, in_plane(k), d)

    def plane_arrive(buf, recv):
        each(1, GROUPS, lambda k: arrive(buf.at[in_plane(k)], recv.at[in_plane(k)]))

    start_each(GROUPS, plane_copy(top_stats, top_send, top_recv), top_send, top_stats.at[0])
    chain(PACE[0])
    for s in (0, 1):
        @pl.when(ends[s])
        def _(s=s):
            arrive(next_final, next_recv)
            final_source(s, 1, FINALS)

    sums_middle(partial, parts, part_mid, part_end, rs_send.at[0], rs_recv.at[0])
    chain(PACE[1])
    value_left, value_right = sums_end(part_mid, part_end, rs_recv.at[0])
    scaled[:, left] = value_left + bias[:, left]
    scaled[:, right] = value_right + bias[:, right]
    projected = scaled[...]
    squares[d] = jnp.broadcast_to(jnp.sum(projected * projected, axis=1, keepdims=True), (ROWS, 128))

    def to_blocks(buf, send, recv):
        def copy(k):
            return remote(buf.at[d], buf.at[d], send.at[k], recv.at[d], l, v, lax.rem(d + k, BLOCKS))

        start_each(BLOCKS, copy, send, buf.at[0])

    def from_blocks(buf, recv):
        def come(k):
            dd = lax.rem(d + k, BLOCKS)
            arrive(buf.at[dd], recv.at[dd])

        each(1, BLOCKS, come)

    to_blocks(squares, sq_send, sq_recv)
    chain(PACE[2])
    from_blocks(squares, sq_recv)
    inverse = lax.rsqrt(jnp.sum(squares[...], axis=0)[:, :1] / D + epsilon)
    scaled[...] = projected * inverse
    normed[d, y, x] = (scaled[...] * gain[...]).astype(bf16)

    mine = normed.at[d, y, x]
    opp_copy = remote(mine, mine, opp_send, opp_recv, l, v, opp)
    opp_copy.start()
    leaving.append(opp_copy.wait_send)

    def to_sibling(block, i):
        copy = remote(normed.at[block], normed.at[block], sib_send.at[i], sib_recv.at[i], l, v, sib)
        copy.start()
        leaving.append(copy.wait_send)

    here, there = normed.at[d], normed.at[opp]
    gather_start(here, ag_send.at[0], ag_recv.at[0])
    chain(PACE[3])
    gather_middle(here, ag_send.at[0], ag_recv.at[0])
    arrive(normed.at[opp, y, x], opp_recv)
    gather_start(there, ag_send.at[1], ag_recv.at[1])
    turned[...] = hidden[...].T
    chain(PACE[4])
    gather_middle(there, ag_send.at[1], ag_recv.at[1])
    plane_arrive(top_stats, top_recv)
    all_top = jnp.max(top_stats[:, 0:1, :], axis=0)
    all_sum = jnp.sum(top_stats[:, 1:2, :] * jnp.exp(top_stats[:, 0:1, :] - all_top[None]), axis=0)
    row_lse = all_top + jnp.log(jnp.where(own_lanes[0:1, :], all_sum, 1.0))
    want_lse[column] = jnp.broadcast_to(jnp.where(own_lanes[0:1, :], row_lse, 0.0), (8, TILE))

    def want_copy(k):
        m = in_column(k)
        return remote(
            want_lse.at[column], want_lse.at[column], wl_send.at[k], wl_recv.at[column],
            lax.div(m, BLOCKS), v, lax.rem(m, BLOCKS),
        )

    start_each(NCOL, want_copy, wl_send, want_lse.at[0])
    chain(PACE[5])
    gather_end(here, ag_recv.at[0])
    to_sibling(d, 0)
    chain(PACE[6])
    gather_end(there, ag_recv.at[1])
    to_sibling(opp, 1)
    own_head.wait()
    own_final.wait()

    def multiply(block, lo, hi, spans=((0, BLOCK),), first=False):
        def go(n):
            at = aligned(n * 256, 256)
            value = None
            for a, b in spans:
                term = jnp.dot(
                    normed[block, :, :, :, a:b].reshape(TOKENS, b - a), heads[block, a:b, at],
                    preferred_element_type=f32,
                )
                value = term if value is None else value + term
            if first:
                logits[:, at] = value
            else:
                logits[:, at] += value

        each(lo, hi, go)

    def passed(k):
        for s in (0, 1):
            arrive(heads.at[opp_sib, rows_of(s, k), :], pass_recv.at[s, k])

    EARLY = CHUNKS // 2
    early = ((0, HALF // 2), (HALF, HALF + HALF // 2))
    late = ((HALF // 2, HALF), (HALF + HALF // 2, BLOCK))
    multiply(d, 0, 2, first=True)
    chain(PACE[7])
    multiply(d, 2, 4, first=True)
    arrive(normed.at[sib], sib_recv.at[0])
    arrive(heads.at[sib], head_recv)
    chain(PACE[8])
    multiply(sib, 0, 2)
    chain(PACE[9])
    multiply(sib, 2, 4)
    chain(PACE[10])
    multiply(opp, 0, 4, early)
    chain(PACE[11])
    arrive(normed.at[opp_sib], sib_recv.at[1])
    each(0, EARLY, passed)
    multiply(opp_sib, 0, 4, early)
    chain(1)
    @pl.when(jnp.logical_not(inner_layer))
    def _():
        each(1, HALF_COLUMN, lambda k: final_copy(k).start())

    multiply(opp, 0, 4, late)
    each(EARLY, CHUNKS, passed)
    multiply(opp_sib, 0, 4, late)

    for t in range(TOKENS // TILE):
        have = logits[t * TILE:(t + 1) * TILE, :]
        have_top = jnp.max(have, axis=1, keepdims=True)
        have_sum = jnp.sum(jnp.exp(have - have_top), axis=1, keepdims=True)
        tile_lane = lax.broadcasted_iota(jnp.int32, (TILE, TILE), 1)
        turned = jnp.where(tile_lane == 0, have_top, have_sum).T
        stats[v, t:t + 1, :] = turned[0:1, :]
        stats[v, 4 + t:5 + t, :] = turned[1:2, :]

    start_each(GROUPS, plane_copy(stats, st_send, st_recv), st_send, stats.at[0])

    def merge(buf):
        top = jnp.max(buf[:, 0:4, :], axis=0)
        return top, jnp.sum(buf[:, 4:8, :] * jnp.exp(buf[:, 0:4, :] - top[None]), axis=0)

    chain(2)
    plane_arrive(stats, st_recv)
    top, total = merge(stats)
    stats2[d] = jnp.concatenate([top, total], axis=0)
    to_blocks(stats2, st2_send, st2_recv)

    def want_arrived(k):
        m = in_column(k)
        arrive(want_lse.at[m], wl_recv.at[m])

    def final_arrived(k):
        m = lax.rem(in_half + k, HALF_COLUMN)
        rows = aligned((h * 2 + lax.rem(m, 2)) * TILE + lax.div(m, 2) * ROWS, ROWS)
        arrive(target.at[rows, :], fin_recv.at[m])

    def final_passed(k):
        for s in (0, 1):
            arrive(target.at[final_rows(s, k, opp_sib), :], fpass_recv.at[s, k])

    each(1, NCOL, want_arrived)
    each(1, HALF_COLUMN, final_arrived)
    each(0, FINALS, final_passed)
    for t in range(BLOCKS):
        lse[4 + t:5 + t, :] = (
            want_lse[t, 0:1, :] + want_lse[4 + t, 0:1, :] + want_lse[8 + t, 0:1, :] + want_lse[12 + t, 0:1, :]
        )
    from_blocks(stats2, st2_recv)
    top, total = merge(stats2)
    lse[0:4, :] = top + jnp.log(total)

    def lse_columns(t):
        have_lse = jnp.broadcast_to(lse[t:t + 1, :], (TILE, TILE)).T[:, 0:1]
        return have_lse, jnp.broadcast_to(lse[4 + t:5 + t, :], (TILE, TILE)).T[:, 0:1]

    for t in range(BLOCKS):
        at = pl.ds(t * TILE, TILE)
        have_lse, target_lse = lse_columns(t)
        want = jnp.exp(target[at, :].astype(f32) - target_lse)
        grads[at, :] = (jnp.exp(logits[at, :] - have_lse) - want).astype(bf16)

    def back(block, lo, hi, write):
        def go(n):
            write(
                n,
                lax.dot_general(
                    grads[...], heads[block, aligned(n * 256, 256), :], (((1,), (1,)), ((), ())),
                    preferred_element_type=f32,
                ),
            )

        each(lo, hi, go)

    def crossing_copy(i, n):
        return remote(crossing.at[i, n], crossed.at[i, n], gx_send.at[i, n], gx_recv.at[i, n], l, v, sib)

    for i, (theirs, ours) in enumerate(((opp_sib, opp), (sib, d))):
        def to_crossing(n, value, i=i):
            crossing[i, n] = value.astype(bf16)
            crossing_copy(i, n).start()

        def to_summing(n, value, i=i):
            arrive(crossed.at[i, n], gx_recv.at[i, n])
            value = (value + crossed[i, n].astype(f32)).astype(bf16)
            summing[i, :, :, :, aligned(n * 256, 256)] = value.reshape(SIDE, SIDE, ROWS, 256)

        back(theirs, 0, 4, to_crossing)
        leaving.append(lambda i=i: each(0, 4, lambda n: crossing_copy(i, n).wait_send()))
        back(ours, 0, 2, to_summing)
        sums_start(summing.at[i], sum_parts.at[i], rs_send.at[1 + i], rs_recv.at[1 + i], (0,))
        back(ours, 2, 4, to_summing)
        sums_start(summing.at[i], sum_parts.at[i], rs_send.at[1 + i], rs_recv.at[1 + i], (1,))

    cross[...] = jnp.zeros((1, QUARTER), f32)
    for t in range(BLOCKS):
        at = pl.ds(t * TILE, TILE)
        wanted = target[at, :].astype(f32)
        have = logits[at, :]
        want = jnp.exp(wanted - lse_columns(t)[1])
        cross[...] += jnp.sum(want * (wanted - have), axis=0, keepdims=True)
        inner = jnp.sum(grads[at, :].astype(f32) * have, axis=1, keepdims=True)
        crosses[v, t:t + 1, :] = jnp.broadcast_to(inner, (TILE, TILE)).T[0:1, :]
    crosses[v, 4:8, :] = jnp.broadcast_to(jnp.sum(cross[...], axis=1, keepdims=True), (4, 128))
    start_each(GROUPS, plane_copy(crosses, cr_send, cr_recv), cr_send, crosses.at[0])

    for i in (0, 1):
        sums_middle(
            summing.at[i], sum_parts.at[i], sum_mid.at[i], sum_end.at[i], rs_send.at[1 + i], rs_recv.at[1 + i]
        )
        if i == 0:
            plane_arrive(crosses, cr_recv)
            crosses2[d] = jnp.sum(crosses[...], axis=0)
            to_blocks(crosses2, cr2_send, cr2_recv)

    value_left, value_right = sums_end(sum_mid.at[0], sum_end.at[0], rs_recv.at[1])
    half_sum[:, left] = value_left.astype(bf16)
    half_sum[:, right] = value_right.astype(bf16)
    go_copy = remote(half_sum, other_sum, go_send, go_recv, l, v, opp)
    go_copy.start()
    leaving.append(go_copy.wait_send)
    value_left, value_right = sums_end(sum_mid.at[1], sum_end.at[1], rs_recv.at[2])
    finals[:, left] = value_left
    finals[:, right] = value_right
    from_blocks(crosses2, cr2_recv)
    crossed_all = jnp.sum(crosses2[...], axis=0)
    div_out[0] = (jnp.sum(crossed_all[4:5, 0:1]) + jnp.sum(lse[0:4, :] - lse[4:8, :])) / TOKENS
    lse[...] = crossed_all
    pad[...] = jnp.broadcast_to(lse[pl.ds(y, 1), :], (TILE, TILE)).T
    inner_mean = pad[own_rows(x), :][:, 0:1] / D
    arrive(other_sum, go_recv)

    grad_scaled = (finals[...] + other_sum[...].astype(f32)) * gain[...]
    inverse = lax.rsqrt(jnp.sum(squares[...], axis=0)[:, :1] / D + epsilon)
    gathered_grad[y, x] = (inverse * (grad_scaled - scaled[...] * inner_mean)).astype(bf16)
    gather_start(gathered_grad, ag_send.at[2], ag_recv.at[2])
    gather_middle(gathered_grad, ag_send.at[2], ag_recv.at[2])
    gather_end(gathered_grad, ag_recv.at[2])

    drain()


def products(
    turned_in, grad_in, divergence, weights_out, offsets_out, div_out, turned, grad, weights, in_sem, out_sem
):
    tiles, tile = grad.shape[0], grad.shape[-1]

    def part(n):
        return pl.ds(n * tile, tile)

    whole = pltpu.make_async_copy(turned_in, turned, in_sem.at[tiles])
    whole.start()
    ins = [pltpu.make_async_copy(grad_in.at[:, :, :, part(n)], grad.at[n], in_sem.at[n]) for n in range(tiles)]
    outs = [pltpu.make_async_copy(weights.at[n], weights_out.at[0, :, part(n)], out_sem.at[n]) for n in range(tiles)]
    for copy in ins:
        copy.start()
    whole.wait()
    for n in range(tiles):
        ins[n].wait()
        value = grad[n].reshape(TOKENS, tile)
        weights[n] = jnp.dot(turned[...], value, preferred_element_type=f32)
        outs[n].start()
        offsets_out[:, part(n)] = jnp.sum(value.astype(f32), axis=0, keepdims=True)
    div_out[0] = divergence[0]
    for copy in outs:
        copy.wait()


def run(hidden, translator, bias, gain, head, final):
    dma = pltpu.SemaphoreType.DMA
    vmem = pltpu.VMEM
    in_vmem = pl.BlockSpec(memory_space=pltpu.VMEM)
    anywhere = pl.BlockSpec(memory_space=pl.ANY)
    width = hidden.shape[1]
    smem = pl.BlockSpec(memory_space=pltpu.SMEM)
    grad, turned, divergence = pl.pallas_call(
        kernel,
        out_shape=[
            jax.ShapeDtypeStruct((SIDE, SIDE, ROWS, BLOCK), bf16),
            jax.ShapeDtypeStruct((width, TOKENS), bf16),
            jax.ShapeDtypeStruct((1,), f32),
        ],
        in_specs=[anywhere] * 6,
        out_specs=[in_vmem, in_vmem, smem],
        scratch_shapes=[
            vmem((TOKENS, width), bf16),
            vmem((width, BLOCK), bf16),
            vmem((1, BLOCK), f32),
            vmem((1, BLOCK), f32),
            vmem((BLOCKS + 1, BLOCK, QUARTER), bf16),
            vmem((BLOCKS, SIDE, SIDE, ROWS, BLOCK), bf16),
            vmem((SIDE, SIDE, ROWS, BLOCK), f32),
            vmem((TOKENS, QUARTER), bf16),
            vmem((ROWS, BLOCKS * QUARTER), bf16),
            vmem((TILE, TILE), f32),
            vmem((ROWS, BLOCK), f32),
            vmem((BLOCKS, ROWS, 128), f32),
            vmem((TOKENS, QUARTER), f32),
            vmem((GROUPS, 8, TILE), f32),
            vmem((LAYERS * BLOCKS, 8, TILE), f32),
            vmem((GROUPS, 8, TILE), f32),
            vmem((BLOCKS, 8, TILE), f32),
            vmem((8, TILE), f32),
            vmem((1, QUARTER), f32),
            vmem((GROUPS, 8, TILE), f32),
            vmem((BLOCKS, 8, TILE), f32),
            vmem((TOKENS, QUARTER), bf16),
            vmem((2, 4, TOKENS, 256), bf16),
            vmem((2, 4, TOKENS, 256), bf16),
            vmem((2, SIDE, SIDE, ROWS, BLOCK), bf16),
            vmem((2, SIDE, SIDE, ROWS, HALF), f32),
            vmem((2, SIDE, ROWS, HALF), f32),
            vmem((2, SIDE, ROWS, HALF), f32),
            vmem((2, 2, SIDE, SIDE, ROWS, HALF), bf16),
            vmem((2, 2, SIDE, ROWS, HALF), bf16),
            vmem((2, 2, SIDE, ROWS, HALF), bf16),
            vmem((ROWS, BLOCK), bf16),
            vmem((ROWS, BLOCK), bf16),
            vmem((ROWS, BLOCK), f32),
            vmem((ROWS, 2 * QUARTER), bf16),
            vmem((TILE, QUARTER), bf16),
            dma((2, 2, CHUNKS)), dma((2, 2, CHUNKS)),
            dma((2, CHUNKS)), dma((2, CHUNKS)),
            dma((2, 2, FINALS)), dma((2, 2, FINALS)),
            dma((2, FINALS)), dma((2, FINALS)),
            dma, dma,
            dma, dma,
            dma((16,)), dma((16,)),
            dma((BLOCKS,)), dma((BLOCKS,)),
            dma, dma,
            dma((2,)), dma((2,)),
            dma((GROUPS,)), dma((GROUPS,)),
            dma((16,)), dma((16,)),
            dma((GROUPS,)), dma((GROUPS,)),
            dma((BLOCKS,)), dma((BLOCKS,)),
            dma((GROUPS,)), dma((GROUPS,)),
            dma((BLOCKS,)), dma((BLOCKS,)),
            dma((2, 4)), dma((2, 4)),
            dma((3, 4, SIDE)), dma((3, 4, SIDE)),
            dma((3, 4, SIDE)), dma((3, 4, SIDE)),
            dma, dma,
            dma((7,)),
        ],
        compiler_params=pltpu.CompilerParams(
            collective_id=0, has_side_effects=True, vmem_limit_bytes=56 * 1024 * 1024
        ),
        name="lens",
    )(hidden, translator, bias, gain, head, final)
    tile = 256
    return pl.pallas_call(
        products,
        out_shape=[
            jax.ShapeDtypeStruct((1, width, BLOCK), f32),
            jax.ShapeDtypeStruct((1, BLOCK), f32),
            jax.ShapeDtypeStruct((1,), f32),
        ],
        in_specs=[anywhere, anywhere, smem],
        out_specs=[anywhere, in_vmem, smem],
        scratch_shapes=[
            vmem((width, TOKENS), bf16),
            vmem((BLOCK // tile, SIDE, SIDE, ROWS, tile), bf16),
            vmem((BLOCK // tile, width, tile), f32),
            dma((BLOCK // tile + 1,)),
            dma((BLOCK // tile,)),
        ],
        name="products",
    )(turned, grad, divergence)


def shards(hidden, translator, bias, gain, head, final_logits):
    return tuple(run(hidden[0], translator[0], bias, gain[None], head, final_logits[0]))


def solution(mesh):
    in_specs = (
        P("layer", None, "vocab"),
        P("layer", "vocab", "dp"),
        P("layer", "dp"),
        P("dp"),
        P("dp", "vocab"),
        P("dp", "layer", "vocab"),
    )
    out_specs = (P("layer", "vocab", "dp"), P("layer", "dp"), P("layer"))
    return jax.shard_map(shards, mesh=mesh, in_specs=in_specs, out_specs=out_specs, check_vma=False)
```

```python
import jax
import jax.numpy as jnp
from jax import lax
from jax.experimental import pallas as pl
from jax.experimental.pallas import tpu as pltpu
from jax.sharding import PartitionSpec as P

D = 4096
TOKENS = 512
LAYERS = 4
GROUPS = 16
SIDE = 4
BLOCKS = 4
BLOCK = D // BLOCKS
QUARTER = 1024
ROWS = TOKENS // GROUPS
TILE = 128
HALF = BLOCK // 2
CHUNK = 32
CHUNKS = HALF // CHUNK
LAG = 3
FINALS = 2 * ROWS // CHUNK
PACE = (0.3, 0.4, 0.5, 0.58, 0.64, 0.82, 0.9, 0.92, 0.94, 0.96, 0.98, 1.0)

epsilon = 1e-05
f32 = jnp.float32
bf16 = jnp.bfloat16
MESH = pl.DeviceIdType.MESH


def aligned(start, size):
    return pl.ds(pl.multiple_of(start, size), size)


def each(lo, hi, f):
    def step(k, carry):
        f(k)
        return carry

    lax.fori_loop(lo, hi, step, 0)


def kernel(
    hidden_hbm, translator_hbm, bias_hbm, gain_hbm, head, final, gathered_grad, turned, div_out,
    hidden, translator, bias, gain,
    heads, normed, partial, target, final_own, pad, scaled, squares, logits,
    top_stats, want_lse, stats, stats2, lse, cross, crosses, crosses2, grads, crossing, crossed, summing,
    parts, part_mid, part_end, sum_parts, sum_mid, sum_end, half_sum, other_sum, finals,
    next_final, passing_final,
    chain_send, chain_recv, pass_send, pass_recv, fchain_send, fchain_recv, fpass_send, fpass_recv,
    next_send, next_recv, head_send, head_recv, fin_send, fin_recv,
    sq_send, sq_recv, opp_send, opp_recv, sib_send, sib_recv,
    top_send, top_recv, wl_send, wl_recv, st_send, st_recv, st2_send, st2_recv, cr_send, cr_recv,
    cr2_send, cr2_recv, gx_send, gx_recv, rs_send, rs_recv, ag_send, ag_recv,
    go_send, go_recv, local_sem,
):
    l = lax.axis_index("layer")
    v = lax.axis_index("vocab")
    d = lax.axis_index("dp")
    y = lax.div(v, SIDE)
    x = lax.rem(v, SIDE)
    h = lax.div(d, 2)
    c = lax.rem(d, 2)
    sib = h * 2 + 1 - c
    opp = lax.rem(d + 2, BLOCKS)
    opp_sib = (1 - h) * 2 + 1 - c
    up_l = lax.rem(l + 1, LAYERS)
    up_d = lax.rem(d + 2 * lax.div(l + 1, LAYERS), BLOCKS)
    down_l = lax.rem(l + LAYERS - 1, LAYERS)
    down_d = lax.rem(d + 2 * (1 - lax.div(l + LAYERS - 1, LAYERS)), BLOCKS)
    column = l * BLOCKS + d
    NCOL = LAYERS * BLOCKS

    def in_plane(k):
        return lax.rem(v + k, GROUPS)

    def in_column(k):
        return lax.rem(column + k, NCOL)

    def along_x(k):
        return lax.rem(x + k, SIDE)

    def along_y(k):
        return lax.rem(y + k, SIDE)

    def remote(src, dst, send, recv, ll, vv, dd):
        return pltpu.make_async_remote_copy(
            src_ref=src, dst_ref=dst, send_sem=send, recv_sem=recv,
            device_id=(ll, vv, dd), device_id_type=MESH,
        )

    def arrive(dst, sem):
        remote(dst, dst, sem, sem, l, v, d).wait_recv()

    def sent(src, sem):
        remote(src, src, sem, sem, l, v, d).wait_send()

    leaving = []

    def drain():
        for f in leaving:
            f()

    def start_each(count, make, send, shape):
        each(1, count, lambda k: make(k).start())
        leaving.append(lambda: each(1, count, lambda k: sent(shape, send.at[k])))

    def cols(q):
        return aligned(q * QUARTER, QUARTER)

    def own_rows(p):
        return aligned(p * ROWS, ROWS)

    staged = [
        pltpu.make_async_copy(src, dst, local_sem.at[3 + n])
        for n, (src, dst) in enumerate(
            ((hidden_hbm, hidden), (translator_hbm, translator), (bias_hbm, bias), (gain_hbm, gain))
        )
    ]
    for copy in staged:
        copy.start()
    own_head = pltpu.make_async_copy(head.at[:, cols(d)], heads.at[d], local_sem.at[0])
    own_head.start()
    own_rows_final = aligned(d * TILE + l * ROWS, ROWS)
    own_final = pltpu.make_async_copy(final.at[:, cols(d)], target.at[own_rows_final, :], local_sem.at[1])
    own_final.start()
    whole_final = pltpu.make_async_copy(final, final_own, local_sem.at[2])
    whole_final.start()

    barrier = pltpu.get_barrier_semaphore()

    def greet_plane(k):
        pl.semaphore_signal(barrier, inc=1, device_id=(l, in_plane(k), d), device_id_type=MESH)

    def greet_column(k):
        m = in_column(k)
        pl.semaphore_signal(
            barrier, inc=1, device_id=(lax.div(m, BLOCKS), v, lax.rem(m, BLOCKS)), device_id_type=MESH
        )

    each(1, GROUPS, greet_plane)
    each(1, NCOL, greet_column)

    def product(n):
        at = aligned(n * 256, 256)
        value = jnp.dot(hidden[...], translator[:, at], preferred_element_type=f32)
        partial[:, :, :, at] = value.reshape(SIDE, SIDE, ROWS, 256)

    for copy in staged:
        copy.wait()
    each(0, BLOCK // 256, product)
    pl.semaphore_wait(barrier, GROUPS - 1 + NCOL - 1)

    def rows_of(s, k):
        return aligned(s * HALF + k * CHUNK, CHUNK)

    def slot(j):
        return opp + j * (BLOCKS - opp)

    def chain_copy(s, j, k, from_own):
        rows = rows_of(s, k)
        ll, dd = (up_l, up_d) if s == 0 else (down_l, down_d)
        if from_own:
            src = head.at[rows, cols((1 - h) * 2 + (c if j == 0 else 1 - c))]
            dst = heads.at[d if j == 0 else BLOCKS, rows, :]
        else:
            src = heads.at[slot(j), rows, :]
            dst = src
        return remote(src, dst, chain_send.at[s, j, k], chain_recv.at[s, j, k], ll, v, dd)

    ends = (l == LAYERS - 1, l == 0)
    relays = (l != LAYERS - 1, l != 0)

    def source(s):
        def one(k):
            chain_copy(s, 0, k, True).start()
            chain_copy(s, 1, k, True).start()

        @pl.when(ends[s])
        def _():
            each(0, CHUNKS, one)

    def final_at(s, k):
        return (LAYERS - 1 - k if s == 0 else k) * ROWS

    def final_rows(s, k, block):
        return aligned(block * TILE + final_at(s, k), CHUNK)

    def final_chain(s, j, k, src, block):
        ll, dd = (up_l, up_d) if s == 0 else (down_l, down_d)
        dst = target.at[final_rows(s, k, block), :] if j == 0 else passing_final.at[aligned(final_at(s, k), CHUNK), :]
        return remote(
            dst if src is None else src, dst, fchain_send.at[s, j, k], fchain_recv.at[s, j, k], ll, v, dd
        )

    def final_source(s, lo, hi):
        def one(k):
            rows = aligned(0, CHUNK)
            for j in (0, 1):
                q = c if j == 0 else 1 - c
                if lo == 0:
                    src = final.at[rows, cols((1 - h) * 2 + q)]
                else:
                    src = next_final.at[rows, cols(q)]
                final_chain(s, j, k, src, d).start()

        each(lo, hi, one)

    next_copy = remote(
        final.at[:, aligned((1 - h) * 2 * QUARTER, 2 * QUARTER)], next_final, next_send, next_recv, 3 * (l - 1), v, d
    )
    inner_layer = jnp.logical_and(l > 0, l < LAYERS - 1)

    def next_sent():
        @pl.when(inner_layer)
        def _():
            next_copy.wait_send()

    leaving.append(next_sent)

    def chain_sent(k):
        for s in (0, 1):
            chain_copy(s, 0, k, False).wait_send()
            chain_copy(s, 1, k, False).wait_send()
            sent(heads.at[BLOCKS, rows_of(s, k), :], pass_send.at[s, k])

    def final_chain_sent(k):
        for s in (0, 1):
            final_chain(s, 0, k, None, opp).wait_send()
            final_chain(s, 1, k, None, opp).wait_send()
            sent(passing_final.at[0:CHUNK, :], fpass_send.at[s, k])

    leaving.append(lambda: each(0, CHUNKS, chain_sent))
    leaving.append(lambda: each(0, FINALS, final_chain_sent))
    lag = (LAG * l, LAG * (LAYERS - 1 - l))
    TURNS = 2 * CHUNKS + LAG * (LAYERS - 1)
    done = [0]

    def chain(until):
        def one(turn):
            for s in (0, 1):
                u = turn - lag[s]

                @pl.when(jnp.logical_and(u >= 0, u < 2 * CHUNKS))
                def _(s=s, u=u):
                    k, j = lax.div(u, 2), lax.rem(u, 2)
                    rows = rows_of(s, k)
                    arrive(heads.at[slot(j), rows, :], chain_recv.at[s, j, k])

                    @pl.when(relays[s])
                    def _():
                        chain_copy(s, j, k, False).start()

                    @pl.when(j == 1)
                    def _():
                        remote(
                            heads.at[BLOCKS, rows, :], heads.at[opp, rows, :],
                            pass_send.at[s, k], pass_recv.at[s, k], l, v, sib,
                        ).start()

                @pl.when(jnp.logical_and(u >= 2 * CHUNKS, u < 2 * (CHUNKS + FINALS)))
                def _(s=s, u=u - 2 * CHUNKS):
                    k, j = lax.div(u, 2), lax.rem(u, 2)
                    rows = final_rows(s, k, opp)
                    passed_rows = passing_final.at[aligned(final_at(s, k), CHUNK), :]

                    @pl.when(j == 0)
                    def _():
                        arrive(target.at[rows, :], fchain_recv.at[s, 0, k])

                        @pl.when(relays[s])
                        def _():
                            final_chain(s, 0, k, None, opp).start()

                    @pl.when(j == 1)
                    def _():
                        arrive(passed_rows, fchain_recv.at[s, 1, k])

                        @pl.when(relays[s])
                        def _():
                            final_chain(s, 1, k, None, opp).start()

                        remote(
                            passed_rows, target.at[rows, :], fpass_send.at[s, k], fpass_recv.at[s, k], l, v, sib
                        ).start()

        hi = min(int(TURNS * until), TURNS + 2 * FINALS)
        each(done[0], hi, one)
        done[0] = hi

    HALF_COLUMN = LAYERS * 2
    in_half = l * 2 + c

    def final_copy(k):
        m = lax.rem(in_half + k, HALF_COLUMN)
        dd = h * 2 + lax.rem(m, 2)
        return remote(
            final.at[:, cols(dd)], target.at[own_rows_final, :],
            fin_send.at[k], fin_recv.at[in_half], lax.div(m, 2), v, dd,
        )

    left = pl.ds(0, HALF)
    right = pl.ds(HALF, HALF)

    def at_x(k):
        return y * SIDE + along_x(k)

    def at_y(k):
        return along_y(k) * SIDE + x

    def sums_start(src, part, send, recv, ways=(0, 1)):
        if 0 in ways:
            start_each(
                SIDE,
                lambda k: remote(
                    src.at[:, along_x(k), :, left], part.at[0, x], send.at[0, k], recv.at[0, x], l, at_x(k), d
                ),
                send.at[0], part.at[0, 0],
            )
        if 1 in ways:
            start_each(
                SIDE,
                lambda k: remote(
                    src.at[along_y(k), :, :, right], part.at[1, y], send.at[1, k], recv.at[1, y], l, at_y(k), d
                ),
                send.at[1], part.at[0, 0],
            )

    def sums_middle(src, part, mid, end, send, recv):
        each(1, SIDE, lambda k: arrive(part.at[0, along_x(k)], recv.at[0, along_x(k)]))
        for n in range(SIDE):
            value = src[n, x, :, left].astype(f32)
            for k in range(1, SIDE):
                value += part[0, along_x(k), n].astype(f32)
            mid[0, n] = value.astype(mid.dtype)
        start_each(
            SIDE,
            lambda k: remote(
                mid.at[0, along_y(k)], end.at[0, y], send.at[2, k], recv.at[2, y], l, at_y(k), d
            ),
            send.at[2], end.at[0, 0],
        )
        each(1, SIDE, lambda k: arrive(part.at[1, along_y(k)], recv.at[1, along_y(k)]))
        for n in range(SIDE):
            value = src[y, n, :, right].astype(f32)
            for k in range(1, SIDE):
                value += part[1, along_y(k), n].astype(f32)
            mid[1, n] = value.astype(mid.dtype)
        start_each(
            SIDE,
            lambda k: remote(
                mid.at[1, along_x(k)], end.at[1, x], send.at[3, k], recv.at[3, x], l, at_x(k), d
            ),
            send.at[3], end.at[0, 0],
        )

    def sums_end(mid, end, recv):
        each(1, SIDE, lambda k: arrive(end.at[0, along_y(k)], recv.at[2, along_y(k)]))
        each(1, SIDE, lambda k: arrive(end.at[1, along_x(k)], recv.at[3, along_x(k)]))
        value_left = mid[0, y].astype(f32)
        value_right = mid[1, x].astype(f32)
        for k in range(1, SIDE):
            value_left += end[0, along_y(k)].astype(f32)
            value_right += end[1, along_x(k)].astype(f32)
        return value_left, value_right

    def gather_start(buf, send, recv):
        my_left = buf.at[y, x, :, left]
        my_right = buf.at[y, x, :, right]
        start_each(
            SIDE, lambda k: remote(my_left, my_left, send.at[0, k], recv.at[0, x], l, at_x(k), d), send.at[0], my_left
        )
        start_each(
            SIDE, lambda k: remote(my_right, my_right, send.at[1, k], recv.at[1, y], l, at_y(k), d),
            send.at[1], my_right,
        )

    def gather_middle(buf, send, recv):
        row_left = buf.at[y, :, :, left]
        column_right = buf.at[:, x, :, right]
        each(1, SIDE, lambda k: arrive(buf.at[y, along_x(k), :, left], recv.at[0, along_x(k)]))
        start_each(
            SIDE, lambda k: remote(row_left, row_left, send.at[2, k], recv.at[2, y], l, at_y(k), d),
            send.at[2], row_left,
        )
        each(1, SIDE, lambda k: arrive(buf.at[along_y(k), x, :, right], recv.at[1, along_y(k)]))
        start_each(
            SIDE, lambda k: remote(column_right, column_right, send.at[3, k], recv.at[3, x], l, at_x(k), d),
            send.at[3], column_right,
        )

    def gather_end(buf, recv):
        each(1, SIDE, lambda k: arrive(buf.at[along_y(k), :, :, left], recv.at[2, along_y(k)]))
        each(1, SIDE, lambda k: arrive(buf.at[:, along_x(k), :, right], recv.at[3, along_x(k)]))

    @pl.when(inner_layer)
    def _():
        next_copy.start()
        each(1, HALF_COLUMN, lambda k: final_copy(k).start())

    leaving.append(lambda: each(1, HALF_COLUMN, lambda k: sent(target.at[own_rows_final, :], fin_send.at[k])))

    source(0)
    source(1)
    for s in (0, 1):
        @pl.when(ends[s])
        def _(s=s):
            final_source(s, 0, 1)

    sums_start(partial, parts, rs_send.at[0], rs_recv.at[0])
    head_copy = remote(head.at[:, cols(sib)], heads.at[d], head_send, head_recv, l, v, sib)
    head_copy.start()
    leaving.append(head_copy.wait_send)

    lane = lax.broadcasted_iota(jnp.int32, (8, TILE), 1)
    own_lanes = jnp.logical_and(lane >= l * ROWS, lane < l * ROWS + ROWS)
    pad[...] = jnp.zeros((TILE, TILE), f32)
    whole_final.wait()
    chain(0.1)
    wanted = final_own[...].astype(f32)
    want_top = jnp.max(wanted, axis=1, keepdims=True)
    want_sum = jnp.sum(jnp.exp(wanted - want_top), axis=1, keepdims=True)
    column_lane = lax.broadcasted_iota(jnp.int32, (ROWS, TILE), 1)
    pad[own_rows(l), :] = jnp.where(column_lane == 0, want_top, want_sum)
    top_stats[v] = pad[...].T[0:8, :]

    def plane_copy(buf, send, recv):
        return lambda k: remote(buf.at[v], buf.at[v], send.at[k], recv.at[v], l, in_plane(k), d)

    def plane_arrive(buf, recv):
        each(1, GROUPS, lambda k: arrive(buf.at[in_plane(k)], recv.at[in_plane(k)]))

    start_each(GROUPS, plane_copy(top_stats, top_send, top_recv), top_send, top_stats.at[0])
    chain(PACE[0])
    for s in (0, 1):
        @pl.when(ends[s])
        def _(s=s):
            arrive(next_final, next_recv)
            final_source(s, 1, FINALS)

    sums_middle(partial, parts, part_mid, part_end, rs_send.at[0], rs_recv.at[0])
    chain(PACE[1])
    value_left, value_right = sums_end(part_mid, part_end, rs_recv.at[0])
    scaled[:, left] = value_left + bias[:, left]
    scaled[:, right] = value_right + bias[:, right]
    projected = scaled[...]
    squares[d] = jnp.broadcast_to(jnp.sum(projected * projected, axis=1, keepdims=True), (ROWS, 128))

    def to_blocks(buf, send, recv):
        def copy(k):
            return remote(buf.at[d], buf.at[d], send.at[k], recv.at[d], l, v, lax.rem(d + k, BLOCKS))

        start_each(BLOCKS, copy, send, buf.at[0])

    def from_blocks(buf, recv):
        def come(k):
            dd = lax.rem(d + k, BLOCKS)
            arrive(buf.at[dd], recv.at[dd])

        each(1, BLOCKS, come)

    to_blocks(squares, sq_send, sq_recv)
    chain(PACE[2])
    from_blocks(squares, sq_recv)
    inverse = lax.rsqrt(jnp.sum(squares[...], axis=0)[:, :1] / D + epsilon)
    scaled[...] = projected * inverse
    normed[d, y, x] = (scaled[...] * gain[...]).astype(bf16)

    mine = normed.at[d, y, x]
    opp_copy = remote(mine, mine, opp_send, opp_recv, l, v, opp)
    opp_copy.start()
    leaving.append(opp_copy.wait_send)

    def to_sibling(block, i):
        copy = remote(normed.at[block], normed.at[block], sib_send.at[i], sib_recv.at[i], l, v, sib)
        copy.start()
        leaving.append(copy.wait_send)

    here, there = normed.at[d], normed.at[opp]
    gather_start(here, ag_send.at[0], ag_recv.at[0])
    chain(PACE[3])
    gather_middle(here, ag_send.at[0], ag_recv.at[0])
    arrive(normed.at[opp, y, x], opp_recv)
    gather_start(there, ag_send.at[1], ag_recv.at[1])
    turned[...] = hidden[...].T
    chain(PACE[4])
    gather_middle(there, ag_send.at[1], ag_recv.at[1])
    plane_arrive(top_stats, top_recv)
    all_top = jnp.max(top_stats[:, 0:1, :], axis=0)
    all_sum = jnp.sum(top_stats[:, 1:2, :] * jnp.exp(top_stats[:, 0:1, :] - all_top[None]), axis=0)
    row_lse = all_top + jnp.log(jnp.where(own_lanes[0:1, :], all_sum, 1.0))
    want_lse[column] = jnp.broadcast_to(jnp.where(own_lanes[0:1, :], row_lse, 0.0), (8, TILE))

    def want_copy(k):
        m = in_column(k)
        return remote(
            want_lse.at[column], want_lse.at[column], wl_send.at[k], wl_recv.at[column],
            lax.div(m, BLOCKS), v, lax.rem(m, BLOCKS),
        )

    start_each(NCOL, want_copy, wl_send, want_lse.at[0])
    chain(PACE[5])
    gather_end(here, ag_recv.at[0])
    to_sibling(d, 0)
    chain(PACE[6])
    gather_end(there, ag_recv.at[1])
    to_sibling(opp, 1)
    own_head.wait()
    own_final.wait()

    def multiply(block, lo, hi, spans=((0, BLOCK),), first=False):
        def go(n):
            at = aligned(n * HALF, HALF)
            value = None
            for a, b in spans:
                term = jnp.dot(
                    normed[block, :, :, :, a:b].reshape(TOKENS, b - a), heads[block, a:b, at],
                    preferred_element_type=f32,
                )
                value = term if value is None else value + term
            if first:
                logits[:, at] = value
            else:
                logits[:, at] += value

        each(lo, hi, go)

    def passed(k):
        for s in (0, 1):
            arrive(heads.at[opp_sib, rows_of(s, k), :], pass_recv.at[s, k])

    EARLY = CHUNKS // 2
    early = ((0, HALF // 2), (HALF, HALF + HALF // 2))
    late = ((HALF // 2, HALF), (HALF + HALF // 2, BLOCK))
    multiply(d, 0, 1, first=True)
    chain(PACE[7])
    multiply(d, 1, 2, first=True)
    arrive(normed.at[sib], sib_recv.at[0])
    arrive(heads.at[sib], head_recv)
    chain(PACE[8])
    multiply(sib, 0, 1)
    chain(PACE[9])
    multiply(sib, 1, 2)
    chain(PACE[10])
    multiply(opp, 0, 2, early)
    chain(PACE[11])
    arrive(normed.at[opp_sib], sib_recv.at[1])
    each(0, EARLY, passed)
    multiply(opp_sib, 0, 2, early)
    chain(1)
    @pl.when(jnp.logical_not(inner_layer))
    def _():
        each(1, HALF_COLUMN, lambda k: final_copy(k).start())

    multiply(opp, 0, 2, late)
    each(EARLY, CHUNKS, passed)
    multiply(opp_sib, 0, 2, late)

    for t in range(TOKENS // TILE):
        have = logits[t * TILE:(t + 1) * TILE, :]
        have_top = jnp.max(have, axis=1, keepdims=True)
        have_sum = jnp.sum(jnp.exp(have - have_top), axis=1, keepdims=True)
        tile_lane = lax.broadcasted_iota(jnp.int32, (TILE, TILE), 1)
        turned = jnp.where(tile_lane == 0, have_top, have_sum).T
        stats[v, t:t + 1, :] = turned[0:1, :]
        stats[v, 4 + t:5 + t, :] = turned[1:2, :]

    start_each(GROUPS, plane_copy(stats, st_send, st_recv), st_send, stats.at[0])

    def merge(buf):
        top = jnp.max(buf[:, 0:4, :], axis=0)
        return top, jnp.sum(buf[:, 4:8, :] * jnp.exp(buf[:, 0:4, :] - top[None]), axis=0)

    chain(2)
    plane_arrive(stats, st_recv)
    top, total = merge(stats)
    stats2[d] = jnp.concatenate([top, total], axis=0)
    to_blocks(stats2, st2_send, st2_recv)

    def want_arrived(k):
        m = in_column(k)
        arrive(want_lse.at[m], wl_recv.at[m])

    def final_arrived(k):
        m = lax.rem(in_half + k, HALF_COLUMN)
        rows = aligned((h * 2 + lax.rem(m, 2)) * TILE + lax.div(m, 2) * ROWS, ROWS)
        arrive(target.at[rows, :], fin_recv.at[m])

    def final_passed(k):
        for s in (0, 1):
            arrive(target.at[final_rows(s, k, opp_sib), :], fpass_recv.at[s, k])

    each(1, NCOL, want_arrived)
    each(1, HALF_COLUMN, final_arrived)
    each(0, FINALS, final_passed)
    for t in range(BLOCKS):
        lse[4 + t:5 + t, :] = (
            want_lse[t, 0:1, :] + want_lse[4 + t, 0:1, :] + want_lse[8 + t, 0:1, :] + want_lse[12 + t, 0:1, :]
        )
    from_blocks(stats2, st2_recv)
    top, total = merge(stats2)
    lse[0:4, :] = top + jnp.log(total)

    def lse_columns(t):
        have_lse = jnp.broadcast_to(lse[t:t + 1, :], (TILE, TILE)).T[:, 0:1]
        return have_lse, jnp.broadcast_to(lse[4 + t:5 + t, :], (TILE, TILE)).T[:, 0:1]

    for t in range(BLOCKS):
        at = pl.ds(t * TILE, TILE)
        have_lse, target_lse = lse_columns(t)
        want = jnp.exp(target[at, :].astype(f32) - target_lse)
        grads[at, :] = (jnp.exp(logits[at, :] - have_lse) - want).astype(bf16)

    def back(block, lo, hi, write):
        def go(n):
            write(
                n,
                lax.dot_general(
                    grads[...], heads[block, aligned(n * HALF, HALF), :], (((1,), (1,)), ((), ())),
                    preferred_element_type=f32,
                ),
            )

        each(lo, hi, go)

    def crossing_copy(i, n):
        return remote(crossing.at[i, n], crossed.at[i, n], gx_send.at[i, n], gx_recv.at[i, n], l, v, sib)

    for i, (theirs, ours) in enumerate(((opp_sib, opp), (sib, d))):
        def to_crossing(n, value, i=i):
            for m in (0, 1):
                crossing[i, 2 * n + m] = value[:, m * 256:(m + 1) * 256].astype(bf16)
                crossing_copy(i, 2 * n + m).start()

        def to_summing(n, value, i=i):
            for m in (0, 1):
                arrive(crossed.at[i, 2 * n + m], gx_recv.at[i, 2 * n + m])
                total = (value[:, m * 256:(m + 1) * 256] + crossed[i, 2 * n + m].astype(f32)).astype(bf16)
                summing[i, :, :, :, aligned(n * HALF + m * 256, 256)] = total.reshape(SIDE, SIDE, ROWS, 256)

        back(theirs, 0, 2, to_crossing)
        leaving.append(lambda i=i: each(0, 4, lambda n: crossing_copy(i, n).wait_send()))
        back(ours, 0, 1, to_summing)
        sums_start(summing.at[i], sum_parts.at[i], rs_send.at[1 + i], rs_recv.at[1 + i], (0,))
        back(ours, 1, 2, to_summing)
        sums_start(summing.at[i], sum_parts.at[i], rs_send.at[1 + i], rs_recv.at[1 + i], (1,))

    cross[...] = jnp.zeros((1, QUARTER), f32)
    for t in range(BLOCKS):
        at = pl.ds(t * TILE, TILE)
        wanted = target[at, :].astype(f32)
        have = logits[at, :]
        want = jnp.exp(wanted - lse_columns(t)[1])
        cross[...] += jnp.sum(want * (wanted - have), axis=0, keepdims=True)
        inner = jnp.sum(grads[at, :].astype(f32) * have, axis=1, keepdims=True)
        crosses[v, t:t + 1, :] = jnp.broadcast_to(inner, (TILE, TILE)).T[0:1, :]
    crosses[v, 4:8, :] = jnp.broadcast_to(jnp.sum(cross[...], axis=1, keepdims=True), (4, 128))
    start_each(GROUPS, plane_copy(crosses, cr_send, cr_recv), cr_send, crosses.at[0])

    for i in (0, 1):
        sums_middle(
            summing.at[i], sum_parts.at[i], sum_mid.at[i], sum_end.at[i], rs_send.at[1 + i], rs_recv.at[1 + i]
        )
        if i == 0:
            plane_arrive(crosses, cr_recv)
            crosses2[d] = jnp.sum(crosses[...], axis=0)
            to_blocks(crosses2, cr2_send, cr2_recv)

    value_left, value_right = sums_end(sum_mid.at[0], sum_end.at[0], rs_recv.at[1])
    half_sum[:, left] = value_left.astype(bf16)
    half_sum[:, right] = value_right.astype(bf16)
    go_copy = remote(half_sum, other_sum, go_send, go_recv, l, v, opp)
    go_copy.start()
    leaving.append(go_copy.wait_send)
    value_left, value_right = sums_end(sum_mid.at[1], sum_end.at[1], rs_recv.at[2])
    finals[:, left] = value_left
    finals[:, right] = value_right
    from_blocks(crosses2, cr2_recv)
    crossed_all = jnp.sum(crosses2[...], axis=0)
    div_out[0] = (jnp.sum(crossed_all[4:5, 0:1]) + jnp.sum(lse[0:4, :] - lse[4:8, :])) / TOKENS
    lse[...] = crossed_all
    pad[...] = jnp.broadcast_to(lse[pl.ds(y, 1), :], (TILE, TILE)).T
    inner_mean = pad[own_rows(x), :][:, 0:1] / D
    arrive(other_sum, go_recv)

    grad_scaled = (finals[...] + other_sum[...].astype(f32)) * gain[...]
    inverse = lax.rsqrt(jnp.sum(squares[...], axis=0)[:, :1] / D + epsilon)
    gathered_grad[y, x] = (inverse * (grad_scaled - scaled[...] * inner_mean)).astype(bf16)
    gather_start(gathered_grad, ag_send.at[2], ag_recv.at[2])
    gather_middle(gathered_grad, ag_send.at[2], ag_recv.at[2])
    gather_end(gathered_grad, ag_recv.at[2])

    drain()


def products(
    turned_in, grad_in, divergence, weights_out, offsets_out, div_out, turned, grad, weights, in_sem, out_sem
):
    tiles, tile = grad.shape[0], grad.shape[-1]

    def part(n):
        return pl.ds(n * tile, tile)

    whole = pltpu.make_async_copy(turned_in, turned, in_sem.at[tiles])
    whole.start()
    ins = [pltpu.make_async_copy(grad_in.at[:, :, :, part(n)], grad.at[n], in_sem.at[n]) for n in range(tiles)]
    outs = [pltpu.make_async_copy(weights.at[n], weights_out.at[0, :, part(n)], out_sem.at[n]) for n in range(tiles)]
    for copy in ins:
        copy.start()
    whole.wait()
    for n in range(tiles):
        ins[n].wait()
        value = grad[n].reshape(TOKENS, tile)
        weights[n] = jnp.dot(turned[...], value, preferred_element_type=f32)
        outs[n].start()
        offsets_out[:, part(n)] = jnp.sum(value.astype(f32), axis=0, keepdims=True)
    div_out[0] = divergence[0]
    for copy in outs:
        copy.wait()


def run(hidden, translator, bias, gain, head, final):
    dma = pltpu.SemaphoreType.DMA
    vmem = pltpu.VMEM
    in_vmem = pl.BlockSpec(memory_space=pltpu.VMEM)
    anywhere = pl.BlockSpec(memory_space=pl.ANY)
    width = hidden.shape[1]
    smem = pl.BlockSpec(memory_space=pltpu.SMEM)
    grad, turned, divergence = pl.pallas_call(
        kernel,
        out_shape=[
            jax.ShapeDtypeStruct((SIDE, SIDE, ROWS, BLOCK), bf16),
            jax.ShapeDtypeStruct((width, TOKENS), bf16),
            jax.ShapeDtypeStruct((1,), f32),
        ],
        in_specs=[anywhere] * 6,
        out_specs=[in_vmem, in_vmem, smem],
        scratch_shapes=[
            vmem((TOKENS, width), bf16),
            vmem((width, BLOCK), bf16),
            vmem((1, BLOCK), f32),
            vmem((1, BLOCK), f32),
            vmem((BLOCKS + 1, BLOCK, QUARTER), bf16),
            vmem((BLOCKS, SIDE, SIDE, ROWS, BLOCK), bf16),
            vmem((SIDE, SIDE, ROWS, BLOCK), f32),
            vmem((TOKENS, QUARTER), bf16),
            vmem((ROWS, BLOCKS * QUARTER), bf16),
            vmem((TILE, TILE), f32),
            vmem((ROWS, BLOCK), f32),
            vmem((BLOCKS, ROWS, 128), f32),
            vmem((TOKENS, QUARTER), f32),
            vmem((GROUPS, 8, TILE), f32),
            vmem((LAYERS * BLOCKS, 8, TILE), f32),
            vmem((GROUPS, 8, TILE), f32),
            vmem((BLOCKS, 8, TILE), f32),
            vmem((8, TILE), f32),
            vmem((1, QUARTER), f32),
            vmem((GROUPS, 8, TILE), f32),
            vmem((BLOCKS, 8, TILE), f32),
            vmem((TOKENS, QUARTER), bf16),
            vmem((2, 4, TOKENS, 256), bf16),
            vmem((2, 4, TOKENS, 256), bf16),
            vmem((2, SIDE, SIDE, ROWS, BLOCK), bf16),
            vmem((2, SIDE, SIDE, ROWS, HALF), f32),
            vmem((2, SIDE, ROWS, HALF), f32),
            vmem((2, SIDE, ROWS, HALF), f32),
            vmem((2, 2, SIDE, SIDE, ROWS, HALF), bf16),
            vmem((2, 2, SIDE, ROWS, HALF), bf16),
            vmem((2, 2, SIDE, ROWS, HALF), bf16),
            vmem((ROWS, BLOCK), bf16),
            vmem((ROWS, BLOCK), bf16),
            vmem((ROWS, BLOCK), f32),
            vmem((ROWS, 2 * QUARTER), bf16),
            vmem((TILE, QUARTER), bf16),
            dma((2, 2, CHUNKS)), dma((2, 2, CHUNKS)),
            dma((2, CHUNKS)), dma((2, CHUNKS)),
            dma((2, 2, FINALS)), dma((2, 2, FINALS)),
            dma((2, FINALS)), dma((2, FINALS)),
            dma, dma,
            dma, dma,
            dma((16,)), dma((16,)),
            dma((BLOCKS,)), dma((BLOCKS,)),
            dma, dma,
            dma((2,)), dma((2,)),
            dma((GROUPS,)), dma((GROUPS,)),
            dma((16,)), dma((16,)),
            dma((GROUPS,)), dma((GROUPS,)),
            dma((BLOCKS,)), dma((BLOCKS,)),
            dma((GROUPS,)), dma((GROUPS,)),
            dma((BLOCKS,)), dma((BLOCKS,)),
            dma((2, 4)), dma((2, 4)),
            dma((3, 4, SIDE)), dma((3, 4, SIDE)),
            dma((3, 4, SIDE)), dma((3, 4, SIDE)),
            dma, dma,
            dma((7,)),
        ],
        compiler_params=pltpu.CompilerParams(
            collective_id=0, has_side_effects=True, vmem_limit_bytes=56 * 1024 * 1024
        ),
        name="lens",
    )(hidden, translator, bias, gain, head, final)
    tile = 256
    return pl.pallas_call(
        products,
        out_shape=[
            jax.ShapeDtypeStruct((1, width, BLOCK), f32),
            jax.ShapeDtypeStruct((1, BLOCK), f32),
            jax.ShapeDtypeStruct((1,), f32),
        ],
        in_specs=[anywhere, anywhere, smem],
        out_specs=[anywhere, in_vmem, smem],
        scratch_shapes=[
            vmem((width, TOKENS), bf16),
            vmem((BLOCK // tile, SIDE, SIDE, ROWS, tile), bf16),
            vmem((BLOCK // tile, width, tile), f32),
            dma((BLOCK // tile + 1,)),
            dma((BLOCK // tile,)),
        ],
        name="products",
    )(turned, grad, divergence)


def shards(hidden, translator, bias, gain, head, final_logits):
    return tuple(run(hidden[0], translator[0], bias, gain[None], head, final_logits[0]))


def solution(mesh):
    in_specs = (
        P("layer", None, "vocab"),
        P("layer", "vocab", "dp"),
        P("layer", "dp"),
        P("dp"),
        P("dp", "vocab"),
        P("dp", "layer", "vocab"),
    )
    out_specs = (P("layer", "vocab", "dp"), P("layer", "dp"), P("layer"))
    return jax.shard_map(shards, mesh=mesh, in_specs=in_specs, out_specs=out_specs, check_vma=False)
```

```python
import jax
import jax.numpy as jnp
from jax import lax
from jax.experimental import pallas as pl
from jax.experimental.pallas import tpu as pltpu
from jax.sharding import PartitionSpec as P

D = 4096
TOKENS = 512
LAYERS = 4
GROUPS = 16
SIDE = 4
BLOCKS = 4
BLOCK = D // BLOCKS
QUARTER = 1024
ROWS = TOKENS // GROUPS
TILE = 128
HALF = BLOCK // 2
CHUNK = 32
CHUNKS = HALF // CHUNK
LAG = 3
FINALS = 2 * ROWS // CHUNK
PACE = (0.3, 0.4, 0.5, 0.58, 0.64, 0.82, 0.9, 0.92, 0.94, 0.96, 0.98, 1.0)

epsilon = 1e-05
f32 = jnp.float32
bf16 = jnp.bfloat16
MESH = pl.DeviceIdType.MESH


def aligned(start, size):
    return pl.ds(pl.multiple_of(start, size), size)


def each(lo, hi, f):
    def step(k, carry):
        f(k)
        return carry

    lax.fori_loop(lo, hi, step, 0)


def kernel(
    hidden_hbm, translator_hbm, bias_hbm, gain_hbm, head, final, gathered_grad, turned, div_out,
    hidden, translator, bias, gain,
    heads, normed, partial, target, final_own, pad, scaled, squares, logits,
    top_stats, want_lse, stats, stats2, lse, cross, crosses, crosses2, grads, crossing, crossed, summing,
    parts, part_mid, part_end, sum_parts, sum_mid, sum_end, half_sum, other_sum, finals,
    next_final, passing_final,
    chain_send, chain_recv, pass_send, pass_recv, fchain_send, fchain_recv, fpass_send, fpass_recv,
    next_send, next_recv, head_send, head_recv, fin_send, fin_recv,
    sq_send, sq_recv, opp_send, opp_recv, sib_send, sib_recv,
    top_send, top_recv, wl_send, wl_recv, st_send, st_recv, st2_send, st2_recv, cr_send, cr_recv,
    cr2_send, cr2_recv, gx_send, gx_recv, rs_send, rs_recv, ag_send, ag_recv,
    go_send, go_recv, local_sem,
):
    l = lax.axis_index("layer")
    v = lax.axis_index("vocab")
    d = lax.axis_index("dp")
    y = lax.div(v, SIDE)
    x = lax.rem(v, SIDE)
    h = lax.div(d, 2)
    c = lax.rem(d, 2)
    sib = h * 2 + 1 - c
    opp = lax.rem(d + 2, BLOCKS)
    opp_sib = (1 - h) * 2 + 1 - c
    up_l = lax.rem(l + 1, LAYERS)
    up_d = lax.rem(d + 2 * lax.div(l + 1, LAYERS), BLOCKS)
    down_l = lax.rem(l + LAYERS - 1, LAYERS)
    down_d = lax.rem(d + 2 * (1 - lax.div(l + LAYERS - 1, LAYERS)), BLOCKS)
    column = l * BLOCKS + d
    NCOL = LAYERS * BLOCKS

    def in_plane(k):
        return lax.rem(v + k, GROUPS)

    def in_column(k):
        return lax.rem(column + k, NCOL)

    def along_x(k):
        return lax.rem(x + k, SIDE)

    def along_y(k):
        return lax.rem(y + k, SIDE)

    def remote(src, dst, send, recv, ll, vv, dd):
        return pltpu.make_async_remote_copy(
            src_ref=src, dst_ref=dst, send_sem=send, recv_sem=recv,
            device_id=(ll, vv, dd), device_id_type=MESH,
        )

    def arrive(dst, sem):
        remote(dst, dst, sem, sem, l, v, d).wait_recv()

    def sent(src, sem):
        remote(src, src, sem, sem, l, v, d).wait_send()

    leaving = []

    def drain():
        for f in leaving:
            f()

    def start_each(count, make, send, shape):
        each(1, count, lambda k: make(k).start())
        leaving.append(lambda: each(1, count, lambda k: sent(shape, send.at[k])))

    def cols(q):
        return aligned(q * QUARTER, QUARTER)

    def own_rows(p):
        return aligned(p * ROWS, ROWS)

    barrier = pltpu.get_barrier_semaphore()

    def greet_plane(k):
        pl.semaphore_signal(barrier, inc=1, device_id=(l, in_plane(k), d), device_id_type=MESH)

    def greet_column(k):
        m = in_column(k)
        pl.semaphore_signal(
            barrier, inc=1, device_id=(lax.div(m, BLOCKS), v, lax.rem(m, BLOCKS)), device_id_type=MESH
        )

    each(1, GROUPS, greet_plane)
    each(1, NCOL, greet_column)

    staged = [
        pltpu.make_async_copy(src, dst, local_sem.at[3 + n])
        for n, (src, dst) in enumerate(
            ((hidden_hbm, hidden), (translator_hbm, translator), (bias_hbm, bias), (gain_hbm, gain))
        )
    ]
    for copy in staged:
        copy.start()
    own_head = pltpu.make_async_copy(head.at[:, cols(d)], heads.at[d], local_sem.at[0])
    own_head.start()
    own_rows_final = aligned(d * TILE + l * ROWS, ROWS)
    own_final = pltpu.make_async_copy(final.at[:, cols(d)], target.at[own_rows_final, :], local_sem.at[1])
    own_final.start()
    whole_final = pltpu.make_async_copy(final, final_own, local_sem.at[2])
    whole_final.start()

    def product(n):
        at = aligned(n * 256, 256)
        value = jnp.dot(hidden[...], translator[:, at], preferred_element_type=f32)
        partial[:, :, :, at] = value.reshape(SIDE, SIDE, ROWS, 256)

    for copy in staged:
        copy.wait()
    each(0, BLOCK // 256, product)
    pl.semaphore_wait(barrier, GROUPS - 1 + NCOL - 1)

    def rows_of(s, k):
        return aligned(s * HALF + k * CHUNK, CHUNK)

    def slot(j):
        return opp + j * (BLOCKS - opp)

    def chain_copy(s, j, k, from_own):
        rows = rows_of(s, k)
        ll, dd = (up_l, up_d) if s == 0 else (down_l, down_d)
        if from_own:
            src = head.at[rows, cols((1 - h) * 2 + (c if j == 0 else 1 - c))]
            dst = heads.at[d if j == 0 else BLOCKS, rows, :]
        else:
            src = heads.at[slot(j), rows, :]
            dst = src
        return remote(src, dst, chain_send.at[s, j, k], chain_recv.at[s, j, k], ll, v, dd)

    ends = (l == LAYERS - 1, l == 0)
    relays = (l != LAYERS - 1, l != 0)

    def source(s):
        def one(k):
            chain_copy(s, 0, k, True).start()
            chain_copy(s, 1, k, True).start()

        @pl.when(ends[s])
        def _():
            each(0, CHUNKS, one)

    def final_at(s, k):
        return (LAYERS - 1 - k if s == 0 else k) * ROWS

    def final_rows(s, k, block):
        return aligned(block * TILE + final_at(s, k), CHUNK)

    def final_chain(s, j, k, src, block):
        ll, dd = (up_l, up_d) if s == 0 else (down_l, down_d)
        dst = target.at[final_rows(s, k, block), :] if j == 0 else passing_final.at[aligned(final_at(s, k), CHUNK), :]
        return remote(
            dst if src is None else src, dst, fchain_send.at[s, j, k], fchain_recv.at[s, j, k], ll, v, dd
        )

    def final_source(s, lo, hi):
        def one(k):
            rows = aligned(0, CHUNK)
            for j in (0, 1):
                q = c if j == 0 else 1 - c
                if lo == 0:
                    src = final.at[rows, cols((1 - h) * 2 + q)]
                else:
                    src = next_final.at[rows, cols(q)]
                final_chain(s, j, k, src, d).start()

        each(lo, hi, one)

    next_copy = remote(
        final.at[:, aligned((1 - h) * 2 * QUARTER, 2 * QUARTER)], next_final, next_send, next_recv, 3 * (l - 1), v, d
    )
    inner_layer = jnp.logical_and(l > 0, l < LAYERS - 1)

    def next_sent():
        @pl.when(inner_layer)
        def _():
            next_copy.wait_send()

    leaving.append(next_sent)

    def chain_sent(k):
        for s in (0, 1):
            chain_copy(s, 0, k, False).wait_send()
            chain_copy(s, 1, k, False).wait_send()
            sent(heads.at[BLOCKS, rows_of(s, k), :], pass_send.at[s, k])

    def final_chain_sent(k):
        for s in (0, 1):
            final_chain(s, 0, k, None, opp).wait_send()
            final_chain(s, 1, k, None, opp).wait_send()
            sent(passing_final.at[0:CHUNK, :], fpass_send.at[s, k])

    leaving.append(lambda: each(0, CHUNKS, chain_sent))
    leaving.append(lambda: each(0, FINALS, final_chain_sent))
    lag = (LAG * l, LAG * (LAYERS - 1 - l))
    TURNS = 2 * CHUNKS + LAG * (LAYERS - 1)
    done = [0]

    def chain(until):
        def one(turn):
            for s in (0, 1):
                u = turn - lag[s]

                @pl.when(jnp.logical_and(u >= 0, u < 2 * CHUNKS))
                def _(s=s, u=u):
                    k, j = lax.div(u, 2), lax.rem(u, 2)
                    rows = rows_of(s, k)
                    arrive(heads.at[slot(j), rows, :], chain_recv.at[s, j, k])

                    @pl.when(relays[s])
                    def _():
                        chain_copy(s, j, k, False).start()

                    @pl.when(j == 1)
                    def _():
                        remote(
                            heads.at[BLOCKS, rows, :], heads.at[opp, rows, :],
                            pass_send.at[s, k], pass_recv.at[s, k], l, v, sib,
                        ).start()

                @pl.when(jnp.logical_and(u >= 2 * CHUNKS, u < 2 * (CHUNKS + FINALS)))
                def _(s=s, u=u - 2 * CHUNKS):
                    k, j = lax.div(u, 2), lax.rem(u, 2)
                    rows = final_rows(s, k, opp)
                    passed_rows = passing_final.at[aligned(final_at(s, k), CHUNK), :]

                    @pl.when(j == 0)
                    def _():
                        arrive(target.at[rows, :], fchain_recv.at[s, 0, k])

                        @pl.when(relays[s])
                        def _():
                            final_chain(s, 0, k, None, opp).start()

                    @pl.when(j == 1)
                    def _():
                        arrive(passed_rows, fchain_recv.at[s, 1, k])

                        @pl.when(relays[s])
                        def _():
                            final_chain(s, 1, k, None, opp).start()

                        remote(
                            passed_rows, target.at[rows, :], fpass_send.at[s, k], fpass_recv.at[s, k], l, v, sib
                        ).start()

        hi = min(int(TURNS * until), TURNS + 2 * FINALS)
        each(done[0], hi, one)
        done[0] = hi

    HALF_COLUMN = LAYERS * 2
    in_half = l * 2 + c

    def final_copy(k):
        m = lax.rem(in_half + k, HALF_COLUMN)
        dd = h * 2 + lax.rem(m, 2)
        return remote(
            final.at[:, cols(dd)], target.at[own_rows_final, :],
            fin_send.at[k], fin_recv.at[in_half], lax.div(m, 2), v, dd,
        )

    left = pl.ds(0, HALF)
    right = pl.ds(HALF, HALF)

    def at_x(k):
        return y * SIDE + along_x(k)

    def at_y(k):
        return along_y(k) * SIDE + x

    def sums_start(src, part, send, recv, ways=(0, 1)):
        if 0 in ways:
            start_each(
                SIDE,
                lambda k: remote(
                    src.at[:, along_x(k), :, left], part.at[0, x], send.at[0, k], recv.at[0, x], l, at_x(k), d
                ),
                send.at[0], part.at[0, 0],
            )
        if 1 in ways:
            start_each(
                SIDE,
                lambda k: remote(
                    src.at[along_y(k), :, :, right], part.at[1, y], send.at[1, k], recv.at[1, y], l, at_y(k), d
                ),
                send.at[1], part.at[0, 0],
            )

    def sums_middle(src, part, mid, end, send, recv):
        each(1, SIDE, lambda k: arrive(part.at[0, along_x(k)], recv.at[0, along_x(k)]))
        for n in range(SIDE):
            value = src[n, x, :, left].astype(f32)
            for k in range(1, SIDE):
                value += part[0, along_x(k), n].astype(f32)
            mid[0, n] = value.astype(mid.dtype)
        start_each(
            SIDE,
            lambda k: remote(
                mid.at[0, along_y(k)], end.at[0, y], send.at[2, k], recv.at[2, y], l, at_y(k), d
            ),
            send.at[2], end.at[0, 0],
        )
        each(1, SIDE, lambda k: arrive(part.at[1, along_y(k)], recv.at[1, along_y(k)]))
        for n in range(SIDE):
            value = src[y, n, :, right].astype(f32)
            for k in range(1, SIDE):
                value += part[1, along_y(k), n].astype(f32)
            mid[1, n] = value.astype(mid.dtype)
        start_each(
            SIDE,
            lambda k: remote(
                mid.at[1, along_x(k)], end.at[1, x], send.at[3, k], recv.at[3, x], l, at_x(k), d
            ),
            send.at[3], end.at[0, 0],
        )

    def sums_end(mid, end, recv):
        each(1, SIDE, lambda k: arrive(end.at[0, along_y(k)], recv.at[2, along_y(k)]))
        each(1, SIDE, lambda k: arrive(end.at[1, along_x(k)], recv.at[3, along_x(k)]))
        value_left = mid[0, y].astype(f32)
        value_right = mid[1, x].astype(f32)
        for k in range(1, SIDE):
            value_left += end[0, along_y(k)].astype(f32)
            value_right += end[1, along_x(k)].astype(f32)
        return value_left, value_right

    def gather_start(buf, send, recv):
        my_left = buf.at[y, x, :, left]
        my_right = buf.at[y, x, :, right]
        start_each(
            SIDE, lambda k: remote(my_left, my_left, send.at[0, k], recv.at[0, x], l, at_x(k), d), send.at[0], my_left
        )
        start_each(
            SIDE, lambda k: remote(my_right, my_right, send.at[1, k], recv.at[1, y], l, at_y(k), d),
            send.at[1], my_right,
        )

    def gather_middle(buf, send, recv):
        row_left = buf.at[y, :, :, left]
        column_right = buf.at[:, x, :, right]
        each(1, SIDE, lambda k: arrive(buf.at[y, along_x(k), :, left], recv.at[0, along_x(k)]))
        start_each(
            SIDE, lambda k: remote(row_left, row_left, send.at[2, k], recv.at[2, y], l, at_y(k), d),
            send.at[2], row_left,
        )
        each(1, SIDE, lambda k: arrive(buf.at[along_y(k), x, :, right], recv.at[1, along_y(k)]))
        start_each(
            SIDE, lambda k: remote(column_right, column_right, send.at[3, k], recv.at[3, x], l, at_x(k), d),
            send.at[3], column_right,
        )

    def gather_end(buf, recv):
        each(1, SIDE, lambda k: arrive(buf.at[along_y(k), :, :, left], recv.at[2, along_y(k)]))
        each(1, SIDE, lambda k: arrive(buf.at[:, along_x(k), :, right], recv.at[3, along_x(k)]))

    @pl.when(inner_layer)
    def _():
        next_copy.start()
        each(1, HALF_COLUMN, lambda k: final_copy(k).start())

    leaving.append(lambda: each(1, HALF_COLUMN, lambda k: sent(target.at[own_rows_final, :], fin_send.at[k])))

    source(0)
    source(1)
    for s in (0, 1):
        @pl.when(ends[s])
        def _(s=s):
            final_source(s, 0, 1)

    sums_start(partial, parts, rs_send.at[0], rs_recv.at[0])
    head_copy = remote(head.at[:, cols(sib)], heads.at[d], head_send, head_recv, l, v, sib)
    head_copy.start()
    leaving.append(head_copy.wait_send)

    lane = lax.broadcasted_iota(jnp.int32, (8, TILE), 1)
    own_lanes = jnp.logical_and(lane >= l * ROWS, lane < l * ROWS + ROWS)
    pad[...] = jnp.zeros((TILE, TILE), f32)
    whole_final.wait()
    chain(0.1)
    wanted = final_own[...].astype(f32)
    want_top = jnp.max(wanted, axis=1, keepdims=True)
    want_sum = jnp.sum(jnp.exp(wanted - want_top), axis=1, keepdims=True)
    column_lane = lax.broadcasted_iota(jnp.int32, (ROWS, TILE), 1)
    pad[own_rows(l), :] = jnp.where(column_lane == 0, want_top, want_sum)
    top_stats[v] = pad[...].T[0:8, :]

    def plane_copy(buf, send, recv):
        return lambda k: remote(buf.at[v], buf.at[v], send.at[k], recv.at[v], l, in_plane(k), d)

    def plane_arrive(buf, recv):
        each(1, GROUPS, lambda k: arrive(buf.at[in_plane(k)], recv.at[in_plane(k)]))

    start_each(GROUPS, plane_copy(top_stats, top_send, top_recv), top_send, top_stats.at[0])
    chain(PACE[0])
    for s in (0, 1):
        @pl.when(ends[s])
        def _(s=s):
            arrive(next_final, next_recv)
            final_source(s, 1, FINALS)

    sums_middle(partial, parts, part_mid, part_end, rs_send.at[0], rs_recv.at[0])
    chain(PACE[1])
    value_left, value_right = sums_end(part_mid, part_end, rs_recv.at[0])
    scaled[:, left] = value_left + bias[:, left]
    scaled[:, right] = value_right + bias[:, right]
    projected = scaled[...]
    squares[d] = jnp.broadcast_to(jnp.sum(projected * projected, axis=1, keepdims=True), (ROWS, 128))

    def to_blocks(buf, send, recv):
        def copy(k):
            return remote(buf.at[d], buf.at[d], send.at[k], recv.at[d], l, v, lax.rem(d + k, BLOCKS))

        start_each(BLOCKS, copy, send, buf.at[0])

    def from_blocks(buf, recv):
        def come(k):
            dd = lax.rem(d + k, BLOCKS)
            arrive(buf.at[dd], recv.at[dd])

        each(1, BLOCKS, come)

    to_blocks(squares, sq_send, sq_recv)
    chain(PACE[2])
    from_blocks(squares, sq_recv)
    inverse = lax.rsqrt(jnp.sum(squares[...], axis=0)[:, :1] / D + epsilon)
    scaled[...] = projected * inverse
    normed[d, y, x] = (scaled[...] * gain[...]).astype(bf16)

    mine = normed.at[d, y, x]
    opp_copy = remote(mine, mine, opp_send, opp_recv, l, v, opp)
    opp_copy.start()
    leaving.append(opp_copy.wait_send)

    def to_sibling(block, i):
        copy = remote(normed.at[block], normed.at[block], sib_send.at[i], sib_recv.at[i], l, v, sib)
        copy.start()
        leaving.append(copy.wait_send)

    here, there = normed.at[d], normed.at[opp]
    gather_start(here, ag_send.at[0], ag_recv.at[0])
    chain(PACE[3])
    gather_middle(here, ag_send.at[0], ag_recv.at[0])
    arrive(normed.at[opp, y, x], opp_recv)
    gather_start(there, ag_send.at[1], ag_recv.at[1])
    turned[...] = hidden[...].T
    chain(PACE[4])
    gather_middle(there, ag_send.at[1], ag_recv.at[1])
    plane_arrive(top_stats, top_recv)
    all_top = jnp.max(top_stats[:, 0:1, :], axis=0)
    all_sum = jnp.sum(top_stats[:, 1:2, :] * jnp.exp(top_stats[:, 0:1, :] - all_top[None]), axis=0)
    row_lse = all_top + jnp.log(jnp.where(own_lanes[0:1, :], all_sum, 1.0))
    want_lse[column] = jnp.broadcast_to(jnp.where(own_lanes[0:1, :], row_lse, 0.0), (8, TILE))

    def want_copy(k):
        m = in_column(k)
        return remote(
            want_lse.at[column], want_lse.at[column], wl_send.at[k], wl_recv.at[column],
            lax.div(m, BLOCKS), v, lax.rem(m, BLOCKS),
        )

    start_each(NCOL, want_copy, wl_send, want_lse.at[0])
    chain(PACE[5])
    gather_end(here, ag_recv.at[0])
    to_sibling(d, 0)
    chain(PACE[6])
    gather_end(there, ag_recv.at[1])
    to_sibling(opp, 1)
    own_head.wait()
    own_final.wait()

    def multiply(block, lo, hi, spans=((0, BLOCK),), first=False):
        def go(n):
            at = aligned(n * HALF, HALF)
            value = None
            for a, b in spans:
                term = jnp.dot(
                    normed[block, :, :, :, a:b].reshape(TOKENS, b - a), heads[block, a:b, at],
                    preferred_element_type=f32,
                )
                value = term if value is None else value + term
            if first:
                logits[:, at] = value
            else:
                logits[:, at] += value

        each(lo, hi, go)

    def passed(k):
        for s in (0, 1):
            arrive(heads.at[opp_sib, rows_of(s, k), :], pass_recv.at[s, k])

    EARLY = CHUNKS // 2
    early = ((0, HALF // 2), (HALF, HALF + HALF // 2))
    late = ((HALF // 2, HALF), (HALF + HALF // 2, BLOCK))
    multiply(d, 0, 1, first=True)
    chain(PACE[7])
    multiply(d, 1, 2, first=True)
    arrive(normed.at[sib], sib_recv.at[0])
    arrive(heads.at[sib], head_recv)
    chain(PACE[8])
    multiply(sib, 0, 1)
    chain(PACE[9])
    multiply(sib, 1, 2)
    chain(PACE[10])
    multiply(opp, 0, 2, early)
    chain(PACE[11])
    arrive(normed.at[opp_sib], sib_recv.at[1])
    each(0, EARLY, passed)
    multiply(opp_sib, 0, 2, early)
    chain(1)
    @pl.when(jnp.logical_not(inner_layer))
    def _():
        each(1, HALF_COLUMN, lambda k: final_copy(k).start())

    multiply(opp, 0, 2, late)
    each(EARLY, CHUNKS, passed)
    multiply(opp_sib, 0, 2, late)

    for t in range(TOKENS // TILE):
        have = logits[t * TILE:(t + 1) * TILE, :]
        have_top = jnp.max(have, axis=1, keepdims=True)
        have_sum = jnp.sum(jnp.exp(have - have_top), axis=1, keepdims=True)
        tile_lane = lax.broadcasted_iota(jnp.int32, (TILE, TILE), 1)
        turned = jnp.where(tile_lane == 0, have_top, have_sum).T
        stats[v, t:t + 1, :] = turned[0:1, :]
        stats[v, 4 + t:5 + t, :] = turned[1:2, :]

    start_each(GROUPS, plane_copy(stats, st_send, st_recv), st_send, stats.at[0])

    def merge(buf):
        top = jnp.max(buf[:, 0:4, :], axis=0)
        return top, jnp.sum(buf[:, 4:8, :] * jnp.exp(buf[:, 0:4, :] - top[None]), axis=0)

    chain(2)
    plane_arrive(stats, st_recv)
    top, total = merge(stats)
    stats2[d] = jnp.concatenate([top, total], axis=0)
    to_blocks(stats2, st2_send, st2_recv)

    def want_arrived(k):
        m = in_column(k)
        arrive(want_lse.at[m], wl_recv.at[m])

    def final_arrived(k):
        m = lax.rem(in_half + k, HALF_COLUMN)
        rows = aligned((h * 2 + lax.rem(m, 2)) * TILE + lax.div(m, 2) * ROWS, ROWS)
        arrive(target.at[rows, :], fin_recv.at[m])

    def final_passed(k):
        for s in (0, 1):
            arrive(target.at[final_rows(s, k, opp_sib), :], fpass_recv.at[s, k])

    each(1, NCOL, want_arrived)
    each(1, HALF_COLUMN, final_arrived)
    each(0, FINALS, final_passed)
    for t in range(BLOCKS):
        lse[4 + t:5 + t, :] = (
            want_lse[t, 0:1, :] + want_lse[4 + t, 0:1, :] + want_lse[8 + t, 0:1, :] + want_lse[12 + t, 0:1, :]
        )
    from_blocks(stats2, st2_recv)
    top, total = merge(stats2)
    lse[0:4, :] = top + jnp.log(total)

    def lse_columns(t):
        have_lse = jnp.broadcast_to(lse[t:t + 1, :], (TILE, TILE)).T[:, 0:1]
        return have_lse, jnp.broadcast_to(lse[4 + t:5 + t, :], (TILE, TILE)).T[:, 0:1]

    for t in range(BLOCKS):
        at = pl.ds(t * TILE, TILE)
        have_lse, target_lse = lse_columns(t)
        want = jnp.exp(target[at, :].astype(f32) - target_lse)
        grads[at, :] = (jnp.exp(logits[at, :] - have_lse) - want).astype(bf16)

    def back(block, lo, hi, write):
        def go(n):
            write(
                n,
                lax.dot_general(
                    grads[...], heads[block, aligned(n * HALF, HALF), :], (((1,), (1,)), ((), ())),
                    preferred_element_type=f32,
                ),
            )

        each(lo, hi, go)

    def crossing_copy(i, n):
        return remote(crossing.at[i, n], crossed.at[i, n], gx_send.at[i, n], gx_recv.at[i, n], l, v, sib)

    for i, (theirs, ours) in enumerate(((opp_sib, opp), (sib, d))):
        def to_crossing(n, value, i=i):
            for m in (0, 1):
                crossing[i, 2 * n + m] = value[:, m * 256:(m + 1) * 256].astype(bf16)
                crossing_copy(i, 2 * n + m).start()

        def to_summing(n, value, i=i):
            for m in (0, 1):
                arrive(crossed.at[i, 2 * n + m], gx_recv.at[i, 2 * n + m])
                total = (value[:, m * 256:(m + 1) * 256] + crossed[i, 2 * n + m].astype(f32)).astype(bf16)
                summing[i, :, :, :, aligned(n * HALF + m * 256, 256)] = total.reshape(SIDE, SIDE, ROWS, 256)

        back(theirs, 0, 2, to_crossing)
        leaving.append(lambda i=i: each(0, 4, lambda n: crossing_copy(i, n).wait_send()))
        back(ours, 0, 1, to_summing)
        sums_start(summing.at[i], sum_parts.at[i], rs_send.at[1 + i], rs_recv.at[1 + i], (0,))
        back(ours, 1, 2, to_summing)
        sums_start(summing.at[i], sum_parts.at[i], rs_send.at[1 + i], rs_recv.at[1 + i], (1,))

    cross[...] = jnp.zeros((1, QUARTER), f32)
    for t in range(BLOCKS):
        at = pl.ds(t * TILE, TILE)
        wanted = target[at, :].astype(f32)
        have = logits[at, :]
        want = jnp.exp(wanted - lse_columns(t)[1])
        cross[...] += jnp.sum(want * (wanted - have), axis=0, keepdims=True)
        inner = jnp.sum(grads[at, :].astype(f32) * have, axis=1, keepdims=True)
        crosses[v, t:t + 1, :] = jnp.broadcast_to(inner, (TILE, TILE)).T[0:1, :]
    crosses[v, 4:8, :] = jnp.broadcast_to(jnp.sum(cross[...], axis=1, keepdims=True), (4, 128))
    start_each(GROUPS, plane_copy(crosses, cr_send, cr_recv), cr_send, crosses.at[0])

    for i in (0, 1):
        sums_middle(
            summing.at[i], sum_parts.at[i], sum_mid.at[i], sum_end.at[i], rs_send.at[1 + i], rs_recv.at[1 + i]
        )
        if i == 0:
            plane_arrive(crosses, cr_recv)
            crosses2[d] = jnp.sum(crosses[...], axis=0)
            to_blocks(crosses2, cr2_send, cr2_recv)

    value_left, value_right = sums_end(sum_mid.at[0], sum_end.at[0], rs_recv.at[1])
    half_sum[:, left] = value_left.astype(bf16)
    half_sum[:, right] = value_right.astype(bf16)
    go_copy = remote(half_sum, other_sum, go_send, go_recv, l, v, opp)
    go_copy.start()
    leaving.append(go_copy.wait_send)
    value_left, value_right = sums_end(sum_mid.at[1], sum_end.at[1], rs_recv.at[2])
    finals[:, left] = value_left
    finals[:, right] = value_right
    from_blocks(crosses2, cr2_recv)
    crossed_all = jnp.sum(crosses2[...], axis=0)
    div_out[0] = (jnp.sum(crossed_all[4:5, 0:1]) + jnp.sum(lse[0:4, :] - lse[4:8, :])) / TOKENS
    lse[...] = crossed_all
    pad[...] = jnp.broadcast_to(lse[pl.ds(y, 1), :], (TILE, TILE)).T
    inner_mean = pad[own_rows(x), :][:, 0:1] / D
    arrive(other_sum, go_recv)

    grad_scaled = (finals[...] + other_sum[...].astype(f32)) * gain[...]
    inverse = lax.rsqrt(jnp.sum(squares[...], axis=0)[:, :1] / D + epsilon)
    gathered_grad[y, x] = (inverse * (grad_scaled - scaled[...] * inner_mean)).astype(bf16)
    gather_start(gathered_grad, ag_send.at[2], ag_recv.at[2])
    gather_middle(gathered_grad, ag_send.at[2], ag_recv.at[2])
    gather_end(gathered_grad, ag_recv.at[2])

    drain()


def products(
    turned_in, grad_in, divergence, weights_out, offsets_out, div_out, turned, grad, weights, in_sem, out_sem
):
    tiles, tile = grad.shape[0], grad.shape[-1]

    def part(n):
        return pl.ds(n * tile, tile)

    whole = pltpu.make_async_copy(turned_in, turned, in_sem.at[tiles])
    whole.start()
    ins = [pltpu.make_async_copy(grad_in.at[:, :, :, part(n)], grad.at[n], in_sem.at[n]) for n in range(tiles)]
    outs = [pltpu.make_async_copy(weights.at[n], weights_out.at[0, :, part(n)], out_sem.at[n]) for n in range(tiles)]
    for copy in ins:
        copy.start()
    whole.wait()
    for n in range(tiles):
        ins[n].wait()
        value = grad[n].reshape(TOKENS, tile)
        weights[n] = jnp.dot(turned[...], value, preferred_element_type=f32)
        outs[n].start()
        offsets_out[:, part(n)] = jnp.sum(value.astype(f32), axis=0, keepdims=True)
    div_out[0] = divergence[0]
    for copy in outs:
        copy.wait()


def run(hidden, translator, bias, gain, head, final):
    dma = pltpu.SemaphoreType.DMA
    vmem = pltpu.VMEM
    in_vmem = pl.BlockSpec(memory_space=pltpu.VMEM)
    anywhere = pl.BlockSpec(memory_space=pl.ANY)
    width = hidden.shape[1]
    smem = pl.BlockSpec(memory_space=pltpu.SMEM)
    grad, turned, divergence = pl.pallas_call(
        kernel,
        out_shape=[
            jax.ShapeDtypeStruct((SIDE, SIDE, ROWS, BLOCK), bf16),
            jax.ShapeDtypeStruct((width, TOKENS), bf16),
            jax.ShapeDtypeStruct((1,), f32),
        ],
        in_specs=[anywhere] * 6,
        out_specs=[in_vmem, in_vmem, smem],
        scratch_shapes=[
            vmem((TOKENS, width), bf16),
            vmem((width, BLOCK), bf16),
            vmem((1, BLOCK), f32),
            vmem((1, BLOCK), f32),
            vmem((BLOCKS + 1, BLOCK, QUARTER), bf16),
            vmem((BLOCKS, SIDE, SIDE, ROWS, BLOCK), bf16),
            vmem((SIDE, SIDE, ROWS, BLOCK), f32),
            vmem((TOKENS, QUARTER), bf16),
            vmem((ROWS, BLOCKS * QUARTER), bf16),
            vmem((TILE, TILE), f32),
            vmem((ROWS, BLOCK), f32),
            vmem((BLOCKS, ROWS, 128), f32),
            vmem((TOKENS, QUARTER), f32),
            vmem((GROUPS, 8, TILE), f32),
            vmem((LAYERS * BLOCKS, 8, TILE), f32),
            vmem((GROUPS, 8, TILE), f32),
            vmem((BLOCKS, 8, TILE), f32),
            vmem((8, TILE), f32),
            vmem((1, QUARTER), f32),
            vmem((GROUPS, 8, TILE), f32),
            vmem((BLOCKS, 8, TILE), f32),
            vmem((TOKENS, QUARTER), bf16),
            vmem((2, 4, TOKENS, 256), bf16),
            vmem((2, 4, TOKENS, 256), bf16),
            vmem((2, SIDE, SIDE, ROWS, BLOCK), bf16),
            vmem((2, SIDE, SIDE, ROWS, HALF), f32),
            vmem((2, SIDE, ROWS, HALF), f32),
            vmem((2, SIDE, ROWS, HALF), f32),
            vmem((2, 2, SIDE, SIDE, ROWS, HALF), bf16),
            vmem((2, 2, SIDE, ROWS, HALF), bf16),
            vmem((2, 2, SIDE, ROWS, HALF), bf16),
            vmem((ROWS, BLOCK), bf16),
            vmem((ROWS, BLOCK), bf16),
            vmem((ROWS, BLOCK), f32),
            vmem((ROWS, 2 * QUARTER), bf16),
            vmem((TILE, QUARTER), bf16),
            dma((2, 2, CHUNKS)), dma((2, 2, CHUNKS)),
            dma((2, CHUNKS)), dma((2, CHUNKS)),
            dma((2, 2, FINALS)), dma((2, 2, FINALS)),
            dma((2, FINALS)), dma((2, FINALS)),
            dma, dma,
            dma, dma,
            dma((16,)), dma((16,)),
            dma((BLOCKS,)), dma((BLOCKS,)),
            dma, dma,
            dma((2,)), dma((2,)),
            dma((GROUPS,)), dma((GROUPS,)),
            dma((16,)), dma((16,)),
            dma((GROUPS,)), dma((GROUPS,)),
            dma((BLOCKS,)), dma((BLOCKS,)),
            dma((GROUPS,)), dma((GROUPS,)),
            dma((BLOCKS,)), dma((BLOCKS,)),
            dma((2, 4)), dma((2, 4)),
            dma((3, 4, SIDE)), dma((3, 4, SIDE)),
            dma((3, 4, SIDE)), dma((3, 4, SIDE)),
            dma, dma,
            dma((7,)),
        ],
        compiler_params=pltpu.CompilerParams(
            collective_id=0, has_side_effects=True, vmem_limit_bytes=56 * 1024 * 1024
        ),
        name="lens",
    )(hidden, translator, bias, gain, head, final)
    tile = 256
    return pl.pallas_call(
        products,
        out_shape=[
            jax.ShapeDtypeStruct((1, width, BLOCK), f32),
            jax.ShapeDtypeStruct((1, BLOCK), f32),
            jax.ShapeDtypeStruct((1,), f32),
        ],
        in_specs=[anywhere, anywhere, smem],
        out_specs=[anywhere, in_vmem, smem],
        scratch_shapes=[
            vmem((width, TOKENS), bf16),
            vmem((BLOCK // tile, SIDE, SIDE, ROWS, tile), bf16),
            vmem((BLOCK // tile, width, tile), f32),
            dma((BLOCK // tile + 1,)),
            dma((BLOCK // tile,)),
        ],
        name="products",
    )(turned, grad, divergence)


def shards(hidden, translator, bias, gain, head, final_logits):
    return tuple(run(hidden[0], translator[0], bias, gain[None], head, final_logits[0]))


def solution(mesh):
    in_specs = (
        P("layer", None, "vocab"),
        P("layer", "vocab", "dp"),
        P("layer", "dp"),
        P("dp"),
        P("dp", "vocab"),
        P("dp", "layer", "vocab"),
    )
    out_specs = (P("layer", "vocab", "dp"), P("layer", "dp"), P("layer"))
    return jax.shard_map(shards, mesh=mesh, in_specs=in_specs, out_specs=out_specs, check_vma=False)
```
